32 devices in a mesh: wide: 16 (over z, y, core), narrow: 2 (over x).
Axes of the slice: x: 2, y: 2, z: 4, core: 2. Of those that a mesh axis runs over, the one named last changes fastest.
Arguments:
- tokens: bfloat16 [32, 2048, 1024], P('wide', 'narrow'), may hold values from -6 to 6
- cotangent: bfloat16 [32, 2048, 1024], P('wide', 'narrow'), may hold values from -6 to 6
- lengths: int32 [32], P('wide'), may hold values from 256 to 2048, as said below
- routes: int32 [32, 256], P('wide'), may hold values from 0 to 2047, as said below
- w_qkv: bfloat16 [1024, 3072], P('wide'), may hold values from -0.1875 to 0.1875
- w_out: bfloat16 [1024, 1024], P('wide'), may hold values from -0.75 to 0.75
- w_up: bfloat16 [1024, 4096], P('wide'), may hold values from -0.1875 to 0.1875
- w_down: bfloat16 [4096, 1024], P('wide'), may hold values from -0.09375 to 0.09375
- gain_attn: bfloat16 [1024], P('wide'), may hold values from 0.099609375 to 1.8984375
- gain_mlp: bfloat16 [1024], P('wide'), may hold values from 0.099609375 to 1.8984375
- router: bfloat16 [1024], replicated, may hold values from -0.1875 to 0.1875
Outputs:
- mixed: bfloat16 [32, 2048, 1024], P('wide', 'narrow')
- grad_tokens: bfloat16 [32, 2048, 1024], P('wide', 'narrow')
- grad_qkv: float32 [1024, 3072], P('wide')
- grad_out: float32 [1024, 1024], P('wide')
- grad_up: float32 [1024, 4096], P('wide')
- grad_down: float32 [4096, 1024], P('wide')
- grad_gain_attn: float32 [1024], P('wide')
- grad_gain_mlp: float32 [1024], P('wide')
- grad_router: float32 [1024], replicated
The draws below stay inside these ranges and needn't reach their ends.
Inputs may be any that keep to these rules, and one draw needn't show every extreme that they name: `lengths`: each run of 2 consecutive sequences holds one of length 2048. `routes`: the first lengths[s] // 8 entries of row s are distinct positions below lengths[s], ascending; the remaining entries are 2047 and unused.
All inputs are finite; a program needn't handle non-finite values.
Results may differ from the reference program's by a relative error of at most 0.012.
Values may be sent and summed in bfloat16 or wider, within the bound.
A program may use at most 192 MiB of HBM per device.

```python
import math
import jax
import jax.numpy as jnp
from jax import lax

D = 1024
HEADS = 16
HEAD_DIM = 64
FF = 4096
SEQ_DEV = 2
SLOTS = 2048
MIN_LEN = 256
KCAP = 256
SEQS = 32


def seq_lengths(key):
    base = jax.random.randint(jax.random.fold_in(key, 11), (SEQS,), MIN_LEN, SLOTS + 1)
    chosen = jax.random.randint(jax.random.fold_in(key, 12), (SEQS // SEQ_DEV,), 0, SEQ_DEV)
    full_len = jnp.arange(SEQS) % SEQ_DEV == jnp.repeat(chosen, SEQ_DEV)
    return jnp.where(full_len, SLOTS, base).astype(jnp.int32)


def draw_lengths(key, part):
    shared = seq_lengths(key)
    return shared


def draw_routes(key, part):
    lengths = seq_lengths(key)
    key = jax.random.fold_in(key, 2)
    scores = jax.random.randint(key, (SEQS, SLOTS), 0, 1 << 19) * SLOTS + jnp.arange(SLOTS)[None, :]
    positions = jnp.arange(SLOTS)[None, :]
    scores = jnp.where(positions < lengths[:, None], scores, -1)
    top_vals, picked = lax.top_k(scores, KCAP)
    counts = lengths // 8
    column = jnp.arange(KCAP)[None, :]
    picked = jnp.where(column < counts[:, None], picked, SLOTS)
    picked = jnp.sort(picked, axis=1)
    return jnp.where(picked == SLOTS, SLOTS - 1, picked).astype(jnp.int32)


def shard_levels(own_key, extent, shards, least, top_value):
    level, own = 1.0, jax.random.fold_in(own_key, 6)
    for axis_at, shards_of in shards:
        heights = jnp.exp(jax.random.uniform(jax.random.fold_in(own, axis_at), (shards_of,), jnp.float32, least / len(shards), top_value / len(shards)))
        level = level * jnp.repeat(heights, extent[axis_at] // shards_of).reshape([-1 if axis == axis_at else 1 for axis in range(len(extent))])
    return level


def gaussian(key, extent, deviation, most, shards=(), held_as=jnp.bfloat16):
    result = jax.random.normal(key, extent, jnp.float32) * deviation
    if len(shards) > 0:
        result = shard_levels(key, extent, shards, -0.22, 0.18) * result
    return jnp.clip(result, min=-most, max=most).astype(held_as)


def setup_inputs(seed: int = 0) -> dict:
    seeds = jax.random.split(jax.random.key(seed), 12)
    tokens = gaussian(seeds[0], (SEQS, SLOTS, D), 1.0, 6.0, ((0, 16), (1, 2)))
    cotangent = gaussian(seeds[1], (SEQS, SLOTS, D), 1.0, 6.0, ((0, 16), (1, 2)))
    lengths = draw_lengths(jax.random.fold_in(seeds[11], 71), 0)
    routes = draw_routes(jax.random.fold_in(seeds[11], 71), 0)
    w_qkv = gaussian(seeds[4], (D, 3 * D), D ** -0.5, 0.1875, ((0, 16),))
    w_out = gaussian(seeds[5], (D, D), (D // 16) ** -0.5, 0.75, ((0, 16),))
    w_up = gaussian(seeds[6], (D, FF), D ** -0.5, 0.1875, ((0, 16),))
    w_down = gaussian(seeds[7], (FF, D), FF ** -0.5, 0.09375, ((0, 16),))
    gain_attn = jnp.clip(1.0 + 0.18 * jax.random.normal(seeds[8], (D,), jnp.float32), 0.099609375, 1.8984375).astype(jnp.bfloat16)
    gain_mlp = jnp.clip(1.0 + 0.18 * jax.random.normal(seeds[9], (D,), jnp.float32), 0.099609375, 1.8984375).astype(jnp.bfloat16)
    router = gaussian(seeds[10], (D,), D ** -0.5, 0.1875)
    return dict(tokens=tokens, cotangent=cotangent, lengths=lengths, routes=routes, w_qkv=w_qkv, w_out=w_out, w_up=w_up, w_down=w_down, gain_attn=gain_attn, gain_mlp=gain_mlp, router=router)


epsilon = 1e-06
masked_score = -1e+30

@jax.custom_vjp
def low(v):
    return lax.optimization_barrier(v.astype(jnp.bfloat16)).astype(jnp.float32)

@jax.custom_vjp
def low_back(v):
    return v

def low_keep(v):
    return (low(v), None)

def low_pass(kept, grad):
    return (grad,)

def back_keep(v):
    return (v, None)

def back_low(kept, grad):
    return (low(grad),)
low.defvjp(low_keep, low_pass)
low_back.defvjp(back_keep, back_low)

def matmul_high(left, right):
    return jnp.matmul(left, right, precision=lax.Precision.HIGHEST)

def rms_scale(values, gain):
    return values * lax.rsqrt(lax.optimization_barrier(jnp.mean(values * values, axis=-1, keepdims=True)) + epsilon) * gain

def layer_rows(inputs_rows, counts, w_qkv, w_out, w_up, w_down, gain_attn, gain_mlp, router):
    groups, entries, width = inputs_rows.shape
    normed = low(rms_scale(inputs_rows, gain_attn))
    project = low_back(low(matmul_high(normed, w_qkv)))
    queries = project[..., :width].reshape(groups, entries, HEADS, HEAD_DIM)
    key_rows = project[..., width:2 * width].reshape(groups, entries, HEADS, HEAD_DIM)
    value_rows = project[..., 2 * width:].reshape(groups, entries, HEADS, HEAD_DIM)
    scores = jnp.einsum('gqhe,gkhe->ghqk', queries, key_rows, precision=lax.Precision.HIGHEST) * 0.125
    scores = low_back(scores)
    order = jnp.arange(entries, dtype=jnp.int32)
    allowed = (order[None, None, None, :] <= order[None, None, :, None]) & (order[None, None, None, :] < counts[:, None, None, None])
    scores = jnp.where(allowed, scores, masked_score)
    top_score = lax.optimization_barrier(jnp.max(scores, axis=-1, keepdims=True))
    expo = jnp.exp(scores - top_score)
    probs = low(expo / lax.optimization_barrier(jnp.sum(expo, axis=-1, keepdims=True)))
    heads_out = jnp.einsum('ghqk,gkhe->gqhe', probs, value_rows, precision=lax.Precision.HIGHEST)
    heads_out = low_back(low(heads_out.reshape(groups, entries, width)))
    attend_out = low_back(matmul_high(heads_out, w_out))
    middle = inputs_rows + attend_out
    normed_two = low(rms_scale(middle, gain_mlp))
    pre_act = low_back(matmul_high(normed_two, w_up))
    activated = low(jax.nn.gelu(pre_act))
    mlp_out = low_back(matmul_high(activated, w_down))
    router_val = matmul_high(inputs_rows, router)
    return inputs_rows + router_val[..., None] * (attend_out + mlp_out)

def reference(tokens, cotangent, lengths, routes, w_qkv, w_out, w_up, w_down, gain_attn, gain_mlp, router):
    counts = (lengths // 8).astype(jnp.int32)
    group = math.gcd(SEQS, max(1, 4096 // KCAP))
    steps_count = SEQS // group
    params32 = (w_qkv.astype(jnp.float32), w_out.astype(jnp.float32), w_up.astype(jnp.float32), w_down.astype(jnp.float32), gain_attn.astype(jnp.float32), gain_mlp.astype(jnp.float32), router.astype(jnp.float32))
    entry = jnp.arange(KCAP, dtype=jnp.int32)
    live = entry[None, :] < counts[:, None]

    def one_group(totals, block_index):
        start = (block_index * group).astype(jnp.int32)
        tok_block = lax.dynamic_slice_in_dim(tokens, start, group, 0).astype(jnp.float32)
        cot_block = lax.dynamic_slice_in_dim(cotangent, start, group, 0).astype(jnp.float32)
        route_block = lax.dynamic_slice_in_dim(routes, start, group, 0).astype(jnp.int32)
        count_block = lax.dynamic_slice_in_dim(counts, start, group, 0)
        live_block = lax.dynamic_slice_in_dim(live, start, group, 0)
        inputs_rows = jnp.take_along_axis(tok_block, route_block[:, :, None], axis=1)
        cot_rows = jnp.take_along_axis(cot_block, route_block[:, :, None], axis=1)
        cot_rows = jnp.where(live_block[:, :, None], cot_rows, jnp.zeros_like(cot_rows))

        def forward(rows_in, p_qkv, p_out, p_up, p_down, p_gain_a, p_gain_m, p_router):
            return layer_rows(rows_in, count_block, p_qkv, p_out, p_up, p_down, p_gain_a, p_gain_m, p_router)
        out_rows, pullback = jax.vjp(forward, inputs_rows, params32[0], params32[1], params32[2], params32[3], params32[4], params32[5], params32[6])
        grads = pullback(cot_rows)
        new_totals = tuple((total + grad for total, grad in zip(totals, grads[1:])))
        return (new_totals, (out_rows, grads[0]))
    init = tuple((jnp.zeros_like(param) for param in params32))
    totals, (out_rows, grad_rows) = lax.scan(one_group, init, jnp.arange(steps_count, dtype=jnp.int32))
    out_rows = out_rows.reshape(SEQS, KCAP, -1)
    grad_rows = grad_rows.reshape(SEQS, KCAP, -1)
    target = jnp.where(live, routes, SLOTS).astype(jnp.int32)
    put = jax.vmap(lambda base, where_to, fresh: base.at[where_to].set(fresh, mode='drop'))
    mixed = put(tokens, target, out_rows.astype(jnp.bfloat16))
    grad_tokens = put(cotangent, target, grad_rows.astype(jnp.bfloat16))
    return (mixed, grad_tokens, totals[0], totals[1], totals[2], totals[3], totals[4], totals[5], totals[6])
```

```python
import functools

import jax
import jax.numpy as jnp
from jax import lax
from jax.experimental import pallas as pl
from jax.experimental.pallas import tpu as pltpu
from jax.sharding import PartitionSpec as P

HEAD_DIM = 64
MESH = pl.DeviceIdType.MESH
F32 = jnp.float32
BF16 = jnp.bfloat16

epsilon = 1e-06
masked_score = -1e30


def rms_parts(values):
    inverse = lax.rsqrt(jnp.mean(values * values, axis=-1, keepdims=True) + epsilon)
    return (values * inverse, inverse)


def rms_back(grad_normed, normed, inverse):
    return inverse * (grad_normed - normed * jnp.mean(grad_normed * normed, axis=-1, keepdims=True))


def attend_scores(queries, keys_all, allowed):
    scores = (
        jnp.einsum("sqhe,skhe->shqk", queries, keys_all, preferred_element_type=jnp.float32) * 0.125
    )
    return jnp.where(allowed, scores, masked_score)


def attend_forward(queries, keys_all, values_all, allowed):
    scores = attend_scores(queries, keys_all, allowed)
    top_score = jnp.max(scores, axis=-1, keepdims=True)
    expo = jnp.exp(scores - top_score)
    total = jnp.sum(expo, axis=-1, keepdims=True)
    log_total = top_score + jnp.log(total)
    probs_low = (expo / total).astype(jnp.bfloat16)
    heads_out = jnp.einsum(
        "shqk,skhe->sqhe", probs_low, values_all, preferred_element_type=jnp.float32
    )
    return (heads_out, log_total)


def attend_backward(queries, keys_all, values_all, allowed, log_total, d_heads):
    probs_again = jnp.exp(attend_scores(queries, keys_all, allowed) - log_total)
    d_probs = jnp.einsum("sqhe,skhe->shqk", d_heads, values_all, preferred_element_type=jnp.float32)
    row_dot = jnp.sum(probs_again * d_probs, axis=-1, keepdims=True)
    d_scores = (probs_again * (d_probs - row_dot)).astype(jnp.bfloat16)
    d_queries = (
        jnp.einsum("shqk,skhe->sqhe", d_scores, keys_all, preferred_element_type=jnp.float32)
        * 0.125
    )
    d_key_part = (
        jnp.einsum("shqk,sqhe->skhe", d_scores, queries, preferred_element_type=jnp.float32) * 0.125
    )
    d_value_part = jnp.einsum(
        "shqk,sqhe->skhe",
        probs_again.astype(jnp.bfloat16),
        d_heads,
        preferred_element_type=jnp.float32,
    )
    return (d_queries, d_key_part, d_value_part)


def general_body(
    tokens, cotangent, lengths, routes, w_qkv, w_out, w_up, w_down, gain_attn, gain_mlp, router
):
    parts_narrow = lax.axis_size("narrow")
    place = lax.axis_index("narrow")
    seqs, span, width = tokens.shape
    list_len = routes.shape[1]
    own_entries = list_len // parts_narrow
    rows_total = seqs * own_entries
    counts = lengths // 8
    entry = jnp.arange(list_len, dtype=jnp.int32)
    live = entry[None, :] < counts[:, None]
    local_slot = routes - place * span
    mine = live & (local_slot >= 0) & (local_slot < span)
    pick = jnp.clip(local_slot, 0, span - 1)
    keep = mine[:, :, None]
    taken_in = jnp.take_along_axis(tokens, pick[:, :, None], axis=1)
    taken_cot = jnp.take_along_axis(cotangent, pick[:, :, None], axis=1)
    blank = jnp.zeros_like(taken_in)
    rows_in, rows_cot = (
        lax.psum_scatter(
            jnp.where(keep, taken_in, blank), "narrow", scatter_dimension=1, tiled=True
        ).astype(jnp.float32),
        lax.psum_scatter(
            jnp.where(keep, taken_cot, blank), "narrow", scatter_dimension=1, tiled=True
        ).astype(jnp.float32),
    )
    inputs_rows = rows_in.reshape(rows_total, width)
    inputs_low = inputs_rows.astype(jnp.bfloat16)
    dout = rows_cot.reshape(rows_total, width)
    gathered = (
        lax.all_gather(w_qkv, "wide", axis=0, tiled=True),
        lax.all_gather(w_out, "wide", axis=0, tiled=True),
        lax.all_gather(w_up, "wide", axis=0, tiled=True),
        lax.all_gather(w_down, "wide", axis=0, tiled=True),
        lax.all_gather(gain_attn, "wide", axis=0, tiled=True),
        lax.all_gather(gain_mlp, "wide", axis=0, tiled=True),
    )
    weight_qkv, weight_out, weight_up, weight_down, gain_first, gain_second = gathered
    scale_first = gain_first.astype(jnp.float32)
    scale_second = gain_second.astype(jnp.float32)
    normed_one, inverse_one = rms_parts(inputs_rows)
    normed_low = (normed_one * scale_first).astype(jnp.bfloat16)
    project = jnp.dot(normed_low, weight_qkv, preferred_element_type=jnp.float32).astype(
        jnp.bfloat16
    )
    queries = project[:, :width].reshape(seqs, own_entries, -1, HEAD_DIM)
    key_own = project[:, width : 2 * width].reshape(seqs, own_entries, width)
    value_own = project[:, 2 * width :].reshape(seqs, own_entries, width)
    keys_all, values_all = (
        lax.all_gather(key_own, "narrow", axis=1, tiled=True),
        lax.all_gather(value_own, "narrow", axis=1, tiled=True),
    )
    keys_all = keys_all.reshape(seqs, list_len, -1, HEAD_DIM)
    values_all = values_all.reshape(seqs, list_len, -1, HEAD_DIM)
    query_pos = place * own_entries + jnp.arange(own_entries, dtype=jnp.int32)
    allowed = (entry[None, None, None, :] <= query_pos[None, None, :, None]) & (
        entry[None, None, None, :] < counts[:, None, None, None]
    )
    heads_out, log_total = attend_forward(queries, keys_all, values_all, allowed)
    heads_low = heads_out.reshape(rows_total, width).astype(jnp.bfloat16)
    attend_out = jnp.dot(heads_low, weight_out, preferred_element_type=jnp.float32)
    middle = inputs_rows + attend_out
    normed_two, inverse_two = rms_parts(middle)
    second_low = (normed_two * scale_second).astype(jnp.bfloat16)
    pre_act = jnp.dot(second_low, weight_up, preferred_element_type=jnp.float32)
    activ_full, gelu_back = jax.vjp(jax.nn.gelu, pre_act)
    activ_low = activ_full.astype(jnp.bfloat16)
    mlp_out = jnp.dot(activ_low, weight_down, preferred_element_type=jnp.float32)
    branch = attend_out + mlp_out
    router_val = jnp.dot(inputs_low, router, preferred_element_type=jnp.float32)
    out_low = (inputs_rows + router_val[:, None] * branch).astype(jnp.bfloat16)
    back_set = (
        lax.all_gather(w_qkv, "wide", axis=0, tiled=True),
        lax.all_gather(w_out, "wide", axis=0, tiled=True),
        lax.all_gather(w_up, "wide", axis=0, tiled=True),
        lax.all_gather(w_down, "wide", axis=0, tiled=True),
        lax.all_gather(gain_attn, "wide", axis=0, tiled=True),
        lax.all_gather(gain_mlp, "wide", axis=0, tiled=True),
    )
    back_qkv, back_out, back_up, back_down, back_gain_a, back_gain_m = back_set
    back_first = back_gain_a.astype(jnp.float32)
    back_second = back_gain_m.astype(jnp.float32)
    d_branch = router_val[:, None] * dout
    d_router_val = jnp.sum(dout * branch, axis=-1)
    d_mlp = d_branch.astype(jnp.bfloat16)
    grad_down_full = jnp.einsum("rf,rd->fd", activ_low, d_mlp, preferred_element_type=jnp.float32)
    d_act = jnp.einsum("rd,fd->rf", d_mlp, back_down, preferred_element_type=jnp.float32)
    d_pre = gelu_back(d_act)[0].astype(jnp.bfloat16)
    grad_up_full = jnp.einsum("rd,rf->df", second_low, d_pre, preferred_element_type=jnp.float32)
    d_normed_two = jnp.einsum("rf,df->rd", d_pre, back_up, preferred_element_type=jnp.float32)
    grad_gain_two = jnp.sum(d_normed_two * normed_two, axis=0)
    d_middle = rms_back(d_normed_two * back_second, normed_two, inverse_two)
    d_attend = (d_branch + d_middle).astype(jnp.bfloat16)
    grad_out_full = jnp.einsum("rd,re->de", heads_low, d_attend, preferred_element_type=jnp.float32)
    d_heads = jnp.einsum(
        "re,de->rd", d_attend, back_out, preferred_element_type=jnp.float32
    ).astype(jnp.bfloat16)
    d_heads_own = d_heads.reshape(seqs, own_entries, -1, HEAD_DIM)
    d_queries, d_key_part, d_value_part = attend_backward(
        queries, keys_all, values_all, allowed, log_total, d_heads_own
    )
    d_key_own, d_value_own = (
        lax.psum_scatter(
            d_key_part.reshape(seqs, list_len, width), "narrow", scatter_dimension=1, tiled=True
        ),
        lax.psum_scatter(
            d_value_part.reshape(seqs, list_len, width), "narrow", scatter_dimension=1, tiled=True
        ),
    )
    d_project = jnp.concatenate(
        [
            d_queries.reshape(rows_total, width),
            d_key_own.reshape(rows_total, width),
            d_value_own.reshape(rows_total, width),
        ],
        axis=-1,
    ).astype(jnp.bfloat16)
    grad_qkv_full = jnp.einsum(
        "rd,re->de", normed_low, d_project, preferred_element_type=jnp.float32
    )
    d_normed = jnp.einsum("re,de->rd", d_project, back_qkv, preferred_element_type=jnp.float32)
    grad_gain_one = jnp.sum(d_normed * normed_one, axis=0)
    d_norm_rows = rms_back(d_normed * back_first, normed_one, inverse_one)
    d_rows = dout + d_middle + d_norm_rows + d_router_val[:, None] * router.astype(jnp.float32)
    grad_router_part = jnp.dot(d_router_val, inputs_rows, precision=lax.Precision.HIGHEST)
    grad_low = d_rows.astype(jnp.bfloat16)
    out_all, grad_all = (
        lax.all_gather(out_low.reshape(seqs, own_entries, width), "narrow", axis=1, tiled=True),
        lax.all_gather(grad_low.reshape(seqs, own_entries, width), "narrow", axis=1, tiled=True),
    )
    target = jnp.where(mine, pick, span)
    put = jax.vmap(lambda base, where_to, fresh: base.at[where_to].set(fresh, mode="drop"))
    mixed = put(tokens, target, out_all)
    grad_tokens = put(cotangent, target, grad_all)
    shards = (
        lax.psum_scatter(grad_qkv_full, "wide", scatter_dimension=0, tiled=True),
        lax.psum_scatter(grad_out_full, "wide", scatter_dimension=0, tiled=True),
        lax.psum_scatter(grad_up_full, "wide", scatter_dimension=0, tiled=True),
        lax.psum_scatter(grad_down_full, "wide", scatter_dimension=0, tiled=True),
        lax.psum_scatter(grad_gain_one, "wide", scatter_dimension=0, tiled=True),
        lax.psum_scatter(grad_gain_two, "wide", scatter_dimension=0, tiled=True),
    )
    summed = lax.psum((shards[0], shards[1], shards[2], shards[3], shards[4], shards[5]), "narrow")
    grad_router = lax.psum(grad_router_part, ("wide", "narrow"))
    return (
        mixed,
        grad_tokens,
        summed[0],
        summed[1],
        summed[2],
        summed[3],
        summed[4],
        summed[5],
        grad_router,
    )


def dot(left, right):
    return jnp.dot(left, right, preferred_element_type=F32)


def dot_nt(left, right):
    return lax.dot_general(left, right, (((1,), (1,)), ((), ())), preferred_element_type=F32)


def dot_tn(left, right):
    return lax.dot_general(left, right, (((0,), (0,)), ((), ())), preferred_element_type=F32)


class Place:
    def __init__(self, wide):
        self.ring = wide // 2
        self.length = self.ring // 2
        self.w = lax.axis_index("wide")
        self.n = lax.axis_index("narrow")
        self.c = self.w % 2
        self.q = self.w // 2
        row = self.q % 2
        col = self.q // 2
        self.r = col + row * (2 * self.length - 1 - 2 * col)

    def chip(self, ring_pos):
        pos = lax.rem(ring_pos + 2 * self.ring, self.ring)
        row = pos // self.length
        col = pos + row * (2 * self.length - 1 - 2 * pos)
        return col * 2 + row

    def at_ring(self, ring_pos):
        return (self.chip(ring_pos) * 2 + self.c, self.n)

    def sibling(self):
        return (self.q * 2 + 1 - self.c, self.n)

    def across(self):
        return (self.w, 1 - self.n)

    def flipped(self, bit):
        return ((self.q + bit - 2 * bit * ((self.q // bit) % 2)) * 2 + self.c, self.n)


def greet(partners):
    barrier = pltpu.get_barrier_semaphore()
    for partner in partners:
        pl.semaphore_signal(barrier, inc=1, device_id=partner, device_id_type=MESH)
    pl.semaphore_wait(barrier, len(partners))


def remote(src, dst, send, recv, device):
    return pltpu.make_async_remote_copy(
        src_ref=src, dst_ref=dst, send_sem=send, recv_sem=recv, device_id=device, device_id_type=MESH
    )


def gather_kernel(
    wide,
    gains,
    wq,
    wo,
    wu,
    wd,
    rows,
    gains_all,
    wq_all,
    wo_all,
    wu_all,
    wd_all,
    rows_got,
    own_sem,
    ring_send,
    ring_recv,
    sib_send,
    sib_recv,
    x_send,
    x_recv,
):
    at = Place(wide)
    ring, steps = at.ring, at.ring // 2
    depth = wo.shape[0]
    width = wo.shape[1]
    parts = [(gains, gains_all, gains.shape[0], 0, gains.shape[0], 0, gains.shape[1])]
    parts += [(wq, wq_all, depth, 0, depth, j * width, width) for j in range(3)]
    parts += [(wo, wo_all, depth, 0, depth, 0, width)]
    parts += [(wu, wu_all, depth, 0, depth, j * width, width) for j in range(wu.shape[1] // width)]
    parts += [
        (wd, wd_all, wd.shape[0], j * depth, depth, 0, width) for j in range(wd.shape[0] // depth)
    ]

    def block(k, ring_pos, core, half, own):
        src, dst, shard, first, taken, col, cols = parts[k]
        size = taken if half is None else taken // 2
        low = first + (0 if half is None else half * size)
        if own:
            return src.at[pl.ds(low, size), pl.ds(col, cols)]
        base = (at.chip(ring_pos) * 2 + core) * shard + low
        return dst.at[pl.ds(pl.multiple_of(base, 8), size), pl.ds(col, cols)]

    def half_of(s, d):
        return d if s == steps else None

    def ring_out(k, s, d):
        pos = at.r - (s - 1) if d == 0 else at.r + (s - 1)
        half = half_of(s, d)
        src = block(k, pos, at.c, half, s == 1)
        dst = block(k, pos, at.c, half, False)
        to = at.at_ring(at.r + 1 if d == 0 else at.r - 1)
        return remote(src, dst, ring_send.at[k, s - 1, d], ring_recv.at[k, s - 1, d], to)

    def ring_in(k, s, d):
        pos = at.r - s if d == 0 else at.r + s
        ref = block(k, pos, at.c, half_of(s, d), False)
        to = at.at_ring(at.r + 1 if d == 0 else at.r - 1)
        return remote(ref, ref, ring_send.at[k, s - 1, d], ring_recv.at[k, s - 1, d], to)

    def sib(k, s, d, core):
        pos = at.r - s if d == 0 else at.r + s
        half = half_of(s, d)
        j = 0 if s == 0 else 1 + 2 * (s - 1) + d
        dst = block(k, pos, core, half, False)
        src = block(k, pos, core, half, s == 0)
        return remote(src, dst, sib_send.at[k, j], sib_recv.at[k, j], at.sibling())

    greet([at.at_ring(at.r + 1), at.at_ring(at.r - 1), at.sibling(), at.across()])
    cross = remote(rows, rows_got, x_send, x_recv, at.across())
    cross.start()
    count = len(parts)
    for i in range(count + steps):
        if i < count:
            for d in (0, 1):
                ring_out(i, 1, d).start()
            sib(i, 0, 0, at.c).start()
            pltpu.make_async_copy(
                block(i, at.r, at.c, None, True), block(i, at.r, at.c, None, False), own_sem.at[i]
            ).start()
        for s in range(1, steps + 1):
            k = i - s
            if 0 <= k < count:
                for d in (0, 1):
                    ring_in(k, s, d).wait_recv()
                    if s < steps:
                        if s + 1 < steps or d == 0:
                            ring_out(k, s + 1, d).start()
                        else:
                            ring_out(k, s + 1, d).start()
                    sib(k, s, d, at.c).start()
    for k in range(count):
        pltpu.make_async_copy(
            block(k, at.r, at.c, None, True), block(k, at.r, at.c, None, False), own_sem.at[k]
        ).wait()
        sib(k, 0, 0, at.c).wait_send()
        sib(k, 0, 0, 1 - at.c).wait_recv()
        for s in range(1, steps + 1):
            for d in (0, 1):
                ring_out(k, s, d).wait_send()
                sib(k, s, d, at.c).wait_send()
                sib(k, s, d, 1 - at.c).wait_recv()
    cross.wait()


def gather_weights(wide, gains, wq, wo, wu, wd, rows):
    count = 1 + 3 + 1 + wu.shape[1] // wo.shape[1] + wd.shape[0] // wo.shape[0]
    steps = wide // 4
    full = [jax.ShapeDtypeStruct((wide * a.shape[0], a.shape[1]), a.dtype) for a in (gains, wq, wo, wu, wd)]
    anywhere = pl.BlockSpec(memory_space=pl.ANY)
    return pl.pallas_call(
        functools.partial(gather_kernel, wide),
        out_shape=full + [jax.ShapeDtypeStruct(rows.shape, rows.dtype)],
        in_specs=[anywhere] * 6,
        out_specs=[anywhere] * 6,
        scratch_shapes=[
            pltpu.SemaphoreType.DMA((count,)),
            pltpu.SemaphoreType.DMA((count, steps, 2)),
            pltpu.SemaphoreType.DMA((count, steps, 2)),
            pltpu.SemaphoreType.DMA((count, 1 + 2 * steps)),
            pltpu.SemaphoreType.DMA((count, 1 + 2 * steps)),
            pltpu.SemaphoreType.DMA,
            pltpu.SemaphoreType.DMA,
        ],
        compiler_params=pltpu.CompilerParams(collective_id=1, has_side_effects=True),
        name="gather",
    )(gains, wq, wo, wu, wd, rows)


def reduce_kernel(
    wide,
    act_t,
    second_t,
    heads_t,
    normed_t,
    d_mlp,
    d_pre,
    d_attend,
    d_project,
    small,
    rows,
    o_qkv,
    o_out,
    o_up,
    o_down,
    o_small,
    rows_got,
    own,
    to_sib,
    mine,
    moving,
    x_out,
    x_in,
    small_acc,
    small_in,
    sib_send,
    sib_recv,
    ring_send,
    ring_recv,
    x_send,
    x_recv,
    small_send,
    small_recv,
    row_send,
    row_recv,
):
    at = Place(wide)
    ring, steps = at.ring, at.ring // 2
    depth, width = o_out.shape
    half = depth // 2
    ups, downs = o_up.shape[1] // width, o_down.shape[0] // depth
    rows_in = d_mlp.shape[0]
    count = downs + ups + 1 + 3
    tile = 256

    def operands(k):
        if k < downs:
            return lambda core: act_t[:, core, k], d_mlp, 0
        k -= downs
        if k < ups:
            return lambda core: second_t[:, core], d_pre, k * width
        k -= ups
        if k < 1:
            return lambda core: heads_t[:, core], d_attend, 0
        return lambda core: normed_t[:, core], d_project, (k - 1) * width

    def product(k, core, put):
        left, right, first = operands(k)
        tall = left(core).reshape(ring * depth, rows_in)

        @pl.loop(0, width // tile)
        def _(t):
            cols = pl.ds(pl.multiple_of(t * tile, tile), tile)
            from_cols = pl.ds(pl.multiple_of(first + t * tile, tile), tile)
            put(cols, dot(tall, right[:, from_cols]).reshape(ring, depth, tile))

    def store(k):
        if k < downs:
            return o_down, k * depth, 0
        k -= downs
        if k < ups:
            return o_up, 0, k * width
        k -= ups
        if k < 1:
            return o_out, 0, 0
        return o_qkv, 0, (k - 1) * width

    def sib(k):
        return remote(
            to_sib.at[k % 2], mine.at[k], sib_send.at[k], sib_recv.at[k], at.sibling()
        )

    def halves(d):
        return pl.ds(d * half, half)

    def ring_out(k, t, d):
        to = at.at_ring(at.r + 1 if d == 0 else at.r - 1)
        if t == 0:
            src = mine.at[k, at.chip(at.r + steps), halves(d)]
            dst = moving.at[k, 0, d, halves(d)]
        else:
            src = moving.at[k, t - 1, d]
            dst = moving.at[k, t, d]
        return remote(src, dst, ring_send.at[k, t, d], ring_recv.at[k, t, d], to)

    def ring_in(k, t, d):
        to = at.at_ring(at.r + 1 if d == 0 else at.r - 1)
        ref = moving.at[k, 0, d, halves(d)] if t == 0 else moving.at[k, t, d]
        return remote(ref, ref, ring_send.at[k, t, d], ring_recv.at[k, t, d], to)

    def cross(k):
        return remote(x_out.at[k], x_in.at[k], x_send.at[k], x_recv.at[k], at.across())

    bits = [1 << b for b in range(ring.bit_length() - 1)]
    partners = [at.sibling(), at.across()] + [at.flipped(bit) for bit in bits]
    stages = len(partners)

    def small_copy(j):
        return remote(
            small_acc.at[j], small_in.at[j], small_send.at[j], small_recv.at[j], partners[j]
        )

    greet(partners + [at.at_ring(at.r + 1), at.at_ring(at.r - 1)])
    rows_copy = remote(rows, rows_got, row_send, row_recv, at.across())
    rows_copy.start()
    small_acc[0] = small[...]
    step = 16

    for i in range(count + steps + 3):
        k = i
        if k < count:
            if k >= 2:
                sib(k - 2).wait_send()

            def keep_other(cols, value):
                to_sib[k % 2, :, :, cols] = value.astype(BF16)

            def keep_own(cols, value):
                own[k % 2, :, :, cols] = value

            product(k, 1 - at.c, keep_other)
            sib(k).start()
            product(k, at.c, keep_own)
        if i <= stages:
            if i > 0:
                small_copy(i - 1).wait_recv()
                small_acc[i] = small_acc[i - 1] + small_in[i - 1]
            if i < stages:
                small_copy(i).start()
            else:
                o_small[...] = small_acc[stages]
        k = i - 1
        if 0 <= k < count:
            sib(k).wait_recv()

            @pl.loop(0, ring)
            def _(chip):
                mine[k, chip] = (mine[k, chip].astype(F32) + own[k % 2, chip]).astype(BF16)

            for d in (0, 1):
                ring_out(k, 0, d).start()
        for t in range(1, steps):
            k = i - 1 - t
            if 0 <= k < count:
                for d in (0, 1):
                    ring_in(k, t - 1, d).wait_recv()
                    dest = at.chip(at.r + (steps - t) if d == 0 else at.r - (steps - t))
                    lows = range(0, depth, half) if t == 1 else (0,)
                    for low in lows:
                        size = half if t == 1 else depth

                        @pl.loop(0, size // step)
                        def _(g):
                            take = pl.ds(pl.multiple_of(low + g * step, step), step)
                            value = mine[k, dest, take]
                            if not (t == 1 and low != d * half):
                                value = (
                                    value.astype(F32) + moving[k, t - 1, d, take].astype(F32)
                                ).astype(BF16)
                            moving[k, t - 1, d, take] = value

                    ring_out(k, t, d).start()
        k = i - 1 - steps
        if 0 <= k < count:
            for d in (0, 1):
                ring_in(k, steps - 1, d).wait_recv()

            @pl.loop(0, depth // step)
            def _(g):
                take = pl.ds(pl.multiple_of(g * step, step), step)
                value = mine[k, at.q, take].astype(F32)
                value = value + moving[k, steps - 1, 0, take].astype(F32)
                value = value + moving[k, steps - 1, 1, take].astype(F32)
                x_out[k, take] = value.astype(BF16)

            cross(k).start()
        k = i - 2 - steps
        if 0 <= k < count:
            cross(k).wait_recv()
            out, low, first = store(k)

            @pl.loop(0, depth // step)
            def _(g):
                take = pl.ds(pl.multiple_of(g * step, step), step)
                put = pl.ds(pl.multiple_of(low + g * step, step), step)
                out[put, first : first + width] = x_out[k, take].astype(F32) + x_in[
                    k, take
                ].astype(F32)

    for k in range(count):
        if k >= count - 2:
            sib(k).wait_send()
        cross(k).wait_send()
        for t in range(steps):
            for d in (0, 1):
                ring_out(k, t, d).wait_send()
    for j in range(stages):
        small_copy(j).wait_send()
    rows_copy.wait()


def reduce_grads(
    wide, act_low, second_low, heads_low, normed_low, d_mlp, d_pre, d_attend, d_project, small, rows
):
    width = normed_low.shape[1]
    ring, steps = wide // 2, wide // 4
    depth = width // wide
    tokens_in = normed_low.shape[0]

    def tall(value):
        return value.T.reshape(ring, 2, depth, tokens_in)

    ff = act_low.shape[1]
    downs = ff // width
    act_t = act_low.T.reshape(ring, 2, downs, depth, tokens_in)
    count = 2 * downs + 4
    stages = 2 + (ring.bit_length() - 1)
    vmem = pl.BlockSpec(memory_space=pltpu.VMEM)
    anywhere = pl.BlockSpec(memory_space=pl.ANY)
    dma = pltpu.SemaphoreType.DMA
    return pl.pallas_call(
        functools.partial(reduce_kernel, wide),
        out_shape=[
            jax.ShapeDtypeStruct((depth, 3 * width), F32),
            jax.ShapeDtypeStruct((depth, width), F32),
            jax.ShapeDtypeStruct((depth, ff), F32),
            jax.ShapeDtypeStruct((ff // wide, width), F32),
            jax.ShapeDtypeStruct(small.shape, F32),
            jax.ShapeDtypeStruct(rows.shape, rows.dtype),
        ],
        in_specs=[vmem] * 9 + [anywhere],
        out_specs=[vmem] * 5 + [anywhere],
        scratch_shapes=[
            pltpu.VMEM((2, ring, depth, width), F32),
            pltpu.VMEM((2, ring, depth, width), BF16),
            pltpu.VMEM((count, ring, depth, width), BF16),
            pltpu.VMEM((count, steps, 2, depth, width), BF16),
            pltpu.VMEM((count, depth, width), BF16),
            pltpu.VMEM((count, depth, width), BF16),
            pltpu.VMEM((stages + 1,) + small.shape, F32),
            pltpu.VMEM((stages,) + small.shape, F32),
            dma((count,)),
            dma((count,)),
            dma((count, steps, 2)),
            dma((count, steps, 2)),
            dma((count,)),
            dma((count,)),
            dma((stages,)),
            dma((stages,)),
            dma,
            dma,
        ],
        compiler_params=pltpu.CompilerParams(
            collective_id=2, has_side_effects=True, vmem_limit_bytes=60 * 1024 * 1024
        ),
        name="reduce",
    )(
        act_t,
        tall(second_low),
        tall(heads_low),
        tall(normed_low),
        d_mlp,
        d_pre,
        d_attend,
        d_project,
        small,
        rows,
    )


def probabilities(count, queries, keys):
    entries = queries.shape[0]
    scores = dot_nt(queries, keys) * 0.125
    q_at = lax.broadcasted_iota(jnp.int32, (entries, entries), 0)
    k_at = lax.broadcasted_iota(jnp.int32, (entries, entries), 1)
    scores = jnp.where((k_at <= q_at) & (k_at < count), scores, masked_score)
    expo = jnp.exp(scores - jnp.max(scores, axis=-1, keepdims=True))
    return expo / jnp.sum(expo, axis=-1, keepdims=True)


def only(value, head):
    lane = lax.broadcasted_iota(jnp.int32, value.shape, 1)
    return jnp.where(lane // HEAD_DIM == head, value, jnp.zeros_like(value))


def attend_kernel(count, q, k, v, out):
    total = jnp.zeros(out.shape, F32)
    for head in (0, 1):
        probs = probabilities(count[0], only(q[...], head), k[...])
        total = total + only(dot(probs.astype(BF16), v[...]), head)
    out[...] = total.astype(BF16)


def attend_back_kernel(count, q, k, v, d_heads, d_project):
    d_q = jnp.zeros(q.shape, F32)
    d_k = jnp.zeros(q.shape, F32)
    d_v = jnp.zeros(q.shape, F32)
    for head in (0, 1):
        probs = probabilities(count[0], only(q[...], head), k[...])
        d_own = only(d_heads[...], head)
        d_probs = dot_nt(d_own, v[...])
        d_scores = probs * (d_probs - jnp.sum(probs * d_probs, axis=-1, keepdims=True))
        d_scores = d_scores.astype(BF16)
        d_q = d_q + only(dot(d_scores, k[...]), head)
        d_k = d_k + only(dot_tn(d_scores, q[...]), head)
        d_v = d_v + dot_tn(probs.astype(BF16), d_own)
    d_project[0] = (d_q * 0.125).astype(BF16)
    d_project[1] = (d_k * 0.125).astype(BF16)
    d_project[2] = d_v.astype(BF16)


def attend(count, project):
    entries = project.shape[0]
    width = project.shape[1] // 3
    pairs = width // (2 * HEAD_DIM)

    def third(j):
        return pl.BlockSpec((entries, 2 * HEAD_DIM), lambda p: (0, j * pairs + p))

    return pl.pallas_call(
        attend_kernel,
        grid=(pairs,),
        out_shape=jax.ShapeDtypeStruct((entries, width), BF16),
        in_specs=[pl.BlockSpec(memory_space=pltpu.SMEM), third(0), third(1), third(2)],
        out_specs=third(0),
        name="attend",
    )(count, project, project, project)


def attend_back(count, project, d_heads):
    entries = project.shape[0]
    width = project.shape[1] // 3
    pairs = width // (2 * HEAD_DIM)

    def third(j):
        return pl.BlockSpec((entries, 2 * HEAD_DIM), lambda p: (0, j * pairs + p))

    return pl.pallas_call(
        attend_back_kernel,
        grid=(pairs,),
        out_shape=jax.ShapeDtypeStruct((3, entries, width), BF16),
        in_specs=[pl.BlockSpec(memory_space=pltpu.SMEM), third(0), third(1), third(2), third(0)],
        out_specs=pl.BlockSpec((3, entries, 2 * HEAD_DIM), lambda p: (0, 0, p)),
        name="attend_back",
    )(count, project, project, project, d_heads)


def paired_body(
    wide, tokens, cotangent, lengths, routes, w_qkv, w_out, w_up, w_down, gain_attn, gain_mlp, router
):
    place = lax.axis_index("narrow")
    seqs, span, width = tokens.shape
    list_len = routes.shape[1]
    depth = gain_attn.shape[0]
    counts = lengths // 8
    entry = jnp.arange(list_len, dtype=jnp.int32)
    live = entry[None, :] < counts[:, None]
    local_slot = jnp.where(live, routes - place * span, -1)
    spots = jnp.arange(span, dtype=jnp.int32)
    chosen = (local_slot[:, :, None] == spots[None, None, :]).astype(BF16)

    def take(source):
        return jnp.einsum("sep,spd->sed", chosen, source, preferred_element_type=F32).astype(BF16)

    picked = jnp.stack([take(tokens), take(cotangent)])
    kept = lax.dynamic_index_in_dim(picked, place, 1, keepdims=False)
    given = lax.dynamic_index_in_dim(picked, 1 - place, 1, keepdims=False)
    gains = jnp.concatenate([gain_attn, gain_mlp]).reshape(1, 2 * depth)
    gains = jnp.pad(gains, ((0, 15), (0, 0)))
    gains_all, weight_qkv, weight_out, weight_up, weight_down, got = gather_weights(
        wide, gains, w_qkv, w_out, w_up, w_down, given
    )
    gains_all = gains_all.reshape(wide, 16, 2 * depth)[:, 0]
    scale_first = gains_all[:, :depth].reshape(width).astype(F32)
    scale_second = gains_all[:, depth:].reshape(width).astype(F32)
    both = kept + got
    inputs_low = both[0]
    inputs_rows = inputs_low.astype(F32)
    dout = both[1].astype(F32)
    count = lax.dynamic_slice_in_dim(counts, place, 1)

    normed_one, inverse_one = rms_parts(inputs_rows)
    normed_low = (normed_one * scale_first).astype(BF16)
    project = dot(normed_low, weight_qkv).astype(BF16)
    heads_low = attend(count, project)
    attend_out = dot(heads_low, weight_out)
    middle = inputs_rows + attend_out
    normed_two, inverse_two = rms_parts(middle)
    second_low = (normed_two * scale_second).astype(BF16)
    pre_act = dot(second_low, weight_up)
    activ_full, gelu_back = jax.vjp(jax.nn.gelu, pre_act)
    activ_low = activ_full.astype(BF16)
    mlp_out = dot(activ_low, weight_down)
    branch = attend_out + mlp_out
    router_row = router.astype(F32)[None, :]
    router_val = jnp.sum(inputs_rows * router_row, axis=-1, keepdims=True)
    out_low = (inputs_rows + router_val * branch).astype(BF16)

    d_branch = router_val * dout
    d_router_val = jnp.sum(dout * branch, axis=-1, keepdims=True)
    d_mlp = d_branch.astype(BF16)
    d_act = dot_nt(d_mlp, weight_down)
    d_pre = gelu_back(d_act)[0].astype(BF16)
    d_normed_two = dot_nt(d_pre, weight_up)
    grad_gain_two = jnp.sum(d_normed_two * normed_two, axis=0)
    d_middle = rms_back(d_normed_two * scale_second, normed_two, inverse_two)
    d_attend = (d_branch + d_middle).astype(BF16)
    d_heads = dot_nt(d_attend, weight_out).astype(BF16)
    d_parts = attend_back(count, project, d_heads)
    d_project = jnp.concatenate([d_parts[0], d_parts[1], d_parts[2]], axis=1)
    d_normed = dot_nt(d_project, weight_qkv)
    grad_gain_one = jnp.sum(d_normed * normed_one, axis=0)
    d_norm_rows = rms_back(d_normed * scale_first, normed_one, inverse_one)
    d_rows = dout + d_middle + d_norm_rows + d_router_val * router_row
    grad_router = jnp.sum(d_router_val * inputs_rows, axis=0)
    grad_low = d_rows.astype(BF16)

    small = jnp.pad(jnp.stack([grad_gain_one, grad_gain_two, grad_router]), ((0, 5), (0, 0)))
    back = jnp.stack([out_low, grad_low])
    grad_qkv, grad_out, grad_up, grad_down, small, back_got = reduce_grads(
        wide,
        activ_low,
        second_low,
        heads_low,
        normed_low,
        d_mlp,
        d_pre,
        d_attend,
        d_project,
        small,
        back,
    )
    first = place == 0
    rows_out = jnp.stack([jnp.where(first, back, back_got), jnp.where(first, back_got, back)], axis=1)
    hit = jnp.any(local_slot[:, :, None] == spots[None, None, :], axis=1)

    def put(base, fresh):
        spread = jnp.einsum("sep,sed->spd", chosen, fresh, preferred_element_type=F32)
        return jnp.where(hit[:, :, None], spread.astype(BF16), base)

    start = lax.axis_index("wide") * depth
    return (
        put(tokens, rows_out[0]),
        put(cotangent, rows_out[1]),
        grad_qkv,
        grad_out,
        grad_up,
        grad_down,
        lax.dynamic_slice_in_dim(small[0], start, depth),
        lax.dynamic_slice_in_dim(small[1], start, depth),
        small[2],
    )


def body(wide, narrow, tokens, *others):
    if narrow == 2 and tokens.shape[0] == 2 and wide >= 8 and wide & (wide - 1) == 0:
        return paired_body(wide, tokens, *others)
    return general_body(tokens, *others)


def solution(mesh):
    in_specs = (
        P("wide", "narrow", None),
        P("wide", "narrow", None),
        P("wide"),
        P("wide", None),
        P("wide", None),
        P("wide", None),
        P("wide", None),
        P("wide", None),
        P("wide"),
        P("wide"),
        P(),
    )
    out_specs = (
        P("wide", "narrow", None),
        P("wide", "narrow", None),
        P("wide", None),
        P("wide", None),
        P("wide", None),
        P("wide", None),
        P("wide"),
        P("wide"),
        P(),
    )
    sizes = mesh.shape["wide"], mesh.shape["narrow"]
    return jax.shard_map(functools.partial(body, *sizes), mesh=mesh, in_specs=in_specs, out_specs=out_specs, check_vma=False)
```

```python
import functools

import jax
import jax.numpy as jnp
from jax import lax
from jax.experimental import pallas as pl
from jax.experimental.pallas import tpu as pltpu
from jax.sharding import PartitionSpec as P

HEAD_DIM = 64
MESH = pl.DeviceIdType.MESH
F32 = jnp.float32
BF16 = jnp.bfloat16

epsilon = 1e-06
masked_score = -1e30


def rms_parts(values):
    inverse = lax.rsqrt(jnp.mean(values * values, axis=-1, keepdims=True) + epsilon)
    return (values * inverse, inverse)


def rms_back(grad_normed, normed, inverse):
    return inverse * (grad_normed - normed * jnp.mean(grad_normed * normed, axis=-1, keepdims=True))


def attend_scores(queries, keys_all, allowed):
    scores = (
        jnp.einsum("sqhe,skhe->shqk", queries, keys_all, preferred_element_type=jnp.float32) * 0.125
    )
    return jnp.where(allowed, scores, masked_score)


def attend_forward(queries, keys_all, values_all, allowed):
    scores = attend_scores(queries, keys_all, allowed)
    top_score = jnp.max(scores, axis=-1, keepdims=True)
    expo = jnp.exp(scores - top_score)
    total = jnp.sum(expo, axis=-1, keepdims=True)
    log_total = top_score + jnp.log(total)
    probs_low = (expo / total).astype(jnp.bfloat16)
    heads_out = jnp.einsum(
        "shqk,skhe->sqhe", probs_low, values_all, preferred_element_type=jnp.float32
    )
    return (heads_out, log_total)


def attend_backward(queries, keys_all, values_all, allowed, log_total, d_heads):
    probs_again = jnp.exp(attend_scores(queries, keys_all, allowed) - log_total)
    d_probs = jnp.einsum("sqhe,skhe->shqk", d_heads, values_all, preferred_element_type=jnp.float32)
    row_dot = jnp.sum(probs_again * d_probs, axis=-1, keepdims=True)
    d_scores = (probs_again * (d_probs - row_dot)).astype(jnp.bfloat16)
    d_queries = (
        jnp.einsum("shqk,skhe->sqhe", d_scores, keys_all, preferred_element_type=jnp.float32)
        * 0.125
    )
    d_key_part = (
        jnp.einsum("shqk,sqhe->skhe", d_scores, queries, preferred_element_type=jnp.float32) * 0.125
    )
    d_value_part = jnp.einsum(
        "shqk,sqhe->skhe",
        probs_again.astype(jnp.bfloat16),
        d_heads,
        preferred_element_type=jnp.float32,
    )
    return (d_queries, d_key_part, d_value_part)


def general_body(
    tokens, cotangent, lengths, routes, w_qkv, w_out, w_up, w_down, gain_attn, gain_mlp, router
):
    parts_narrow = lax.axis_size("narrow")
    place = lax.axis_index("narrow")
    seqs, span, width = tokens.shape
    list_len = routes.shape[1]
    own_entries = list_len // parts_narrow
    rows_total = seqs * own_entries
    counts = lengths // 8
    entry = jnp.arange(list_len, dtype=jnp.int32)
    live = entry[None, :] < counts[:, None]
    local_slot = routes - place * span
    mine = live & (local_slot >= 0) & (local_slot < span)
    pick = jnp.clip(local_slot, 0, span - 1)
    keep = mine[:, :, None]
    taken_in = jnp.take_along_axis(tokens, pick[:, :, None], axis=1)
    taken_cot = jnp.take_along_axis(cotangent, pick[:, :, None], axis=1)
    blank = jnp.zeros_like(taken_in)
    rows_in, rows_cot = (
        lax.psum_scatter(
            jnp.where(keep, taken_in, blank), "narrow", scatter_dimension=1, tiled=True
        ).astype(jnp.float32),
        lax.psum_scatter(
            jnp.where(keep, taken_cot, blank), "narrow", scatter_dimension=1, tiled=True
        ).astype(jnp.float32),
    )
    inputs_rows = rows_in.reshape(rows_total, width)
    inputs_low = inputs_rows.astype(jnp.bfloat16)
    dout = rows_cot.reshape(rows_total, width)
    gathered = (
        lax.all_gather(w_qkv, "wide", axis=0, tiled=True),
        lax.all_gather(w_out, "wide", axis=0, tiled=True),
        lax.all_gather(w_up, "wide", axis=0, tiled=True),
        lax.all_gather(w_down, "wide", axis=0, tiled=True),
        lax.all_gather(gain_attn, "wide", axis=0, tiled=True),
        lax.all_gather(gain_mlp, "wide", axis=0, tiled=True),
    )
    weight_qkv, weight_out, weight_up, weight_down, gain_first, gain_second = gathered
    scale_first = gain_first.astype(jnp.float32)
    scale_second = gain_second.astype(jnp.float32)
    normed_one, inverse_one = rms_parts(inputs_rows)
    normed_low = (normed_one * scale_first).astype(jnp.bfloat16)
    project = jnp.dot(normed_low, weight_qkv, preferred_element_type=jnp.float32).astype(
        jnp.bfloat16
    )
    queries = project[:, :width].reshape(seqs, own_entries, -1, HEAD_DIM)
    key_own = project[:, width : 2 * width].reshape(seqs, own_entries, width)
    value_own = project[:, 2 * width :].reshape(seqs, own_entries, width)
    keys_all, values_all = (
        lax.all_gather(key_own, "narrow", axis=1, tiled=True),
        lax.all_gather(value_own, "narrow", axis=1, tiled=True),
    )
    keys_all = keys_all.reshape(seqs, list_len, -1, HEAD_DIM)
    values_all = values_all.reshape(seqs, list_len, -1, HEAD_DIM)
    query_pos = place * own_entries + jnp.arange(own_entries, dtype=jnp.int32)
    allowed = (entry[None, None, None, :] <= query_pos[None, None, :, None]) & (
        entry[None, None, None, :] < counts[:, None, None, None]
    )
    heads_out, log_total = attend_forward(queries, keys_all, values_all, allowed)
    heads_low = heads_out.reshape(rows_total, width).astype(jnp.bfloat16)
    attend_out = jnp.dot(heads_low, weight_out, preferred_element_type=jnp.float32)
    middle = inputs_rows + attend_out
    normed_two, inverse_two = rms_parts(middle)
    second_low = (normed_two * scale_second).astype(jnp.bfloat16)
    pre_act = jnp.dot(second_low, weight_up, preferred_element_type=jnp.float32)
    activ_full, gelu_back = jax.vjp(jax.nn.gelu, pre_act)
    activ_low = activ_full.astype(jnp.bfloat16)
    mlp_out = jnp.dot(activ_low, weight_down, preferred_element_type=jnp.float32)
    branch = attend_out + mlp_out
    router_val = jnp.dot(inputs_low, router, preferred_element_type=jnp.float32)
    out_low = (inputs_rows + router_val[:, None] * branch).astype(jnp.bfloat16)
    back_set = (
        lax.all_gather(w_qkv, "wide", axis=0, tiled=True),
        lax.all_gather(w_out, "wide", axis=0, tiled=True),
        lax.all_gather(w_up, "wide", axis=0, tiled=True),
        lax.all_gather(w_down, "wide", axis=0, tiled=True),
        lax.all_gather(gain_attn, "wide", axis=0, tiled=True),
        lax.all_gather(gain_mlp, "wide", axis=0, tiled=True),
    )
    back_qkv, back_out, back_up, back_down, back_gain_a, back_gain_m = back_set
    back_first = back_gain_a.astype(jnp.float32)
    back_second = back_gain_m.astype(jnp.float32)
    d_branch = router_val[:, None] * dout
    d_router_val = jnp.sum(dout * branch, axis=-1)
    d_mlp = d_branch.astype(jnp.bfloat16)
    grad_down_full = jnp.einsum("rf,rd->fd", activ_low, d_mlp, preferred_element_type=jnp.float32)
    d_act = jnp.einsum("rd,fd->rf", d_mlp, back_down, preferred_element_type=jnp.float32)
    d_pre = gelu_back(d_act)[0].astype(jnp.bfloat16)
    grad_up_full = jnp.einsum("rd,rf->df", second_low, d_pre, preferred_element_type=jnp.float32)
    d_normed_two = jnp.einsum("rf,df->rd", d_pre, back_up, preferred_element_type=jnp.float32)
    grad_gain_two = jnp.sum(d_normed_two * normed_two, axis=0)
    d_middle = rms_back(d_normed_two * back_second, normed_two, inverse_two)
    d_attend = (d_branch + d_middle).astype(jnp.bfloat16)
    grad_out_full = jnp.einsum("rd,re->de", heads_low, d_attend, preferred_element_type=jnp.float32)
    d_heads = jnp.einsum(
        "re,de->rd", d_attend, back_out, preferred_element_type=jnp.float32
    ).astype(jnp.bfloat16)
    d_heads_own = d_heads.reshape(seqs, own_entries, -1, HEAD_DIM)
    d_queries, d_key_part, d_value_part = attend_backward(
        queries, keys_all, values_all, allowed, log_total, d_heads_own
    )
    d_key_own, d_value_own = (
        lax.psum_scatter(
            d_key_part.reshape(seqs, list_len, width), "narrow", scatter_dimension=1, tiled=True
        ),
        lax.psum_scatter(
            d_value_part.reshape(seqs, list_len, width), "narrow", scatter_dimension=1, tiled=True
        ),
    )
    d_project = jnp.concatenate(
        [
            d_queries.reshape(rows_total, width),
            d_key_own.reshape(rows_total, width),
            d_value_own.reshape(rows_total, width),
        ],
        axis=-1,
    ).astype(jnp.bfloat16)
    grad_qkv_full = jnp.einsum(
        "rd,re->de", normed_low, d_project, preferred_element_type=jnp.float32
    )
    d_normed = jnp.einsum("re,de->rd", d_project, back_qkv, preferred_element_type=jnp.float32)
    grad_gain_one = jnp.sum(d_normed * normed_one, axis=0)
    d_norm_rows = rms_back(d_normed * back_first, normed_one, inverse_one)
    d_rows = dout + d_middle + d_norm_rows + d_router_val[:, None] * router.astype(jnp.float32)
    grad_router_part = jnp.dot(d_router_val, inputs_rows, precision=lax.Precision.HIGHEST)
    grad_low = d_rows.astype(jnp.bfloat16)
    out_all, grad_all = (
        lax.all_gather(out_low.reshape(seqs, own_entries, width), "narrow", axis=1, tiled=True),
        lax.all_gather(grad_low.reshape(seqs, own_entries, width), "narrow", axis=1, tiled=True),
    )
    target = jnp.where(mine, pick, span)
    put = jax.vmap(lambda base, where_to, fresh: base.at[where_to].set(fresh, mode="drop"))
    mixed = put(tokens, target, out_all)
    grad_tokens = put(cotangent, target, grad_all)
    shards = (
        lax.psum_scatter(grad_qkv_full, "wide", scatter_dimension=0, tiled=True),
        lax.psum_scatter(grad_out_full, "wide", scatter_dimension=0, tiled=True),
        lax.psum_scatter(grad_up_full, "wide", scatter_dimension=0, tiled=True),
        lax.psum_scatter(grad_down_full, "wide", scatter_dimension=0, tiled=True),
        lax.psum_scatter(grad_gain_one, "wide", scatter_dimension=0, tiled=True),
        lax.psum_scatter(grad_gain_two, "wide", scatter_dimension=0, tiled=True),
    )
    summed = lax.psum((shards[0], shards[1], shards[2], shards[3], shards[4], shards[5]), "narrow")
    grad_router = lax.psum(grad_router_part, ("wide", "narrow"))
    return (
        mixed,
        grad_tokens,
        summed[0],
        summed[1],
        summed[2],
        summed[3],
        summed[4],
        summed[5],
        grad_router,
    )


def dot(left, right):
    return jnp.dot(left, right, preferred_element_type=F32)


def dot_nt(left, right):
    return lax.dot_general(left, right, (((1,), (1,)), ((), ())), preferred_element_type=F32)


def dot_tn(left, right):
    return lax.dot_general(left, right, (((0,), (0,)), ((), ())), preferred_element_type=F32)


class Place:
    def __init__(self, wide):
        self.ring = wide // 2
        self.length = self.ring // 2
        self.w = lax.axis_index("wide")
        self.n = lax.axis_index("narrow")
        self.c = self.w % 2
        self.q = self.w // 2
        row = self.q % 2
        col = self.q // 2
        self.r = col + row * (2 * self.length - 1 - 2 * col)

    def chip(self, ring_pos):
        pos = lax.rem(ring_pos + 2 * self.ring, self.ring)
        row = pos // self.length
        col = pos + row * (2 * self.length - 1 - 2 * pos)
        return col * 2 + row

    def at_ring(self, ring_pos):
        return (self.chip(ring_pos) * 2 + self.c, self.n)

    def sibling(self):
        return (self.q * 2 + 1 - self.c, self.n)

    def across(self):
        return (self.w, 1 - self.n)

    def flipped(self, bit):
        return ((self.q + bit - 2 * bit * ((self.q // bit) % 2)) * 2 + self.c, self.n)


def greet(partners):
    barrier = pltpu.get_barrier_semaphore()
    for partner in partners:
        pl.semaphore_signal(barrier, inc=1, device_id=partner, device_id_type=MESH)
    pl.semaphore_wait(barrier, len(partners))


def remote(src, dst, send, recv, device):
    return pltpu.make_async_remote_copy(
        src_ref=src, dst_ref=dst, send_sem=send, recv_sem=recv, device_id=device, device_id_type=MESH
    )


def probabilities(live, queries, keys):
    entries = queries.shape[0]
    scores = dot_nt(queries, keys) * 0.125
    q_at = lax.broadcasted_iota(jnp.int32, (entries, entries), 0)
    k_at = lax.broadcasted_iota(jnp.int32, (entries, entries), 1)
    scores = jnp.where((k_at <= q_at) & (live > 0), scores, masked_score)
    expo = jnp.exp(scores - jnp.max(scores, axis=-1, keepdims=True))
    return expo / jnp.sum(expo, axis=-1, keepdims=True)


def only(value, head):
    lane = lax.broadcasted_iota(jnp.int32, value.shape, 1)
    return jnp.where(lane // HEAD_DIM == head, value, jnp.zeros_like(value))


def gelu_pair(x):
    inner = 0.7978845608028654 * (x + 0.044715 * (x * x * x))
    bent = jnp.tanh(inner)
    half = 0.5 * (1.0 + bent)
    slope = 0.7978845608028654 * (1.0 + 0.134145 * (x * x))
    return x * half, half + 0.5 * x * (1.0 - bent * bent) * slope


def forward_kernel(
    wide,
    gains,
    wq,
    wo,
    wu,
    wd,
    kept,
    given,
    router,
    live,
    wq_all,
    wo_all,
    normed_t,
    heads_t,
    second_t,
    act_t,
    d_pre,
    d_mlp,
    d_attend,
    project,
    base,
    out_low,
    rows_low,
    small,
    scales,
    wu_all,
    wd_all,
    gains_all,
    got,
    normed,
    heads,
    attend_out,
    second_n,
    second,
    d_act,
    act,
    mlp_out,
    d_second,
    router_val,
    inverse_two,
    own_sem,
    ring_send,
    ring_recv,
    sib_send,
    sib_recv,
    x_send,
    x_recv,
    row_send,
    row_recv,
):
    at = Place(wide)
    ring, steps = at.ring, at.ring // 2
    depth, width = wo.shape
    quarter = depth // 4
    carried = depth - quarter
    entries = kept.shape[1]
    ups, downs = wu.shape[1] // width, wd.shape[0]
    tile = 256
    chips_of_tile = tile // (2 * depth)
    owners_chips = ring // downs

    def column(ref, first, size):
        return ref.at[:, :, :, pl.ds(first, size)]

    parts = [(gains, gains_all, 0)]
    parts += [(wq.at[:, pl.ds(j * width, width)], column(wq_all, j * width, width), j) for j in range(3)]
    parts += [(wo, wo_all, 0)]
    parts += [(wd.at[j], wd_all.at[:, :, j], 0) for j in range(downs)]
    parts += [(wu.at[:, pl.ds(j * width, width)], column(wu_all, j * width, width), j) for j in range(ups)]
    count = len(parts)

    def window(k, s=0, d=0):
        if k == 0:
            return pl.ds(0, gains.shape[0]), pl.ds(0, gains.shape[1])
        rows = pl.ds(pl.multiple_of(at.n * quarter, quarter), carried)
        if s == steps:
            return rows, pl.ds(d * (width // 2), width // 2)
        return rows, pl.ds(0, width)

    def idle(k, s, d):
        return k == 0 and s == steps and d == 1

    def toward(d):
        return at.at_ring(at.r + 1 if d == 0 else at.r - 1)

    def ring_out(k, s, d):
        pos = at.r - (s - 1) if d == 0 else at.r + (s - 1)
        rows, cols = window(k, s, d)
        dst = parts[k][1].at[at.chip(pos), at.c, rows, cols]
        src = parts[k][0].at[rows, cols] if s == 1 else dst
        return remote(src, dst, ring_send.at[k, s - 1, d], ring_recv.at[k, s - 1, d], toward(d))

    def ring_in(k, s, d):
        pos = at.r - s if d == 0 else at.r + s
        rows, cols = window(k, s, d)
        ref = parts[k][1].at[at.chip(pos), at.c, rows, cols]
        return remote(ref, ref, ring_send.at[k, s - 1, d], ring_recv.at[k, s - 1, d], toward(d))

    def own_copy(k):
        rows, cols = window(k)
        return pltpu.make_async_copy(
            parts[k][0].at[rows, cols], parts[k][1].at[at.q, at.c, rows, cols], own_sem.at[k]
        )

    def cross(k, incoming=False):
        side = 1 - at.n if incoming else at.n
        rows = pl.ds(pl.multiple_of(side * carried, quarter), quarter)
        ref = parts[k][1].at[:, at.c, rows]
        return remote(ref, ref, x_send.at[k], x_recv.at[k], at.across())

    def sib(k, incoming=False):
        ref = parts[k][1].at[:, 1 - at.c if incoming else at.c]
        return remote(ref, ref, sib_send.at[k], sib_recv.at[k], at.sibling())

    def row_copy(j):
        return remote(given.at[j], got.at[j], row_send.at[j], row_recv.at[j], at.across())

    def over(size, step):
        def run(piece):
            @pl.loop(0, size // step)
            def _(t):
                piece(pl.multiple_of(t * step, step))

        return run

    def turned(src, dst, first=0):
        @over(src.shape[1], tile)
        def _(low):
            dst[pl.ds(first + low, tile), :] = src[:, pl.ds(low, tile)].T

    def normalise():
        lane = lax.broadcasted_iota(jnp.int32, (8, 2 * HEAD_DIM), 1)
        for chip in range(ring):
            pair = jnp.where(
                lane < depth, gains_all[chip, 0].astype(F32)[:8], gains_all[chip, 1].astype(F32)[:8]
            )
            scales[:, chip * 2 * depth : (chip + 1) * 2 * depth] = pair

        @over(entries, 32)
        def _(low):
            rows = pl.ds(low, 32)
            low_rows = kept[0, rows] + got[0, rows]
            value = low_rows.astype(F32)
            rows_low[rows, :] = low_rows
            inverse = lax.rsqrt(jnp.mean(value * value, axis=-1, keepdims=True) + epsilon)
            normed[rows, :] = (value * inverse * scales[0:1, :]).astype(BF16)
            router_val[rows, :] = jnp.sum(value * router[...], axis=-1, keepdims=True)

    def project_part(j):
        @over(width, tile)
        def _(low):
            cols = pl.ds(j * width + low, tile)
            weight = wq_all[:, :, :, cols].reshape(width, tile)
            project[:, cols] = dot(normed[...], weight).astype(BF16)

    def attention(first, last):
        @pl.loop(first, last)
        def _(p):
            lanes = 2 * HEAD_DIM
            q = project[:, pl.ds(pl.multiple_of(p * lanes, lanes), lanes)]
            k = project[:, pl.ds(pl.multiple_of(width + p * lanes, lanes), lanes)]
            v = project[:, pl.ds(pl.multiple_of(2 * width + p * lanes, lanes), lanes)]
            total = jnp.zeros((entries, lanes), F32)
            for head in (0, 1):
                probs = probabilities(live[...], only(q, head), k)
                total = total + only(dot(probs.astype(BF16), v), head)
            heads[:, pl.ds(pl.multiple_of(p * lanes, lanes), lanes)] = total.astype(BF16)

    def attend_project():
        @over(width, tile)
        def _(low):
            cols = pl.ds(low, tile)
            weight = wo_all[:, :, :, cols].reshape(width, tile)
            attend_out[:, cols] = dot(heads[...], weight)

        @over(entries, 32)
        def _(low):
            rows = pl.ds(low, 32)
            middle = rows_low[rows, :].astype(F32) + attend_out[rows, :]
            inverse = lax.rsqrt(jnp.mean(middle * middle, axis=-1, keepdims=True) + epsilon)
            value = middle * inverse
            second_n[rows, :] = value
            inverse_two[rows, :] = inverse
            second[rows, :] = (value * scales[1:2, :]).astype(BF16)

    def branch_grad():
        @over(entries, 32)
        def _(low):
            rows = pl.ds(low, 32)
            dout = (kept[1, rows] + got[1, rows]).astype(F32)
            d_mlp[rows, :] = (router_val[rows, :] * dout).astype(BF16)

    def act_grad():
        @pl.loop(0, ring)
        def _(chip):
            for core in (0, 1):
                size = downs * depth
                cols = pl.ds(pl.multiple_of(chip * (2 * size) + core * size, size), size)
                d_act[:, cols] = dot_nt(d_mlp[...], wd_all[chip, core].reshape(size, width))

    def up_part(j):
        @over(width, tile)
        def _(low):
            cols = pl.ds(j * width + low, tile)
            pre = dot(second[...], wu_all[:, :, :, cols].reshape(width, tile))
            value, slope = gelu_pair(pre)
            value = value.astype(BF16)
            act[:, pl.ds(low, tile)] = value
            d_pre[:, cols] = (d_act[:, cols] * slope).astype(BF16)
            act_t[cols, :] = value.T

        @over(width, tile)
        def _(low):
            cols = pl.ds(low, tile)
            down = wd_all[j * owners_chips : (j + 1) * owners_chips, :, :, :, cols]
            part = dot(act[...], down.reshape(width, tile))
            chip = low // (2 * depth)
            up = wu_all[pl.ds(chip, chips_of_tile), :, :, pl.ds(j * width, width)]
            back = dot_nt(d_pre[:, pl.ds(j * width, width)], up.reshape(tile, width))
            if j == 0:
                mlp_out[:, cols] = part
                d_second[:, cols] = back
            else:
                mlp_out[:, cols] += part
                d_second[:, cols] += back

    def close():
        small[...] = jnp.zeros_like(small)

        @over(entries, 32)
        def _(low):
            rows = pl.ds(low, 32)
            value = rows_low[rows, :].astype(F32)
            dout = (kept[1, rows] + got[1, rows]).astype(F32)
            gate = router_val[rows, :]
            branch = attend_out[rows, :] + mlp_out[rows, :]
            out_low[rows, :] = (value + gate * branch).astype(BF16)
            d_gate = jnp.sum(dout * branch, axis=-1, keepdims=True)
            normed_value = second_n[rows, :]
            back = d_second[rows, :]
            small[1:2, :] += jnp.sum(back * normed_value, axis=0, keepdims=True)
            small[2:3, :] += jnp.sum(d_gate * value, axis=0, keepdims=True)
            back = back * scales[1:2, :]
            back = inverse_two[rows, :] * (
                back - normed_value * jnp.mean(back * normed_value, axis=-1, keepdims=True)
            )
            d_attend[rows, :] = (gate * dout + back).astype(BF16)
            base[rows, :] = dout + back + d_gate * router[...]

    pairs = width // (2 * HEAD_DIM)
    cuts = [pairs * j // 8 for j in (0, 2, 5, 8)]
    work = [
        [normalise, lambda: turned(normed, normed_t)],
        [lambda: project_part(0)],
        [lambda: project_part(1)],
        [lambda: project_part(2), lambda: attention(cuts[0], cuts[1])],
        [lambda: attention(cuts[1], cuts[2])],
        [lambda: attention(cuts[2], cuts[3])],
        [attend_project],
        [branch_grad, lambda: turned(heads, heads_t), lambda: turned(second, second_t)],
    ]
    work += [[]] * (1 + 3 + 1 + downs - 1 - len(work)) + [[act_grad]]
    work += [[functools.partial(up_part, j)] for j in range(ups)]

    greet([at.at_ring(at.r + 1), at.at_ring(at.r - 1), at.sibling(), at.across()])
    row_copy(0).start()
    for i in range(count + steps + 2):
        if i < count:
            for d in (0, 1):
                ring_out(i, 1, d).start()
            own_copy(i).start()
        if i == 2:
            row_copy(1).start()
        for s in range(1, steps + 1):
            k = i - s
            if 0 <= k < count:
                for d in (0, 1):
                    if not idle(k, s, d):
                        ring_in(k, s, d).wait_recv()
                    if s < steps and not idle(k, s + 1, d):
                        ring_out(k, s + 1, d).start()
                if s == steps:
                    own_copy(k).wait()
                    if k > 0:
                        cross(k).start()
        k = i - steps - 1
        if 0 <= k < count:
            if k > 0:
                cross(k, True).wait_recv()
            sib(k).start()
        k = i - steps - 2
        if 0 <= k < count:
            sib(k, True).wait_recv()
            if k == 0:
                for j in (0, 1):
                    row_copy(j).wait_recv()
            for piece in work[k]:
                piece()
    close()
    for k in range(count):
        sib(k).wait_send()
        if k > 0:
            cross(k).wait_send()
        for s in range(1, steps + 1):
            for d in (0, 1):
                if not idle(k, s, d):
                    ring_out(k, s, d).wait_send()
    for j in (0, 1):
        row_copy(j).wait_send()


def forward(wide, gains, wq, wo, wu, wd, kept, given, router, live):
    depth, width = wo.shape
    ring, steps = wide // 2, wide // 4
    entries = kept.shape[1]
    ff = wu.shape[1]
    downs = wd.shape[0] // depth
    count = 1 + 3 + 1 + downs + ff // width
    vmem = pl.BlockSpec(memory_space=pltpu.VMEM)
    anywhere = pl.BlockSpec(memory_space=pl.ANY)
    dma = pltpu.SemaphoreType.DMA
    shape = jax.ShapeDtypeStruct
    return pl.pallas_call(
        functools.partial(forward_kernel, wide),
        out_shape=[
            shape((ring, 2, depth, 3 * width), BF16),
            shape((ring, 2, depth, width), BF16),
            shape((width, entries), BF16),
            shape((width, entries), BF16),
            shape((width, entries), BF16),
            shape((ff, entries), BF16),
            shape((entries, ff), BF16),
            shape((entries, width), BF16),
            shape((entries, width), BF16),
            shape((entries, 3 * width), BF16),
            shape((entries, width), F32),
            shape((entries, width), BF16),
            shape((entries, width), BF16),
            shape((8, width), F32),
            shape((8, width), F32),
        ],
        in_specs=[anywhere] * 5 + [vmem, anywhere, vmem, vmem],
        out_specs=[vmem] * 15,
        scratch_shapes=[
            pltpu.VMEM((ring, 2, depth, ff), BF16),
            pltpu.VMEM((ring, 2, downs, depth, width), BF16),
            pltpu.VMEM((ring, 2) + gains.shape, BF16),
            pltpu.VMEM((2, entries, width), BF16),
            pltpu.VMEM((entries, width), BF16),
            pltpu.VMEM((entries, width), BF16),
            pltpu.VMEM((entries, width), F32),
            pltpu.VMEM((entries, width), F32),
            pltpu.VMEM((entries, width), BF16),
            pltpu.VMEM((entries, ff), F32),
            pltpu.VMEM((entries, width), BF16),
            pltpu.VMEM((entries, width), F32),
            pltpu.VMEM((entries, width), F32),
            pltpu.VMEM((entries, 1), F32),
            pltpu.VMEM((entries, 1), F32),
            dma((count,)),
            dma((count, steps, 2)),
            dma((count, steps, 2)),
            dma((count,)),
            dma((count,)),
            dma((count,)),
            dma((count,)),
            dma((2,)),
            dma((2,)),
        ],
        compiler_params=pltpu.CompilerParams(
            collective_id=1, has_side_effects=True, vmem_limit_bytes=60 * 1024 * 1024
        ),
        name="gather",
    )(gains, wq, wo, wu, wd.reshape(downs, depth, width), kept, given, router, live)


def reduce_kernel(
    wide,
    act_t,
    second_t,
    heads_t,
    normed_t,
    d_mlp,
    d_pre,
    d_attend,
    d_project,
    small,
    rows,
    o_qkv,
    o_out,
    o_up,
    o_down,
    o_small,
    rows_got,
    own,
    to_sib,
    mine,
    moving,
    x_out,
    x_in,
    small_acc,
    small_in,
    sib_send,
    sib_recv,
    ring_send,
    ring_recv,
    x_send,
    x_recv,
    small_send,
    small_recv,
    row_send,
    row_recv,
):
    at = Place(wide)
    ring, steps = at.ring, at.ring // 2
    depth, width = o_out.shape
    half = depth // 2
    ups, downs = o_up.shape[1] // width, o_down.shape[0] // depth
    rows_in = d_mlp.shape[0]
    count = downs + ups + 1 + 3
    tile = 256

    def operands(k):
        if k < downs:
            return lambda core: act_t[:, core, k], d_mlp, 0
        k -= downs
        if k < ups:
            return lambda core: second_t[:, core], d_pre, k * width
        k -= ups
        if k < 1:
            return lambda core: heads_t[:, core], d_attend, 0
        return lambda core: normed_t[:, core], d_project, (k - 1) * width

    def product(k, core, put):
        left, right, first = operands(k)
        tall = left(core).reshape(ring * depth, rows_in)

        @pl.loop(0, width // tile)
        def _(t):
            cols = pl.ds(pl.multiple_of(t * tile, tile), tile)
            from_cols = pl.ds(pl.multiple_of(first + t * tile, tile), tile)
            put(cols, dot(tall, right[:, from_cols]).reshape(ring, depth, tile))

    def store(k):
        if k < downs:
            return o_down, k * depth, 0
        k -= downs
        if k < ups:
            return o_up, 0, k * width
        k -= ups
        if k < 1:
            return o_out, 0, 0
        return o_qkv, 0, (k - 1) * width

    def sib(k):
        return remote(
            to_sib.at[k % 2], mine.at[k], sib_send.at[k], sib_recv.at[k], at.sibling()
        )

    def halves(d):
        return pl.ds(d * half, half)

    def ring_out(k, t, d):
        to = at.at_ring(at.r + 1 if d == 0 else at.r - 1)
        if t == 0:
            src = mine.at[k, at.chip(at.r + steps), halves(d)]
            dst = moving.at[k, 0, d, halves(d)]
        else:
            src = moving.at[k, t - 1, d]
            dst = moving.at[k, t, d]
        return remote(src, dst, ring_send.at[k, t, d], ring_recv.at[k, t, d], to)

    def ring_in(k, t, d):
        to = at.at_ring(at.r + 1 if d == 0 else at.r - 1)
        ref = moving.at[k, 0, d, halves(d)] if t == 0 else moving.at[k, t, d]
        return remote(ref, ref, ring_send.at[k, t, d], ring_recv.at[k, t, d], to)

    def cross(k):
        return remote(x_out.at[k], x_in.at[k], x_send.at[k], x_recv.at[k], at.across())

    bits = [1 << b for b in range(ring.bit_length() - 1)]
    partners = [at.sibling(), at.across()] + [at.flipped(bit) for bit in bits]
    stages = len(partners)

    def small_copy(j):
        return remote(
            small_acc.at[j], small_in.at[j], small_send.at[j], small_recv.at[j], partners[j]
        )

    greet(partners + [at.at_ring(at.r + 1), at.at_ring(at.r - 1)])
    rows_copy = remote(rows, rows_got, row_send, row_recv, at.across())
    rows_copy.start()
    small_acc[0] = small[...]
    step = 16

    for i in range(count + steps + 3):
        k = i
        if k < count:
            if k >= 2:
                sib(k - 2).wait_send()

            def keep_other(cols, value):
                to_sib[k % 2, :, :, cols] = value.astype(BF16)

            def keep_own(cols, value):
                own[k % 2, :, :, cols] = value

            product(k, 1 - at.c, keep_other)
            sib(k).start()
            product(k, at.c, keep_own)
        if i <= stages:
            if i > 0:
                small_copy(i - 1).wait_recv()
                small_acc[i] = small_acc[i - 1] + small_in[i - 1]
            if i < stages:
                small_copy(i).start()
            else:
                o_small[...] = small_acc[stages]
        k = i - 1
        if 0 <= k < count:
            sib(k).wait_recv()

            @pl.loop(0, ring)
            def _(chip):
                mine[k, chip] = (mine[k, chip].astype(F32) + own[k % 2, chip]).astype(BF16)

            for d in (0, 1):
                ring_out(k, 0, d).start()
        for t in range(1, steps):
            k = i - 1 - t
            if 0 <= k < count:
                for d in (0, 1):
                    ring_in(k, t - 1, d).wait_recv()
                    dest = at.chip(at.r + (steps - t) if d == 0 else at.r - (steps - t))
                    lows = range(0, depth, half) if t == 1 else (0,)
                    for low in lows:
                        size = half if t == 1 else depth

                        @pl.loop(0, size // step)
                        def _(g):
                            take = pl.ds(pl.multiple_of(low + g * step, step), step)
                            value = mine[k, dest, take]
                            if not (t == 1 and low != d * half):
                                value = (
                                    value.astype(F32) + moving[k, t - 1, d, take].astype(F32)
                                ).astype(BF16)
                            moving[k, t - 1, d, take] = value

                    ring_out(k, t, d).start()
        k = i - 1 - steps
        if 0 <= k < count:
            for d in (0, 1):
                ring_in(k, steps - 1, d).wait_recv()

            @pl.loop(0, depth // step)
            def _(g):
                take = pl.ds(pl.multiple_of(g * step, step), step)
                value = mine[k, at.q, take].astype(F32)
                value = value + moving[k, steps - 1, 0, take].astype(F32)
                value = value + moving[k, steps - 1, 1, take].astype(F32)
                x_out[k, take] = value.astype(BF16)

            cross(k).start()
        k = i - 2 - steps
        if 0 <= k < count:
            cross(k).wait_recv()
            out, low, first = store(k)

            @pl.loop(0, depth // step)
            def _(g):
                take = pl.ds(pl.multiple_of(g * step, step), step)
                put = pl.ds(pl.multiple_of(low + g * step, step), step)
                out[put, first : first + width] = x_out[k, take].astype(F32) + x_in[
                    k, take
                ].astype(F32)

    for k in range(count):
        if k >= count - 2:
            sib(k).wait_send()
        cross(k).wait_send()
        for t in range(steps):
            for d in (0, 1):
                ring_out(k, t, d).wait_send()
    for j in range(stages):
        small_copy(j).wait_send()
    rows_copy.wait()


def reduce_grads(
    wide, act_t, second_t, heads_t, normed_t, d_mlp, d_pre, d_attend, d_project, small, rows
):
    width = d_mlp.shape[1]
    ring, steps = wide // 2, wide // 4
    depth = width // wide
    tokens_in = d_mlp.shape[0]

    def tall(value):
        return value.reshape(ring, 2, depth, tokens_in)

    ff = d_pre.shape[1]
    downs = ff // width
    act_t = act_t.reshape(ring, 2, downs, depth, tokens_in)
    count = 2 * downs + 4
    stages = 2 + (ring.bit_length() - 1)
    vmem = pl.BlockSpec(memory_space=pltpu.VMEM)
    anywhere = pl.BlockSpec(memory_space=pl.ANY)
    dma = pltpu.SemaphoreType.DMA
    return pl.pallas_call(
        functools.partial(reduce_kernel, wide),
        out_shape=[
            jax.ShapeDtypeStruct((depth, 3 * width), F32),
            jax.ShapeDtypeStruct((depth, width), F32),
            jax.ShapeDtypeStruct((depth, ff), F32),
            jax.ShapeDtypeStruct((ff // wide, width), F32),
            jax.ShapeDtypeStruct(small.shape, F32),
            jax.ShapeDtypeStruct(rows.shape, rows.dtype),
        ],
        in_specs=[vmem] * 9 + [anywhere],
        out_specs=[vmem] * 5 + [anywhere],
        scratch_shapes=[
            pltpu.VMEM((2, ring, depth, width), F32),
            pltpu.VMEM((2, ring, depth, width), BF16),
            pltpu.VMEM((count, ring, depth, width), BF16),
            pltpu.VMEM((count, steps, 2, depth, width), BF16),
            pltpu.VMEM((count, depth, width), BF16),
            pltpu.VMEM((count, depth, width), BF16),
            pltpu.VMEM((stages + 1,) + small.shape, F32),
            pltpu.VMEM((stages,) + small.shape, F32),
            dma((count,)),
            dma((count,)),
            dma((count, steps, 2)),
            dma((count, steps, 2)),
            dma((count,)),
            dma((count,)),
            dma((stages,)),
            dma((stages,)),
            dma,
            dma,
        ],
        compiler_params=pltpu.CompilerParams(
            collective_id=2, has_side_effects=True, vmem_limit_bytes=60 * 1024 * 1024
        ),
        name="reduce",
    )(
        act_t,
        tall(second_t),
        tall(heads_t),
        tall(normed_t),
        d_mlp,
        d_pre,
        d_attend,
        d_project,
        small,
        rows,
    )


def attend_back_kernel(live, q, k, v, d_heads, d_project):
    d_q = jnp.zeros(q.shape, F32)
    d_k = jnp.zeros(q.shape, F32)
    d_v = jnp.zeros(q.shape, F32)
    for head in (0, 1):
        probs = probabilities(live[...], only(q[...], head), k[...])
        d_own = only(d_heads[...], head)
        d_probs = dot_nt(d_own, v[...])
        d_scores = probs * (d_probs - jnp.sum(probs * d_probs, axis=-1, keepdims=True))
        d_scores = d_scores.astype(BF16)
        d_q = d_q + only(dot(d_scores, k[...]), head)
        d_k = d_k + only(dot_tn(d_scores, q[...]), head)
        d_v = d_v + dot_tn(probs.astype(BF16), d_own)
    d_project[0] = (d_q * 0.125).astype(BF16)
    d_project[1] = (d_k * 0.125).astype(BF16)
    d_project[2] = d_v.astype(BF16)


def attend_back(live, project, d_heads):
    entries = project.shape[0]
    width = project.shape[1] // 3
    pairs = width // (2 * HEAD_DIM)

    def third(j):
        return pl.BlockSpec((entries, 2 * HEAD_DIM), lambda p: (0, j * pairs + p))

    return pl.pallas_call(
        attend_back_kernel,
        grid=(pairs,),
        out_shape=jax.ShapeDtypeStruct((3, entries, width), BF16),
        in_specs=[pl.BlockSpec((1, entries), lambda p: (0, 0)), third(0), third(1), third(2), third(0)],
        out_specs=pl.BlockSpec((3, entries, 2 * HEAD_DIM), lambda p: (0, 0, p)),
        name="attend_back",
    )(live, project, project, project, d_heads)


def paired_body(
    wide, tokens, cotangent, lengths, routes, w_qkv, w_out, w_up, w_down, gain_attn, gain_mlp, router
):
    place = lax.axis_index("narrow")
    seqs, span, width = tokens.shape
    list_len = routes.shape[1]
    depth = gain_attn.shape[0]
    counts = lengths // 8
    entry = jnp.arange(list_len, dtype=jnp.int32)
    live = entry[None, :] < counts[:, None]
    local_slot = jnp.where(live, routes - place * span, -1)
    spots = jnp.arange(span, dtype=jnp.int32)
    chosen = (local_slot[:, :, None] == spots[None, None, :]).astype(BF16)

    def take(source):
        return jnp.einsum("sep,spd->sed", chosen, source, preferred_element_type=F32).astype(BF16)

    picked = jnp.stack([take(tokens), take(cotangent)])
    kept = lax.dynamic_index_in_dim(picked, place, 1, keepdims=False)
    given = lax.dynamic_index_in_dim(picked, 1 - place, 1, keepdims=False)
    gains = jnp.stack(
        [jnp.concatenate([gain_attn, gain_attn]), jnp.concatenate([gain_mlp, gain_mlp])]
    )
    gains = jnp.pad(gains, ((0, 14), (0, 0)))
    router_row = router.astype(F32)[None, :]
    live_row = lax.dynamic_index_in_dim(live, place, 0, keepdims=True).astype(jnp.int32)
    (
        weight_qkv,
        weight_out,
        normed_t,
        heads_t,
        second_t,
        act_t,
        d_pre,
        d_mlp,
        d_attend,
        project,
        base,
        out_low,
        rows_low,
        small,
        scales,
    ) = forward(wide, gains, w_qkv, w_out, w_up, w_down, kept, given, router_row, live_row)

    d_heads = dot_nt(d_attend, weight_out.reshape(width, width)).astype(BF16)
    d_parts = attend_back(live_row, project, d_heads)
    d_project = jnp.concatenate([d_parts[0], d_parts[1], d_parts[2]], axis=1)
    d_normed = dot_nt(d_project, weight_qkv.reshape(width, 3 * width))
    normed_one, inverse_one = rms_parts(rows_low.astype(F32))
    grad_gain_one = jnp.sum(d_normed * normed_one, axis=0)
    d_norm_rows = rms_back(d_normed * scales[0:1], normed_one, inverse_one)
    grad_low = (base + d_norm_rows).astype(BF16)

    small = jnp.concatenate([grad_gain_one[None, :], small[1:]])
    back = jnp.stack([out_low, grad_low])
    grad_qkv, grad_out, grad_up, grad_down, small, back_got = reduce_grads(
        wide, act_t, second_t, heads_t, normed_t, d_mlp, d_pre, d_attend, d_project, small, back
    )
    first = place == 0
    rows_out = jnp.stack([jnp.where(first, back, back_got), jnp.where(first, back_got, back)], axis=1)
    hit = jnp.any(local_slot[:, :, None] == spots[None, None, :], axis=1)

    def put(base, fresh):
        spread = jnp.einsum("sep,sed->spd", chosen, fresh, preferred_element_type=F32)
        return jnp.where(hit[:, :, None], spread.astype(BF16), base)

    start = lax.axis_index("wide") * depth
    return (
        put(tokens, rows_out[0]),
        put(cotangent, rows_out[1]),
        grad_qkv,
        grad_out,
        grad_up,
        grad_down,
        lax.dynamic_slice_in_dim(small[0], start, depth),
        lax.dynamic_slice_in_dim(small[1], start, depth),
        small[2],
    )


def body(wide, narrow, tokens, *others):
    if narrow == 2 and tokens.shape[0] == 2 and wide >= 8 and wide & (wide - 1) == 0:
        return paired_body(wide, tokens, *others)
    return general_body(tokens, *others)


def solution(mesh):
    in_specs = (
        P("wide", "narrow", None),
        P("wide", "narrow", None),
        P("wide"),
        P("wide", None),
        P("wide", None),
        P("wide", None),
        P("wide", None),
        P("wide", None),
        P("wide"),
        P("wide"),
        P(),
    )
    out_specs = (
        P("wide", "narrow", None),
        P("wide", "narrow", None),
        P("wide", None),
        P("wide", None),
        P("wide", None),
        P("wide", None),
        P("wide"),
        P("wide"),
        P(),
    )
    sizes = mesh.shape["wide"], mesh.shape["narrow"]
    return jax.shard_map(functools.partial(body, *sizes), mesh=mesh, in_specs=in_specs, out_specs=out_specs, check_vma=False)
```

```python
import functools

import jax
import jax.numpy as jnp
from jax import lax
from jax.experimental import pallas as pl
from jax.experimental.pallas import tpu as pltpu
from jax.sharding import PartitionSpec as P

HEAD_DIM = 64
MESH = pl.DeviceIdType.MESH
F32 = jnp.float32
BF16 = jnp.bfloat16
LAG = 2
PIECES = (512, 512)
FIRST_PIECES = (256, 256, 512)
LAST_PIECES = (512, 256, 256)
GIVE = 128
GIVE_SKIP = (3, 6)
ROW_PIECES = 8

epsilon = 1e-06
masked_score = -1e30


def rms_parts(values):
    inverse = lax.rsqrt(jnp.mean(values * values, axis=-1, keepdims=True) + epsilon)
    return (values * inverse, inverse)


def rms_back(grad_normed, normed, inverse):
    return inverse * (grad_normed - normed * jnp.mean(grad_normed * normed, axis=-1, keepdims=True))


def attend_scores(queries, keys_all, allowed):
    scores = (
        jnp.einsum("sqhe,skhe->shqk", queries, keys_all, preferred_element_type=jnp.float32) * 0.125
    )
    return jnp.where(allowed, scores, masked_score)


def attend_forward(queries, keys_all, values_all, allowed):
    scores = attend_scores(queries, keys_all, allowed)
    top_score = jnp.max(scores, axis=-1, keepdims=True)
    expo = jnp.exp(scores - top_score)
    total = jnp.sum(expo, axis=-1, keepdims=True)
    log_total = top_score + jnp.log(total)
    probs_low = (expo / total).astype(jnp.bfloat16)
    heads_out = jnp.einsum(
        "shqk,skhe->sqhe", probs_low, values_all, preferred_element_type=jnp.float32
    )
    return (heads_out, log_total)


def attend_backward(queries, keys_all, values_all, allowed, log_total, d_heads):
    probs_again = jnp.exp(attend_scores(queries, keys_all, allowed) - log_total)
    d_probs = jnp.einsum("sqhe,skhe->shqk", d_heads, values_all, preferred_element_type=jnp.float32)
    row_dot = jnp.sum(probs_again * d_probs, axis=-1, keepdims=True)
    d_scores = (probs_again * (d_probs - row_dot)).astype(jnp.bfloat16)
    d_queries = (
        jnp.einsum("shqk,skhe->sqhe", d_scores, keys_all, preferred_element_type=jnp.float32)
        * 0.125
    )
    d_key_part = (
        jnp.einsum("shqk,sqhe->skhe", d_scores, queries, preferred_element_type=jnp.float32) * 0.125
    )
    d_value_part = jnp.einsum(
        "shqk,sqhe->skhe",
        probs_again.astype(jnp.bfloat16),
        d_heads,
        preferred_element_type=jnp.float32,
    )
    return (d_queries, d_key_part, d_value_part)


def general_body(
    tokens, cotangent, lengths, routes, w_qkv, w_out, w_up, w_down, gain_attn, gain_mlp, router
):
    parts_narrow = lax.axis_size("narrow")
    place = lax.axis_index("narrow")
    seqs, span, width = tokens.shape
    list_len = routes.shape[1]
    own_entries = list_len // parts_narrow
    rows_total = seqs * own_entries
    counts = lengths // 8
    entry = jnp.arange(list_len, dtype=jnp.int32)
    live = entry[None, :] < counts[:, None]
    local_slot = routes - place * span
    mine = live & (local_slot >= 0) & (local_slot < span)
    pick = jnp.clip(local_slot, 0, span - 1)
    keep = mine[:, :, None]
    taken_in = jnp.take_along_axis(tokens, pick[:, :, None], axis=1)
    taken_cot = jnp.take_along_axis(cotangent, pick[:, :, None], axis=1)
    blank = jnp.zeros_like(taken_in)
    rows_in, rows_cot = (
        lax.psum_scatter(
            jnp.where(keep, taken_in, blank), "narrow", scatter_dimension=1, tiled=True
        ).astype(jnp.float32),
        lax.psum_scatter(
            jnp.where(keep, taken_cot, blank), "narrow", scatter_dimension=1, tiled=True
        ).astype(jnp.float32),
    )
    inputs_rows = rows_in.reshape(rows_total, width)
    inputs_low = inputs_rows.astype(jnp.bfloat16)
    dout = rows_cot.reshape(rows_total, width)
    gathered = (
        lax.all_gather(w_qkv, "wide", axis=0, tiled=True),
        lax.all_gather(w_out, "wide", axis=0, tiled=True),
        lax.all_gather(w_up, "wide", axis=0, tiled=True),
        lax.all_gather(w_down, "wide", axis=0, tiled=True),
        lax.all_gather(gain_attn, "wide", axis=0, tiled=True),
        lax.all_gather(gain_mlp, "wide", axis=0, tiled=True),
    )
    weight_qkv, weight_out, weight_up, weight_down, gain_first, gain_second = gathered
    scale_first = gain_first.astype(jnp.float32)
    scale_second = gain_second.astype(jnp.float32)
    normed_one, inverse_one = rms_parts(inputs_rows)
    normed_low = (normed_one * scale_first).astype(jnp.bfloat16)
    project = jnp.dot(normed_low, weight_qkv, preferred_element_type=jnp.float32).astype(
        jnp.bfloat16
    )
    queries = project[:, :width].reshape(seqs, own_entries, -1, HEAD_DIM)
    key_own = project[:, width : 2 * width].reshape(seqs, own_entries, width)
    value_own = project[:, 2 * width :].reshape(seqs, own_entries, width)
    keys_all, values_all = (
        lax.all_gather(key_own, "narrow", axis=1, tiled=True),
        lax.all_gather(value_own, "narrow", axis=1, tiled=True),
    )
    keys_all = keys_all.reshape(seqs, list_len, -1, HEAD_DIM)
    values_all = values_all.reshape(seqs, list_len, -1, HEAD_DIM)
    query_pos = place * own_entries + jnp.arange(own_entries, dtype=jnp.int32)
    allowed = (entry[None, None, None, :] <= query_pos[None, None, :, None]) & (
        entry[None, None, None, :] < counts[:, None, None, None]
    )
    heads_out, log_total = attend_forward(queries, keys_all, values_all, allowed)
    heads_low = heads_out.reshape(rows_total, width).astype(jnp.bfloat16)
    attend_out = jnp.dot(heads_low, weight_out, preferred_element_type=jnp.float32)
    middle = inputs_rows + attend_out
    normed_two, inverse_two = rms_parts(middle)
    second_low = (normed_two * scale_second).astype(jnp.bfloat16)
    pre_act = jnp.dot(second_low, weight_up, preferred_element_type=jnp.float32)
    activ_full, gelu_back = jax.vjp(jax.nn.gelu, pre_act)
    activ_low = activ_full.astype(jnp.bfloat16)
    mlp_out = jnp.dot(activ_low, weight_down, preferred_element_type=jnp.float32)
    branch = attend_out + mlp_out
    router_val = jnp.dot(inputs_low, router, preferred_element_type=jnp.float32)
    out_low = (inputs_rows + router_val[:, None] * branch).astype(jnp.bfloat16)
    back_set = (
        lax.all_gather(w_qkv, "wide", axis=0, tiled=True),
        lax.all_gather(w_out, "wide", axis=0, tiled=True),
        lax.all_gather(w_up, "wide", axis=0, tiled=True),
        lax.all_gather(w_down, "wide", axis=0, tiled=True),
        lax.all_gather(gain_attn, "wide", axis=0, tiled=True),
        lax.all_gather(gain_mlp, "wide", axis=0, tiled=True),
    )
    back_qkv, back_out, back_up, back_down, back_gain_a, back_gain_m = back_set
    back_first = back_gain_a.astype(jnp.float32)
    back_second = back_gain_m.astype(jnp.float32)
    d_branch = router_val[:, None] * dout
    d_router_val = jnp.sum(dout * branch, axis=-1)
    d_mlp = d_branch.astype(jnp.bfloat16)
    grad_down_full = jnp.einsum("rf,rd->fd", activ_low, d_mlp, preferred_element_type=jnp.float32)
    d_act = jnp.einsum("rd,fd->rf", d_mlp, back_down, preferred_element_type=jnp.float32)
    d_pre = gelu_back(d_act)[0].astype(jnp.bfloat16)
    grad_up_full = jnp.einsum("rd,rf->df", second_low, d_pre, preferred_element_type=jnp.float32)
    d_normed_two = jnp.einsum("rf,df->rd", d_pre, back_up, preferred_element_type=jnp.float32)
    grad_gain_two = jnp.sum(d_normed_two * normed_two, axis=0)
    d_middle = rms_back(d_normed_two * back_second, normed_two, inverse_two)
    d_attend = (d_branch + d_middle).astype(jnp.bfloat16)
    grad_out_full = jnp.einsum("rd,re->de", heads_low, d_attend, preferred_element_type=jnp.float32)
    d_heads = jnp.einsum(
        "re,de->rd", d_attend, back_out, preferred_element_type=jnp.float32
    ).astype(jnp.bfloat16)
    d_heads_own = d_heads.reshape(seqs, own_entries, -1, HEAD_DIM)
    d_queries, d_key_part, d_value_part = attend_backward(
        queries, keys_all, values_all, allowed, log_total, d_heads_own
    )
    d_key_own, d_value_own = (
        lax.psum_scatter(
            d_key_part.reshape(seqs, list_len, width), "narrow", scatter_dimension=1, tiled=True
        ),
        lax.psum_scatter(
            d_value_part.reshape(seqs, list_len, width), "narrow", scatter_dimension=1, tiled=True
        ),
    )
    d_project = jnp.concatenate(
        [
            d_queries.reshape(rows_total, width),
            d_key_own.reshape(rows_total, width),
            d_value_own.reshape(rows_total, width),
        ],
        axis=-1,
    ).astype(jnp.bfloat16)
    grad_qkv_full = jnp.einsum(
        "rd,re->de", normed_low, d_project, preferred_element_type=jnp.float32
    )
    d_normed = jnp.einsum("re,de->rd", d_project, back_qkv, preferred_element_type=jnp.float32)
    grad_gain_one = jnp.sum(d_normed * normed_one, axis=0)
    d_norm_rows = rms_back(d_normed * back_first, normed_one, inverse_one)
    d_rows = dout + d_middle + d_norm_rows + d_router_val[:, None] * router.astype(jnp.float32)
    grad_router_part = jnp.dot(d_router_val, inputs_rows, precision=lax.Precision.HIGHEST)
    grad_low = d_rows.astype(jnp.bfloat16)
    out_all, grad_all = (
        lax.all_gather(out_low.reshape(seqs, own_entries, width), "narrow", axis=1, tiled=True),
        lax.all_gather(grad_low.reshape(seqs, own_entries, width), "narrow", axis=1, tiled=True),
    )
    target = jnp.where(mine, pick, span)
    put = jax.vmap(lambda base, where_to, fresh: base.at[where_to].set(fresh, mode="drop"))
    mixed = put(tokens, target, out_all)
    grad_tokens = put(cotangent, target, grad_all)
    shards = (
        lax.psum_scatter(grad_qkv_full, "wide", scatter_dimension=0, tiled=True),
        lax.psum_scatter(grad_out_full, "wide", scatter_dimension=0, tiled=True),
        lax.psum_scatter(grad_up_full, "wide", scatter_dimension=0, tiled=True),
        lax.psum_scatter(grad_down_full, "wide", scatter_dimension=0, tiled=True),
        lax.psum_scatter(grad_gain_one, "wide", scatter_dimension=0, tiled=True),
        lax.psum_scatter(grad_gain_two, "wide", scatter_dimension=0, tiled=True),
    )
    summed = lax.psum((shards[0], shards[1], shards[2], shards[3], shards[4], shards[5]), "narrow")
    grad_router = lax.psum(grad_router_part, ("wide", "narrow"))
    return (
        mixed,
        grad_tokens,
        summed[0],
        summed[1],
        summed[2],
        summed[3],
        summed[4],
        summed[5],
        grad_router,
    )


def dot(left, right):
    return jnp.dot(left, right, preferred_element_type=F32)


def dot_nt(left, right):
    return lax.dot_general(left, right, (((1,), (1,)), ((), ())), preferred_element_type=F32)


def dot_tn(left, right):
    return lax.dot_general(left, right, (((0,), (0,)), ((), ())), preferred_element_type=F32)


class Place:
    def __init__(self, wide):
        self.ring = wide // 2
        self.length = self.ring // 2
        self.w = lax.axis_index("wide")
        self.n = lax.axis_index("narrow")
        self.c = self.w % 2
        self.q = self.w // 2
        row = self.q % 2
        col = self.q // 2
        self.r = col + row * (2 * self.length - 1 - 2 * col)

        self.around = {}
        for offset in range(-(self.ring // 2), self.ring // 2 + 1):
            pos = lax.rem(self.r + offset + self.ring, self.ring)
            row = pos // self.length
            col = pos + row * (2 * self.length - 1 - 2 * pos)
            self.around[offset] = col * 2 + row

    def chip(self, offset):
        return self.around[offset]

    def at_ring(self, offset):
        return (self.around[offset] * 2 + self.c, self.n)

    def sibling(self):
        return (self.q * 2 + 1 - self.c, self.n)

    def across(self):
        return (self.w, 1 - self.n)

    def flipped(self, bit):
        return ((self.q + bit - 2 * bit * ((self.q // bit) % 2)) * 2 + self.c, self.n)


def greet(partners):
    barrier = pltpu.get_barrier_semaphore()
    for partner in partners:
        pl.semaphore_signal(barrier, inc=1, device_id=partner, device_id_type=MESH)
    pl.semaphore_wait(barrier, len(partners))


def remote(src, dst, send, recv, device):
    return pltpu.make_async_remote_copy(
        src_ref=src, dst_ref=dst, send_sem=send, recv_sem=recv, device_id=device, device_id_type=MESH
    )


def probabilities(live, queries, keys):
    entries = queries.shape[0]
    scores = dot_nt(queries, keys) * 0.125
    q_at = lax.broadcasted_iota(jnp.int32, (entries, entries), 0)
    k_at = lax.broadcasted_iota(jnp.int32, (entries, entries), 1)
    scores = jnp.where((k_at <= q_at) & (live > 0), scores, masked_score)
    expo = jnp.exp(scores - jnp.max(scores, axis=-1, keepdims=True))
    return expo / jnp.sum(expo, axis=-1, keepdims=True)


def only(value, head):
    lane = lax.broadcasted_iota(jnp.int32, value.shape, 1)
    return jnp.where(lane // HEAD_DIM == head, value, jnp.zeros_like(value))


def gelu_pair(x):
    inner = 0.7978845608028654 * (x + 0.044715 * (x * x * x))
    bent = jnp.tanh(inner)
    half = 0.5 * (1.0 + bent)
    slope = 0.7978845608028654 * (1.0 + 0.134145 * (x * x))
    return x * half, half + 0.5 * x * (1.0 - bent * bent) * slope


def forward_kernel(
    wide,
    gains,
    wq,
    wo,
    wu,
    wd,
    kept,
    given,
    router,
    live,
    wq_all,
    wo_all,
    normed_t,
    heads_t,
    second_t,
    act_t,
    d_pre,
    d_mlp,
    d_attend,
    project,
    base,
    out_low,
    rows_low,
    small,
    scales,
    wu_all,
    wd_all,
    gains_all,
    got,
    normed,
    heads,
    attend_out,
    second_n,
    second,
    d_act,
    act,
    mlp_out,
    d_second,
    router_val,
    inverse_two,
    own_sem,
    ring_send,
    ring_recv,
    sib_send,
    sib_recv,
    x_send,
    x_recv,
    row_send,
    row_recv,
):
    at = Place(wide)
    ring, steps = at.ring, at.ring // 2
    depth, width = wo.shape
    quarter = depth // 4
    carried = depth - quarter
    entries = kept.shape[1]
    ups, downs = wu.shape[1] // width, wd.shape[0]
    tile = 256
    chips_of_tile = tile // (2 * depth)

    parts = [(gains, gains_all)]
    ready = {0: [0]}

    def add(name, shard, full, first, pieces=PIECES):
        for size in pieces:
            cols = pl.ds(first, size)
            parts.append((shard.at[:, cols], full.at[:, :, :, cols], size))
            if name is None:
                ready[len(parts) - 1] = [(first, size)]
            first += size
        if name is not None:
            ready[len(parts) - 1] = [name]

    for j in range(3):
        add(1 + j, wq, wq_all, j * width)
    add(4, wo, wo_all, 0)
    for j in range(downs):
        add(5 + j, wd.at[j], wd_all.at[:, :, j], 0)
    for j in range(ups):
        add(None, wu, wu_all, j * width, LAST_PIECES if j == ups - 1 else PIECES)
    count = len(parts)

    def window(k, s=0, d=0):
        if k == 0:
            return pl.ds(0, gains.shape[0]), pl.ds(0, gains.shape[1])
        rows = pl.ds(pl.multiple_of(at.n * quarter, quarter), carried)
        if s == steps:
            return rows, pl.ds(d * (parts[k][2] // 2), parts[k][2] // 2)
        return rows, pl.ds(0, parts[k][2])

    def idle(k, s, d):
        return k == 0 and s == steps and d == 1

    def toward(d):
        return at.at_ring(1 if d == 0 else -1)

    def ring_out(k, s, d):
        pos = -(s - 1) if d == 0 else s - 1
        rows, cols = window(k, s, d)
        dst = parts[k][1].at[at.chip(pos), at.c, rows, cols]
        src = parts[k][0].at[rows, cols] if s == 1 else dst
        return remote(src, dst, ring_send.at[k, s - 1, d], ring_recv.at[k, s - 1, d], toward(d))

    def ring_in(k, s, d):
        pos = -s if d == 0 else s
        rows, cols = window(k, s, d)
        ref = parts[k][1].at[at.chip(pos), at.c, rows, cols]
        return remote(ref, ref, ring_send.at[k, s - 1, d], ring_recv.at[k, s - 1, d], toward(d))

    def own_copy(k):
        rows, cols = window(k)
        return pltpu.make_async_copy(
            parts[k][0].at[rows, cols], parts[k][1].at[at.q, at.c, rows, cols], own_sem.at[k]
        )

    def cross(k, incoming=False):
        side = 1 - at.n if incoming else at.n
        rows = pl.ds(pl.multiple_of(side * carried, quarter), quarter)
        ref = parts[k][1].at[:, at.c, rows]
        return remote(ref, ref, x_send.at[k], x_recv.at[k], at.across())

    def sib(k, incoming=False):
        ref = parts[k][1].at[:, 1 - at.c if incoming else at.c]
        return remote(ref, ref, sib_send.at[k], sib_recv.at[k], at.sibling())

    def row_copy(j):
        return remote(given.at[j], got.at[j], row_send.at[j], row_recv.at[j], at.across())

    def over(size, step):
        def run(piece):
            @pl.loop(0, size // step)
            def _(t):
                piece(pl.multiple_of(t * step, step))

        return run

    def turned(src, dst, first=0):
        @over(src.shape[1], tile)
        def _(low):
            dst[pl.ds(first + low, tile), :] = src[:, pl.ds(low, tile)].T

    def normalise():
        lane = lax.broadcasted_iota(jnp.int32, (8, 2 * HEAD_DIM), 1)
        for chip in range(ring):
            pair = jnp.where(
                lane < depth, gains_all[chip, 0].astype(F32)[:8], gains_all[chip, 1].astype(F32)[:8]
            )
            scales[:, chip * 2 * depth : (chip + 1) * 2 * depth] = pair

        @over(entries, 32)
        def _(low):
            rows = pl.ds(low, 32)
            low_rows = kept[0, rows] + got[0, rows]
            value = low_rows.astype(F32)
            rows_low[rows, :] = low_rows
            inverse = lax.rsqrt(jnp.mean(value * value, axis=-1, keepdims=True) + epsilon)
            normed[rows, :] = (value * inverse * scales[0:1, :]).astype(BF16)
            router_val[rows, :] = jnp.sum(value * router[...], axis=-1, keepdims=True)

    def project_part(j):
        @over(width, tile)
        def _(low):
            cols = pl.ds(j * width + low, tile)
            weight = wq_all[:, :, :, cols].reshape(width, tile)
            project[:, cols] = dot(normed[...], weight).astype(BF16)

    def attention(first, last):
        @pl.loop(first, last)
        def _(p):
            lanes = 2 * HEAD_DIM
            q = project[:, pl.ds(pl.multiple_of(p * lanes, lanes), lanes)]
            k = project[:, pl.ds(pl.multiple_of(width + p * lanes, lanes), lanes)]
            v = project[:, pl.ds(pl.multiple_of(2 * width + p * lanes, lanes), lanes)]
            total = jnp.zeros((entries, lanes), F32)
            for head in (0, 1):
                probs = probabilities(live[...], only(q, head), k)
                total = total + only(dot(probs.astype(BF16), v), head)
            heads[:, pl.ds(pl.multiple_of(p * lanes, lanes), lanes)] = total.astype(BF16)

    def attend_project():
        @over(width, tile)
        def _(low):
            cols = pl.ds(low, tile)
            weight = wo_all[:, :, :, cols].reshape(width, tile)
            attend_out[:, cols] = dot(heads[...], weight)

        @over(entries, 32)
        def _(low):
            rows = pl.ds(low, 32)
            middle = rows_low[rows, :].astype(F32) + attend_out[rows, :]
            inverse = lax.rsqrt(jnp.mean(middle * middle, axis=-1, keepdims=True) + epsilon)
            value = middle * inverse
            second_n[rows, :] = value
            inverse_two[rows, :] = inverse
            second[rows, :] = (value * scales[1:2, :]).astype(BF16)

    def branch_grad():
        @over(entries, 32)
        def _(low):
            rows = pl.ds(low, 32)
            dout = (kept[1, rows] + got[1, rows]).astype(F32)
            d_mlp[rows, :] = (router_val[rows, :] * dout).astype(BF16)

    def act_grad():
        @pl.loop(0, ring)
        def _(chip):
            for core in (0, 1):
                size = downs * depth
                cols = pl.ds(pl.multiple_of(chip * (2 * size) + core * size, size), size)
                d_act[:, cols] = dot_nt(d_mlp[...], wd_all[chip, core].reshape(size, width))

    def up_part(first, size):
        @over(size, tile)
        def _(low):
            cols = pl.ds(first + low, tile)
            pre = dot(second[...], wu_all[:, :, :, cols].reshape(width, tile))
            value, slope = gelu_pair(pre)
            value = value.astype(BF16)
            act[:, pl.ds(low, tile)] = value
            d_pre[:, cols] = (d_act[:, cols] * slope).astype(BF16)
            act_t[cols, :] = value.T

        owner = 2 * depth * downs
        chip, core = first // owner, first % owner // (owner // 2)

        @over(width, tile)
        def _(low):
            cols = pl.ds(low, tile)
            if size == owner:
                down = wd_all[chip, :, :, :, cols]
            else:
                down = wd_all[chip, core, :, :, cols]
            part = dot(act[:, 0:size], down.reshape(size, tile))
            chips = pl.ds(low // (2 * depth), chips_of_tile)
            up = wu_all[chips, :, :, pl.ds(first, size)]
            back = dot_nt(d_pre[:, pl.ds(first, size)], up.reshape(tile, size))
            if first == 0:
                mlp_out[:, cols] = part
                d_second[:, cols] = back
            else:
                mlp_out[:, cols] += part
                d_second[:, cols] += back

    def close():
        small[...] = jnp.zeros_like(small)

        @over(entries, 32)
        def _(low):
            rows = pl.ds(low, 32)
            value = rows_low[rows, :].astype(F32)
            dout = (kept[1, rows] + got[1, rows]).astype(F32)
            gate = router_val[rows, :]
            branch = attend_out[rows, :] + mlp_out[rows, :]
            out_low[rows, :] = (value + gate * branch).astype(BF16)
            d_gate = jnp.sum(dout * branch, axis=-1, keepdims=True)
            normed_value = second_n[rows, :]
            back = d_second[rows, :]
            small[1:2, :] += jnp.sum(back * normed_value, axis=0, keepdims=True)
            small[2:3, :] += jnp.sum(d_gate * value, axis=0, keepdims=True)
            back = back * scales[1:2, :]
            back = inverse_two[rows, :] * (
                back - normed_value * jnp.mean(back * normed_value, axis=-1, keepdims=True)
            )
            d_attend[rows, :] = (gate * dout + back).astype(BF16)
            base[rows, :] = dout + back + d_gate * router[...]

    pairs = width // (2 * HEAD_DIM)
    cuts = [pairs * j // 8 for j in (0, 2, 5, 8)]
    work = [
        [normalise, lambda: turned(normed, normed_t)],
        [lambda: project_part(0)],
        [lambda: project_part(1)],
        [lambda: project_part(2), lambda: attention(cuts[0], cuts[1])],
        [lambda: attention(cuts[1], cuts[2])],
        [lambda: attention(cuts[2], cuts[3])],
        [attend_project],
        [branch_grad, lambda: turned(heads, heads_t), lambda: turned(second, second_t)],
    ]
    work += [[]] * (1 + 3 + 1 + downs - 1 - len(work)) + [[act_grad]]

    greet([at.at_ring(1), at.at_ring(-1), at.sibling(), at.across()])
    row_copy(0).start()
    lag = LAG
    for i in range(count + lag * (steps + 1) + 1):
        if i < count:
            for d in (0, 1):
                ring_out(i, 1, d).start()
            own_copy(i).start()
        if i == 2:
            row_copy(1).start()
        for s in range(1, steps + 1):
            k = i - lag * s
            if 0 <= k < count:
                for d in (0, 1):
                    if not idle(k, s, d):
                        ring_in(k, s, d).wait_recv()
                    if s < steps and not idle(k, s + 1, d):
                        ring_out(k, s + 1, d).start()
                if s == steps:
                    own_copy(k).wait()
                    if k > 0:
                        cross(k).start()
        k = i - lag * (steps + 1)
        if 0 <= k < count:
            if k > 0:
                cross(k, True).wait_recv()
            sib(k).start()
        k = i - lag * (steps + 1) - 1
        if 0 <= k < count:
            sib(k, True).wait_recv()
            if k == 0:
                for j in (0, 1):
                    row_copy(j).wait_recv()
            if k in ready:
                for piece in ready[k]:
                    if isinstance(piece, int):
                        for job in work[piece]:
                            job()
                    else:
                        up_part(*piece)
    close()
    for k in range(count):
        sib(k).wait_send()
        if k > 0:
            cross(k).wait_send()
        for s in range(1, steps + 1):
            for d in (0, 1):
                if not idle(k, s, d):
                    ring_out(k, s, d).wait_send()
    for j in (0, 1):
        row_copy(j).wait_send()


def forward(wide, gains, wq, wo, wu, wd, kept, given, router, live):
    depth, width = wo.shape
    ring, steps = wide // 2, wide // 4
    entries = kept.shape[1]
    ff = wu.shape[1]
    downs = wd.shape[0] // depth
    count = 1 + (3 + downs + ff // width) * len(PIECES) + len(LAST_PIECES)
    vmem = pl.BlockSpec(memory_space=pltpu.VMEM)
    anywhere = pl.BlockSpec(memory_space=pl.ANY)
    dma = pltpu.SemaphoreType.DMA
    shape = jax.ShapeDtypeStruct
    return pl.pallas_call(
        functools.partial(forward_kernel, wide),
        out_shape=[
            shape((ring, 2, depth, 3 * width), BF16),
            shape((ring, 2, depth, width), BF16),
            shape((width, entries), BF16),
            shape((width, entries), BF16),
            shape((width, entries), BF16),
            shape((ff, entries), BF16),
            shape((entries, ff), BF16),
            shape((entries, width), BF16),
            shape((entries, width), BF16),
            shape((entries, 3 * width), BF16),
            shape((entries, width), F32),
            shape((entries, width), BF16),
            shape((entries, width), BF16),
            shape((8, width), F32),
            shape((8, width), F32),
        ],
        in_specs=[anywhere] * 5 + [vmem, anywhere, vmem, vmem],
        out_specs=[vmem] * 15,
        scratch_shapes=[
            pltpu.VMEM((ring, 2, depth, ff), BF16),
            pltpu.VMEM((ring, 2, downs, depth, width), BF16),
            pltpu.VMEM((ring, 2) + gains.shape, BF16),
            pltpu.VMEM((2, entries, width), BF16),
            pltpu.VMEM((entries, width), BF16),
            pltpu.VMEM((entries, width), BF16),
            pltpu.VMEM((entries, width), F32),
            pltpu.VMEM((entries, width), F32),
            pltpu.VMEM((entries, width), BF16),
            pltpu.VMEM((entries, ff), F32),
            pltpu.VMEM((entries, width), BF16),
            pltpu.VMEM((entries, width), F32),
            pltpu.VMEM((entries, width), F32),
            pltpu.VMEM((entries, 1), F32),
            pltpu.VMEM((entries, 1), F32),
            dma((count,)),
            dma((count, steps, 2)),
            dma((count, steps, 2)),
            dma((count,)),
            dma((count,)),
            dma((count,)),
            dma((count,)),
            dma((2,)),
            dma((2,)),
        ],
        compiler_params=pltpu.CompilerParams(
            collective_id=1, has_side_effects=True, vmem_limit_bytes=60 * 1024 * 1024
        ),
        name="gather",
    )(gains, wq, wo, wu, wd.reshape(downs, depth, width), kept, given, router, live)


def backward_kernel(
    wide,
    chunks,
    wq_all,
    wo_all,
    act_t,
    second_t,
    heads_t,
    normed_t,
    d_mlp,
    d_pre,
    d_attend,
    project,
    base,
    rows_low,
    scales,
    small,
    live,
    out_low,
    o_qkv,
    o_out,
    o_up,
    o_down,
    o_small,
    rows_got,
    grad_low,
    d_heads,
    d_project,
    d_normed,
    own,
    to_sib,
    mine,
    landed,
    moving,
    x_pre,
    x_out,
    x_in,
    small_acc,
    small_in,
    sib_send,
    sib_recv,
    pre_send,
    pre_recv,
    ring_send,
    ring_recv,
    x_send,
    x_recv,
    small_send,
    small_recv,
    row_send,
    row_recv,
):
    at = Place(wide)
    ring, steps = at.ring, at.ring // 2
    depth, width = o_out.shape
    half = depth // 2
    entries = d_mlp.shape[0]
    count = len(chunks)
    tile = 256
    step = 16
    starts = [sum(c[3] for c in chunks[:k]) for k in range(count)]
    give_starts = [sum(c[4] for c in chunks[:k]) for k in range(count)]

    def lanes(first, size):
        return pl.ds(first if isinstance(first, int) else pl.multiple_of(first, 128), size)

    def whole(k):
        return lanes(starts[k], chunks[k][3])

    def carried(k):
        size, give = chunks[k][3:]
        return lanes(starts[k] + give * at.n, size - give)

    def kept_alone(k):
        size, give = chunks[k][3:]
        return lanes(starts[k] + (size - give) * at.n, give)

    def product(k, core, put):
        kind, j, first, size, _ = chunks[k]
        if kind == "down":
            left, right = act_t[:, core, j], d_mlp
        else:
            tall, right = {
                "up": (second_t, d_pre),
                "out": (heads_t, d_attend),
                "qkv": (normed_t, d_project),
            }[kind]
            left = tall[:, core]
        left = left.reshape(ring * depth, entries)

        @pl.loop(0, size // tile)
        def _(t):
            cols = pl.ds(pl.multiple_of(t * tile, tile), tile)
            take = pl.ds(pl.multiple_of(first + t * tile, tile), tile)
            put(cols, dot(left, right[:, take]).reshape(ring, depth, tile))

    def store(k):
        kind, j, first, size, _ = chunks[k]
        out = {"up": o_up, "down": o_down, "out": o_out, "qkv": o_qkv}[kind]
        return out, j * depth if kind == "down" else 0, first

    def sib(k):
        src = to_sib.at[k % 2, :, :, pl.ds(0, chunks[k][3])]
        return remote(src, mine.at[:, :, whole(k)], sib_send.at[k], sib_recv.at[k], at.sibling())

    def pre(k):
        size, give = chunks[k][3:]
        src = mine.at[:, :, lanes(starts[k] + (size - give) * (1 - at.n), give)]
        dst = x_pre.at[:, :, lanes(give_starts[k], give)]
        return remote(src, dst, pre_send.at[k], pre_recv.at[k], at.across())

    def toward(d):
        return at.at_ring(1 if d == 0 else -1)

    def dest(t, d):
        return at.chip(steps - t if d == 0 else t - steps)

    def arrival(k, t, d):
        cols = carried(k)
        return landed.at[d, :, cols] if t == 0 else moving.at[t - 1, d, :, cols]

    def ring_out(k, t, d):
        rows = pl.ds(d * half, half) if t == 0 else pl.ds(0, depth)
        src = mine.at[dest(t, d), rows, carried(k)]
        return remote(
            src, arrival(k, t, d), ring_send.at[k, t, d], ring_recv.at[k, t, d], toward(d)
        )

    def cross(k):
        cols = carried(k)
        return remote(x_out.at[:, cols], x_in.at[:, cols], x_send.at[k], x_recv.at[k], at.across())

    bits = [1 << b for b in range(ring.bit_length() - 1)]
    partners = [at.sibling(), at.across()] + [at.flipped(bit) for bit in bits]
    stages = len(partners)

    def small_copy(j):
        return remote(
            small_acc.at[j], small_in.at[j], small_send.at[j], small_recv.at[j], partners[j]
        )

    def row_copy(j, p):
        rows = pl.ds(p * (entries // ROW_PIECES), entries // ROW_PIECES)
        src = out_low if j == 0 else grad_low
        return remote(
            src.at[rows], rows_got.at[j, rows], row_send.at[j, p], row_recv.at[j, p], at.across()
        )

    def over(size, piece_size):
        def run(piece):
            @pl.loop(0, size // piece_size)
            def _(t):
                piece(pl.multiple_of(t * piece_size, piece_size))

        return run

    def heads_grad():
        @over(width, tile)
        def _(low):
            chips = pl.ds(low // (2 * depth), tile // (2 * depth))
            weight = wo_all[chips].reshape(tile, width)
            d_heads[:, pl.ds(low, tile)] = dot_nt(d_attend[...], weight).astype(BF16)

    def attention(first, last):
        span = 2 * HEAD_DIM

        @pl.loop(first, last)
        def _(p):
            places = [lanes(j * width + p * span, span) for j in range(3)]
            q, k, v = [project[:, place] for place in places]
            d_pair = d_heads[:, places[0]]
            d_q = jnp.zeros((entries, span), F32)
            d_k = jnp.zeros((entries, span), F32)
            d_v = jnp.zeros((entries, span), F32)
            for head in (0, 1):
                probs = probabilities(live[...], only(q, head), k)
                d_own = only(d_pair, head)
                d_probs = dot_nt(d_own, v)
                d_scores = probs * (d_probs - jnp.sum(probs * d_probs, axis=-1, keepdims=True))
                d_scores = d_scores.astype(BF16)
                d_q = d_q + only(dot(d_scores, k), head)
                d_k = d_k + only(dot_tn(d_scores, q), head)
                d_v = d_v + dot_tn(probs.astype(BF16), d_own)
            d_project[:, places[0]] = (d_q * 0.125).astype(BF16)
            d_project[:, places[1]] = (d_k * 0.125).astype(BF16)
            d_project[:, places[2]] = d_v.astype(BF16)

    def normed_grad(j):
        @over(width, tile)
        def _(low):
            chips = pl.ds(low // (2 * depth), tile // (2 * depth))
            weight = wq_all[chips, :, :, pl.ds(j * width, width)].reshape(tile, width)
            part = dot_nt(d_project[:, pl.ds(j * width, width)], weight)
            cols = pl.ds(low, tile)
            if j == 0:
                d_normed[:, cols] = part
            else:
                d_normed[:, cols] += part

    def finish():
        small_acc[0] = small[...]

        @over(entries, 32)
        def _(low):
            rows = pl.ds(low, 32)
            value = rows_low[rows, :].astype(F32)
            inverse = lax.rsqrt(jnp.mean(value * value, axis=-1, keepdims=True) + epsilon)
            value = value * inverse
            back = d_normed[rows, :]
            small_acc[0, 0:1, :] += jnp.sum(back * value, axis=0, keepdims=True)
            back = back * scales[0:1, :]
            back = inverse * (back - value * jnp.mean(back * value, axis=-1, keepdims=True))
            grad_low[rows, :] = (base[rows, :] + back).astype(BF16)

    pairs = width // (2 * HEAD_DIM)
    cuts = [pairs * j // 4 for j in range(5)]
    work = [heads_grad]
    work += [functools.partial(attention, cuts[j], cuts[j + 1]) for j in range(4)]
    work += [functools.partial(normed_grad, j) for j in range(3)]
    work += [finish]

    x_out[...] = jnp.zeros_like(x_out)
    x_in[...] = jnp.zeros_like(x_in)
    greet(partners + [at.at_ring(1), at.at_ring(-1)])
    lag = LAG
    ring_at = 1 + lag
    total = count + ring_at + lag * steps + lag + 1
    small_at = len(work)
    for i in range(total):
        k = i - ring_at - lag * steps - lag
        if 0 <= k < count:
            cross(k).wait_recv()
            out, low, first = store(k)
            size = chunks[k][3]

            @over(depth, step)
            def _(row):
                rows = pl.ds(row, step)
                value = x_out[rows, whole(k)].astype(F32) + x_in[rows, whole(k)].astype(F32)
                out[pl.ds(low + row, step), first : first + size] = value

        k = i - ring_at - lag * steps
        if 0 <= k < count:
            cols = carried(k)
            for d in (0, 1):
                remote(
                    arrival(k, steps - 1, d),
                    arrival(k, steps - 1, d),
                    ring_send.at[k, steps - 1, d],
                    ring_recv.at[k, steps - 1, d],
                    toward(d),
                ).wait_recv()

            @over(depth, step)
            def _(row):
                rows = pl.ds(row, step)
                value = mine[at.q, rows, cols].astype(F32)
                value = value + moving[steps - 2, 0, rows, cols].astype(F32)
                value = value + moving[steps - 2, 1, rows, cols].astype(F32)
                x_out[rows, cols] = value.astype(BF16)

            cross(k).start()
        for t in range(steps - 1, 0, -1):
            k = i - ring_at - lag * t
            if 0 <= k < count:
                cols = carried(k)
                for d in (0, 1):
                    remote(
                        arrival(k, t - 1, d),
                        arrival(k, t - 1, d),
                        ring_send.at[k, t - 1, d],
                        ring_recv.at[k, t - 1, d],
                        toward(d),
                    ).wait_recv()
                    to = dest(t, d)
                    size = half if t == 1 else depth
                    base_row = d * half if t == 1 else 0

                    @over(size, step)
                    def _(row):
                        into = pl.ds(base_row + row, step)
                        if t == 1:
                            got = landed[d, pl.ds(row, step), cols]
                        else:
                            got = moving[t - 2, d, pl.ds(row, step), cols]
                        value = mine[to, into, cols].astype(F32) + got.astype(F32)
                        mine[to, into, cols] = value.astype(BF16)

                    ring_out(k, t, d).start()
        k = i - ring_at
        if 0 <= k < count:
            if chunks[k][4] > 0:
                pre(k).wait_recv()
                cols = kept_alone(k)
                take = lanes(give_starts[k], chunks[k][4])

                @pl.loop(0, ring)
                def _(chip):
                    value = mine[chip, :, cols].astype(F32) + x_pre[chip, :, take].astype(F32)
                    mine[chip, :, cols] = value.astype(BF16)

            for d in (0, 1):
                ring_out(k, 0, d).start()
        k = i - 1
        if 0 <= k < count:
            remote(
                mine.at[:, :, whole(k)],
                mine.at[:, :, whole(k)],
                sib_send.at[k],
                sib_recv.at[k],
                at.sibling(),
            ).wait_recv()
            size = chunks[k][3]

            @pl.loop(0, ring)
            def _(chip):
                value = mine[chip, :, whole(k)].astype(F32) + own[chip, :, 0:size]
                mine[chip, :, whole(k)] = value.astype(BF16)

            if chunks[k][4] > 0:
                pre(k).start()
        k = i
        if k < count:
            if k >= 2:
                sib(k - 2).wait_send()

            def keep_other(cols, value):
                to_sib[k % 2, :, :, cols] = value.astype(BF16)

            def keep_own(cols, value):
                own[:, :, cols] = value

            product(k, 1 - at.c, keep_other)
            sib(k).start()
            product(k, at.c, keep_own)
        if i < len(work):
            work[i]()
        if i < ROW_PIECES:
            row_copy(0, i).start()
        p = i - max(len(work), count - ROW_PIECES)
        if 0 <= p < ROW_PIECES:
            row_copy(1, p).start()
        j = i - small_at
        if 0 <= j <= stages:
            if j > 0:
                small_copy(j - 1).wait_recv()
                small_acc[j] = small_acc[j - 1] + small_in[j - 1]
            if j < stages:
                small_copy(j).start()
            else:
                o_small[...] = small_acc[stages]

    for k in range(count):
        if k >= count - 2:
            sib(k).wait_send()
        if chunks[k][4] > 0:
            pre(k).wait_send()
        cross(k).wait_send()
        for t in range(steps):
            for d in (0, 1):
                ring_out(k, t, d).wait_send()
    for j in range(stages):
        small_copy(j).wait_send()
    for j in (0, 1):
        for p in range(ROW_PIECES):
            row_copy(j, p).wait()


def backward(
    wide,
    wq_all,
    wo_all,
    act_t,
    second_t,
    heads_t,
    normed_t,
    d_mlp,
    d_pre,
    d_attend,
    project,
    base,
    rows_low,
    scales,
    small,
    live,
    out_low,
):
    entries, width = d_mlp.shape
    ring, steps = wide // 2, wide // 4
    depth = width // wide
    ff = d_pre.shape[1]
    ups = downs = ff // width
    chunks = []
    panels = [("up", j, j * width) for j in range(ups)]
    panels += [("down", j, 0) for j in range(downs)]
    panels += [("out", 0, 0)]
    panels += [("qkv", j, j * width) for j in range(3)]
    last = len(panels) - 1
    for index, (kind, j, first) in enumerate(panels):
        for size in FIRST_PIECES if index == 0 else LAST_PIECES if index == last else PIECES:
            chunks.append((kind, j, first, size))
            first += size
    chunks = [
        c + (GIVE if GIVE_SKIP[0] <= k < len(chunks) - GIVE_SKIP[1] and c[3] == 512 else 0,)
        for k, c in enumerate(chunks)
    ]
    chunks = tuple(chunks)
    count = len(chunks)
    everything = sum(c[3] for c in chunks)
    given = sum(c[4] for c in chunks)
    stages = 2 + (ring.bit_length() - 1)
    vmem = pl.BlockSpec(memory_space=pltpu.VMEM)
    anywhere = pl.BlockSpec(memory_space=pl.ANY)
    dma = pltpu.SemaphoreType.DMA
    shape = jax.ShapeDtypeStruct

    def tall(value):
        return value.reshape(ring, 2, depth, entries)

    return pl.pallas_call(
        functools.partial(backward_kernel, wide, chunks),
        out_shape=[
            shape((depth, 3 * width), F32),
            shape((depth, width), F32),
            shape((depth, ff), F32),
            shape((ff // wide, width), F32),
            shape((8, width), F32),
            shape((2, entries, width), BF16),
            shape((entries, width), BF16),
        ],
        in_specs=[vmem] * 15 + [anywhere],
        out_specs=[vmem] * 5 + [anywhere, vmem],
        scratch_shapes=[
            pltpu.VMEM((entries, width), BF16),
            pltpu.VMEM((entries, 3 * width), BF16),
            pltpu.VMEM((entries, width), F32),
            pltpu.VMEM((ring, depth, 512), F32),
            pltpu.VMEM((2, ring, depth, 512), BF16),
            pltpu.VMEM((ring, depth, everything), BF16),
            pltpu.VMEM((2, depth // 2, everything), BF16),
            pltpu.VMEM((steps - 1, 2, depth, everything), BF16),
            pltpu.VMEM((ring, depth, max(given, 128)), BF16),
            pltpu.VMEM((depth, everything), BF16),
            pltpu.VMEM((depth, everything), BF16),
            pltpu.VMEM((stages + 1, 8, width), F32),
            pltpu.VMEM((stages, 8, width), F32),
            dma((count,)),
            dma((count,)),
            dma((count,)),
            dma((count,)),
            dma((count, steps, 2)),
            dma((count, steps, 2)),
            dma((count,)),
            dma((count,)),
            dma((stages,)),
            dma((stages,)),
            dma((2, ROW_PIECES)),
            dma((2, ROW_PIECES)),
        ],
        compiler_params=pltpu.CompilerParams(
            collective_id=2, has_side_effects=True, vmem_limit_bytes=62 * 1024 * 1024
        ),
        name="reduce",
    )(
        wq_all,
        wo_all,
        act_t.reshape(ring, 2, downs, depth, entries),
        tall(second_t),
        tall(heads_t),
        tall(normed_t),
        d_mlp,
        d_pre,
        d_attend,
        project,
        base,
        rows_low,
        scales,
        small,
        live,
        out_low,
    )


def paired_body(
    wide, tokens, cotangent, lengths, routes, w_qkv, w_out, w_up, w_down, gain_attn, gain_mlp, router
):
    place = lax.axis_index("narrow")
    seqs, span, width = tokens.shape
    list_len = routes.shape[1]
    depth = gain_attn.shape[0]
    counts = lengths // 8
    entry = jnp.arange(list_len, dtype=jnp.int32)
    live = entry[None, :] < counts[:, None]
    local_slot = jnp.where(live, routes - place * span, -1)
    spots = jnp.arange(span, dtype=jnp.int32)
    chosen = (local_slot[:, :, None] == spots[None, None, :]).astype(BF16)

    def take(source):
        return jnp.einsum("sep,spd->sed", chosen, source, preferred_element_type=F32).astype(BF16)

    picked = jnp.stack([take(tokens), take(cotangent)])
    kept = lax.dynamic_index_in_dim(picked, place, 1, keepdims=False)
    given = lax.dynamic_index_in_dim(picked, 1 - place, 1, keepdims=False)
    gains = jnp.stack(
        [jnp.concatenate([gain_attn, gain_attn]), jnp.concatenate([gain_mlp, gain_mlp])]
    )
    gains = jnp.pad(gains, ((0, 14), (0, 0)))
    router_row = router.astype(F32)[None, :]
    live_row = lax.dynamic_index_in_dim(live, place, 0, keepdims=True).astype(jnp.int32)
    (
        weight_qkv,
        weight_out,
        normed_t,
        heads_t,
        second_t,
        act_t,
        d_pre,
        d_mlp,
        d_attend,
        project,
        base,
        out_low,
        rows_low,
        small,
        scales,
    ) = forward(wide, gains, w_qkv, w_out, w_up, w_down, kept, given, router_row, live_row)

    grad_qkv, grad_out, grad_up, grad_down, small, back_got, grad_low = backward(
        wide,
        weight_qkv,
        weight_out,
        act_t,
        second_t,
        heads_t,
        normed_t,
        d_mlp,
        d_pre,
        d_attend,
        project,
        base,
        rows_low,
        scales,
        small,
        live_row,
        out_low,
    )
    back = jnp.stack([out_low, grad_low])
    first = place == 0
    rows_out = jnp.stack([jnp.where(first, back, back_got), jnp.where(first, back_got, back)], axis=1)
    hit = jnp.any(local_slot[:, :, None] == spots[None, None, :], axis=1)

    def put(base, fresh):
        spread = jnp.einsum("sep,sed->spd", chosen, fresh, preferred_element_type=F32)
        return jnp.where(hit[:, :, None], spread.astype(BF16), base)

    start = lax.axis_index("wide") * depth
    return (
        put(tokens, rows_out[0]),
        put(cotangent, rows_out[1]),
        grad_qkv,
        grad_out,
        grad_up,
        grad_down,
        lax.dynamic_slice_in_dim(small[0], start, depth),
        lax.dynamic_slice_in_dim(small[1], start, depth),
        small[2],
    )


def body(wide, narrow, tokens, *others):
    if narrow == 2 and tokens.shape[0] == 2 and wide == 16:
        return paired_body(wide, tokens, *others)
    return general_body(tokens, *others)


def solution(mesh):
    in_specs = (
        P("wide", "narrow", None),
        P("wide", "narrow", None),
        P("wide"),
        P("wide", None),
        P("wide", None),
        P("wide", None),
        P("wide", None),
        P("wide", None),
        P("wide"),
        P("wide"),
        P(),
    )
    out_specs = (
        P("wide", "narrow", None),
        P("wide", "narrow", None),
        P("wide", None),
        P("wide", None),
        P("wide", None),
        P("wide", None),
        P("wide"),
        P("wide"),
        P(),
    )
    sizes = mesh.shape["wide"], mesh.shape["narrow"]
    return jax.shard_map(functools.partial(body, *sizes), mesh=mesh, in_specs=in_specs, out_specs=out_specs, check_vma=False)
```

```python
import functools
from typing import NamedTuple

import jax
import jax.numpy as jnp
from jax import lax
from jax.experimental import pallas as pl
from jax.experimental.pallas import tpu as pltpu
from jax.sharding import PartitionSpec as P

HEAD_DIM = 64
MESH = pl.DeviceIdType.MESH
F32 = jnp.float32
BF16 = jnp.bfloat16
LAG = 2
PIECES = (512, 512)
LAST_PIECES = (512, 256, 256)
GIVE = 128
GIVE_SKIP = (3, 6)
ROW_PIECES = 8

epsilon = 1e-06
masked_score = -1e30


def rms_parts(values):
    inverse = lax.rsqrt(jnp.mean(values * values, axis=-1, keepdims=True) + epsilon)
    return (values * inverse, inverse)


def rms_back(grad_normed, normed, inverse):
    return inverse * (grad_normed - normed * jnp.mean(grad_normed * normed, axis=-1, keepdims=True))


def attend_scores(queries, keys_all, allowed):
    scores = (
        jnp.einsum("sqhe,skhe->shqk", queries, keys_all, preferred_element_type=jnp.float32) * 0.125
    )
    return jnp.where(allowed, scores, masked_score)


def attend_forward(queries, keys_all, values_all, allowed):
    scores = attend_scores(queries, keys_all, allowed)
    top_score = jnp.max(scores, axis=-1, keepdims=True)
    expo = jnp.exp(scores - top_score)
    total = jnp.sum(expo, axis=-1, keepdims=True)
    log_total = top_score + jnp.log(total)
    probs_low = (expo / total).astype(jnp.bfloat16)
    heads_out = jnp.einsum(
        "shqk,skhe->sqhe", probs_low, values_all, preferred_element_type=jnp.float32
    )
    return (heads_out, log_total)


def attend_backward(queries, keys_all, values_all, allowed, log_total, d_heads):
    probs_again = jnp.exp(attend_scores(queries, keys_all, allowed) - log_total)
    d_probs = jnp.einsum("sqhe,skhe->shqk", d_heads, values_all, preferred_element_type=jnp.float32)
    row_dot = jnp.sum(probs_again * d_probs, axis=-1, keepdims=True)
    d_scores = (probs_again * (d_probs - row_dot)).astype(jnp.bfloat16)
    d_queries = (
        jnp.einsum("shqk,skhe->sqhe", d_scores, keys_all, preferred_element_type=jnp.float32)
        * 0.125
    )
    d_key_part = (
        jnp.einsum("shqk,sqhe->skhe", d_scores, queries, preferred_element_type=jnp.float32) * 0.125
    )
    d_value_part = jnp.einsum(
        "shqk,sqhe->skhe",
        probs_again.astype(jnp.bfloat16),
        d_heads,
        preferred_element_type=jnp.float32,
    )
    return (d_queries, d_key_part, d_value_part)


def general_body(
    tokens, cotangent, lengths, routes, w_qkv, w_out, w_up, w_down, gain_attn, gain_mlp, router
):
    parts_narrow = lax.axis_size("narrow")
    place = lax.axis_index("narrow")
    seqs, span, width = tokens.shape
    list_len = routes.shape[1]
    own_entries = list_len // parts_narrow
    rows_total = seqs * own_entries
    counts = lengths // 8
    entry = jnp.arange(list_len, dtype=jnp.int32)
    live = entry[None, :] < counts[:, None]
    local_slot = routes - place * span
    mine = live & (local_slot >= 0) & (local_slot < span)
    pick = jnp.clip(local_slot, 0, span - 1)
    keep = mine[:, :, None]
    taken_in = jnp.take_along_axis(tokens, pick[:, :, None], axis=1)
    taken_cot = jnp.take_along_axis(cotangent, pick[:, :, None], axis=1)
    blank = jnp.zeros_like(taken_in)
    rows_in, rows_cot = (
        lax.psum_scatter(
            jnp.where(keep, taken_in, blank), "narrow", scatter_dimension=1, tiled=True
        ).astype(jnp.float32),
        lax.psum_scatter(
            jnp.where(keep, taken_cot, blank), "narrow", scatter_dimension=1, tiled=True
        ).astype(jnp.float32),
    )
    inputs_rows = rows_in.reshape(rows_total, width)
    inputs_low = inputs_rows.astype(jnp.bfloat16)
    dout = rows_cot.reshape(rows_total, width)
    gathered = (
        lax.all_gather(w_qkv, "wide", axis=0, tiled=True),
        lax.all_gather(w_out, "wide", axis=0, tiled=True),
        lax.all_gather(w_up, "wide", axis=0, tiled=True),
        lax.all_gather(w_down, "wide", axis=0, tiled=True),
        lax.all_gather(gain_attn, "wide", axis=0, tiled=True),
        lax.all_gather(gain_mlp, "wide", axis=0, tiled=True),
    )
    weight_qkv, weight_out, weight_up, weight_down, gain_first, gain_second = gathered
    scale_first = gain_first.astype(jnp.float32)
    scale_second = gain_second.astype(jnp.float32)
    normed_one, inverse_one = rms_parts(inputs_rows)
    normed_low = (normed_one * scale_first).astype(jnp.bfloat16)
    project = jnp.dot(normed_low, weight_qkv, preferred_element_type=jnp.float32).astype(
        jnp.bfloat16
    )
    queries = project[:, :width].reshape(seqs, own_entries, -1, HEAD_DIM)
    key_own = project[:, width : 2 * width].reshape(seqs, own_entries, width)
    value_own = project[:, 2 * width :].reshape(seqs, own_entries, width)
    keys_all, values_all = (
        lax.all_gather(key_own, "narrow", axis=1, tiled=True),
        lax.all_gather(value_own, "narrow", axis=1, tiled=True),
    )
    keys_all = keys_all.reshape(seqs, list_len, -1, HEAD_DIM)
    values_all = values_all.reshape(seqs, list_len, -1, HEAD_DIM)
    query_pos = place * own_entries + jnp.arange(own_entries, dtype=jnp.int32)
    allowed = (entry[None, None, None, :] <= query_pos[None, None, :, None]) & (
        entry[None, None, None, :] < counts[:, None, None, None]
    )
    heads_out, log_total = attend_forward(queries, keys_all, values_all, allowed)
    heads_low = heads_out.reshape(rows_total, width).astype(jnp.bfloat16)
    attend_out = jnp.dot(heads_low, weight_out, preferred_element_type=jnp.float32)
    middle = inputs_rows + attend_out
    normed_two, inverse_two = rms_parts(middle)
    second_low = (normed_two * scale_second).astype(jnp.bfloat16)
    pre_act = jnp.dot(second_low, weight_up, preferred_element_type=jnp.float32)
    activ_full, gelu_back = jax.vjp(jax.nn.gelu, pre_act)
    activ_low = activ_full.astype(jnp.bfloat16)
    mlp_out = jnp.dot(activ_low, weight_down, preferred_element_type=jnp.float32)
    branch = attend_out + mlp_out
    router_val = jnp.dot(inputs_low, router, preferred_element_type=jnp.float32)
    out_low = (inputs_rows + router_val[:, None] * branch).astype(jnp.bfloat16)
    back_set = (
        lax.all_gather(w_qkv, "wide", axis=0, tiled=True),
        lax.all_gather(w_out, "wide", axis=0, tiled=True),
        lax.all_gather(w_up, "wide", axis=0, tiled=True),
        lax.all_gather(w_down, "wide", axis=0, tiled=True),
        lax.all_gather(gain_attn, "wide", axis=0, tiled=True),
        lax.all_gather(gain_mlp, "wide", axis=0, tiled=True),
    )
    back_qkv, back_out, back_up, back_down, back_gain_a, back_gain_m = back_set
    back_first = back_gain_a.astype(jnp.float32)
    back_second = back_gain_m.astype(jnp.float32)
    d_branch = router_val[:, None] * dout
    d_router_val = jnp.sum(dout * branch, axis=-1)
    d_mlp = d_branch.astype(jnp.bfloat16)
    grad_down_full = jnp.einsum("rf,rd->fd", activ_low, d_mlp, preferred_element_type=jnp.float32)
    d_act = jnp.einsum("rd,fd->rf", d_mlp, back_down, preferred_element_type=jnp.float32)
    d_pre = gelu_back(d_act)[0].astype(jnp.bfloat16)
    grad_up_full = jnp.einsum("rd,rf->df", second_low, d_pre, preferred_element_type=jnp.float32)
    d_normed_two = jnp.einsum("rf,df->rd", d_pre, back_up, preferred_element_type=jnp.float32)
    grad_gain_two = jnp.sum(d_normed_two * normed_two, axis=0)
    d_middle = rms_back(d_normed_two * back_second, normed_two, inverse_two)
    d_attend = (d_branch + d_middle).astype(jnp.bfloat16)
    grad_out_full = jnp.einsum("rd,re->de", heads_low, d_attend, preferred_element_type=jnp.float32)
    d_heads = jnp.einsum(
        "re,de->rd", d_attend, back_out, preferred_element_type=jnp.float32
    ).astype(jnp.bfloat16)
    d_heads_own = d_heads.reshape(seqs, own_entries, -1, HEAD_DIM)
    d_queries, d_key_part, d_value_part = attend_backward(
        queries, keys_all, values_all, allowed, log_total, d_heads_own
    )
    d_key_own, d_value_own = (
        lax.psum_scatter(
            d_key_part.reshape(seqs, list_len, width), "narrow", scatter_dimension=1, tiled=True
        ),
        lax.psum_scatter(
            d_value_part.reshape(seqs, list_len, width), "narrow", scatter_dimension=1, tiled=True
        ),
    )
    d_project = jnp.concatenate(
        [
            d_queries.reshape(rows_total, width),
            d_key_own.reshape(rows_total, width),
            d_value_own.reshape(rows_total, width),
        ],
        axis=-1,
    ).astype(jnp.bfloat16)
    grad_qkv_full = jnp.einsum(
        "rd,re->de", normed_low, d_project, preferred_element_type=jnp.float32
    )
    d_normed = jnp.einsum("re,de->rd", d_project, back_qkv, preferred_element_type=jnp.float32)
    grad_gain_one = jnp.sum(d_normed * normed_one, axis=0)
    d_norm_rows = rms_back(d_normed * back_first, normed_one, inverse_one)
    d_rows = dout + d_middle + d_norm_rows + d_router_val[:, None] * router.astype(jnp.float32)
    grad_router_part = jnp.dot(d_router_val, inputs_rows, precision=lax.Precision.HIGHEST)
    grad_low = d_rows.astype(jnp.bfloat16)
    out_all, grad_all = (
        lax.all_gather(out_low.reshape(seqs, own_entries, width), "narrow", axis=1, tiled=True),
        lax.all_gather(grad_low.reshape(seqs, own_entries, width), "narrow", axis=1, tiled=True),
    )
    target = jnp.where(mine, pick, span)
    put = jax.vmap(lambda base, where_to, fresh: base.at[where_to].set(fresh, mode="drop"))
    mixed = put(tokens, target, out_all)
    grad_tokens = put(cotangent, target, grad_all)
    shards = (
        lax.psum_scatter(grad_qkv_full, "wide", scatter_dimension=0, tiled=True),
        lax.psum_scatter(grad_out_full, "wide", scatter_dimension=0, tiled=True),
        lax.psum_scatter(grad_up_full, "wide", scatter_dimension=0, tiled=True),
        lax.psum_scatter(grad_down_full, "wide", scatter_dimension=0, tiled=True),
        lax.psum_scatter(grad_gain_one, "wide", scatter_dimension=0, tiled=True),
        lax.psum_scatter(grad_gain_two, "wide", scatter_dimension=0, tiled=True),
    )
    summed = lax.psum((shards[0], shards[1], shards[2], shards[3], shards[4], shards[5]), "narrow")
    grad_router = lax.psum(grad_router_part, ("wide", "narrow"))
    return (
        mixed,
        grad_tokens,
        summed[0],
        summed[1],
        summed[2],
        summed[3],
        summed[4],
        summed[5],
        grad_router,
    )


def dot(left, right):
    return jnp.dot(left, right, preferred_element_type=F32)


def dot_nt(left, right):
    return lax.dot_general(left, right, (((1,), (1,)), ((), ())), preferred_element_type=F32)


def dot_tn(left, right):
    return lax.dot_general(left, right, (((0,), (0,)), ((), ())), preferred_element_type=F32)


class Place:
    def __init__(self, wide):
        self.ring = wide // 2
        self.length = self.ring // 2
        self.w = lax.axis_index("wide")
        self.n = lax.axis_index("narrow")
        self.c = self.w % 2
        self.q = self.w // 2
        row = self.q % 2
        col = self.q // 2
        self.r = col + row * (2 * self.length - 1 - 2 * col)

        self.around = {}
        for offset in range(-(self.ring // 2), self.ring // 2 + 1):
            pos = lax.rem(self.r + offset + self.ring, self.ring)
            row = pos // self.length
            col = pos + row * (2 * self.length - 1 - 2 * pos)
            self.around[offset] = col * 2 + row

    def chip(self, offset):
        return self.around[offset]

    def at_ring(self, offset):
        return (self.around[offset] * 2 + self.c, self.n)

    def sibling(self):
        return (self.q * 2 + 1 - self.c, self.n)

    def across(self):
        return (self.w, 1 - self.n)

    def flipped(self, bit):
        return ((self.q + bit - 2 * bit * ((self.q // bit) % 2)) * 2 + self.c, self.n)


def greet(partners):
    barrier = pltpu.get_barrier_semaphore()
    for partner in partners:
        pl.semaphore_signal(barrier, inc=1, device_id=partner, device_id_type=MESH)
    pl.semaphore_wait(barrier, len(partners))


def remote(src, dst, send, recv, device):
    return pltpu.make_async_remote_copy(
        src_ref=src, dst_ref=dst, send_sem=send, recv_sem=recv, device_id=device, device_id_type=MESH
    )


def probabilities(live, queries, keys):
    entries = queries.shape[0]
    scores = dot_nt(queries, keys) * 0.125
    q_at = lax.broadcasted_iota(jnp.int32, (entries, entries), 0)
    k_at = lax.broadcasted_iota(jnp.int32, (entries, entries), 1)
    scores = jnp.where((k_at <= q_at) & (live > 0), scores, masked_score)
    expo = jnp.exp(scores - jnp.max(scores, axis=-1, keepdims=True))
    return expo / jnp.sum(expo, axis=-1, keepdims=True)


def only(value, head):
    lane = lax.broadcasted_iota(jnp.int32, value.shape, 1)
    return jnp.where(lane // HEAD_DIM == head, value, jnp.zeros_like(value))


def gelu_pair(x):
    inner = 0.7978845608028654 * (x + 0.044715 * (x * x * x))
    bent = jnp.tanh(inner)
    half = 0.5 * (1.0 + bent)
    slope = 0.7978845608028654 * (1.0 + 0.134145 * (x * x))
    return x * half, half + 0.5 * x * (1.0 - bent * bent) * slope


def layer_kernel(
    wide,
    chunks,
    gains,
    wq,
    wo,
    wu,
    wd,
    kept,
    given,
    router,
    live,
    o_qkv,
    o_out,
    o_up,
    o_down,
    o_small,
    rows_got,
    out_low,
    grad_low,
    wq_all,
    wo_all,
    wu_all,
    wd_all,
    gains_all,
    scales,
    got,
    rows_low,
    normed,
    project,
    heads,
    attend_out,
    second_n,
    second,
    act,
    d_pre,
    mlp_out,
    d_second,
    d_mlp,
    d_attend,
    base,
    d_project,
    normed_t,
    heads_t,
    second_t,
    act_t,
    router_val,
    inverse_two,
    own,
    to_sib,
    mine,
    landed,
    moving,
    x_pre,
    x_in,
    staged,
    small_acc,
    small_in,
    own_sem,
    g_ring_send,
    g_ring_recv,
    g_sib_send,
    g_sib_recv,
    g_x_send,
    g_x_recv,
    in_send,
    in_recv,
    sib_send,
    sib_recv,
    pre_send,
    pre_recv,
    ring_send,
    ring_recv,
    x_send,
    x_recv,
    out_sem,
    small_send,
    small_recv,
    row_send,
    row_recv,
    free,
):
    at = Place(wide)
    ring, steps = at.ring, at.ring // 2
    depth, width = wo.shape
    quarter = depth // 4
    half = depth // 2
    most = depth - quarter
    entries = kept.shape[1]
    ups, downs = wu.shape[1] // width, wd.shape[0]
    tile = 256
    step = 16
    lag = LAG
    chips_of_tile = tile // (2 * depth)

    def lanes(first, size):
        return pl.ds(first if isinstance(first, int) else pl.multiple_of(first, 128), size)

    def over(size, piece_size):
        def run(piece):
            @pl.loop(0, size // piece_size)
            def _(t):
                piece(pl.multiple_of(t * piece_size, piece_size))

        return run

    def toward(d):
        return at.at_ring(1 if d == 0 else -1)

    parts = [(gains, gains_all, 0)]
    ready = {0: [0]}

    def add(name, shard, full, first, pieces=PIECES):
        for size in pieces:
            cols = pl.ds(first, size)
            parts.append((shard.at[:, cols], full.at[:, :, :, cols], size))
            if name is None:
                ready[len(parts) - 1] = [(first, size)]
            first += size
        if name is not None:
            ready[len(parts) - 1] = [name]

    for j in range(3):
        add(1 + j, wq, wq_all, j * width)
    add(4, wo, wo_all, 0)
    for j in range(downs):
        add(5 + j, wd.at[j], wd_all.at[:, :, j], 0)
    up_at = len(parts)
    for j in range(ups):
        add(None, wu, wu_all, j * width, LAST_PIECES if j == ups - 1 else PIECES)
    parts_count = len(parts)
    up_chunks = parts_count - up_at

    def window(k, s=0, d=0):
        if k == 0:
            return pl.ds(0, gains.shape[0]), pl.ds(0, gains.shape[1])
        rows = pl.ds(pl.multiple_of(at.n * quarter, quarter), most)
        if s == steps:
            return rows, pl.ds(d * (parts[k][2] // 2), parts[k][2] // 2)
        return rows, pl.ds(0, parts[k][2])

    def idle(k, s, d):
        return k == 0 and s == steps and d == 1

    def g_ring_out(k, s, d):
        pos = -(s - 1) if d == 0 else s - 1
        rows, cols = window(k, s, d)
        dst = parts[k][1].at[at.chip(pos), at.c, rows, cols]
        src = parts[k][0].at[rows, cols] if s == 1 else dst
        return remote(src, dst, g_ring_send.at[k, s - 1, d], g_ring_recv.at[k, s - 1, d], toward(d))

    def g_ring_in(k, s, d):
        pos = -s if d == 0 else s
        rows, cols = window(k, s, d)
        ref = parts[k][1].at[at.chip(pos), at.c, rows, cols]
        return remote(ref, ref, g_ring_send.at[k, s - 1, d], g_ring_recv.at[k, s - 1, d], toward(d))

    def own_copy(k):
        rows, cols = window(k)
        return pltpu.make_async_copy(
            parts[k][0].at[rows, cols], parts[k][1].at[at.q, at.c, rows, cols], own_sem.at[k]
        )

    def g_cross(k, incoming=False):
        side = 1 - at.n if incoming else at.n
        rows = pl.ds(pl.multiple_of(side * most, quarter), quarter)
        ref = parts[k][1].at[:, at.c, rows]
        return remote(ref, ref, g_x_send.at[k], g_x_recv.at[k], at.across())

    def g_sib(k, incoming=False):
        ref = parts[k][1].at[:, 1 - at.c if incoming else at.c]
        return remote(ref, ref, g_sib_send.at[k], g_sib_recv.at[k], at.sibling())

    def in_copy(j):
        return remote(given.at[j], got.at[j], in_send.at[j], in_recv.at[j], at.across())

    def turned(src, dst):
        @over(width, tile)
        def _(low):
            chips = pl.ds(low // (2 * depth), chips_of_tile)
            dst[chips] = src[:, pl.ds(low, tile)].T.reshape(chips_of_tile, 2, depth, entries)

    def normalise():
        lane = lax.broadcasted_iota(jnp.int32, (8, 2 * HEAD_DIM), 1)
        for chip in range(ring):
            pair = jnp.where(
                lane < depth, gains_all[chip, 0].astype(F32)[:8], gains_all[chip, 1].astype(F32)[:8]
            )
            scales[:, chip * 2 * depth : (chip + 1) * 2 * depth] = pair

        @over(entries, 32)
        def _(low):
            rows = pl.ds(low, 32)
            low_rows = kept[0, rows] + got[0, rows]
            value = low_rows.astype(F32)
            rows_low[rows, :] = low_rows
            inverse = lax.rsqrt(jnp.mean(value * value, axis=-1, keepdims=True) + epsilon)
            normed[rows, :] = (value * inverse * scales[0:1, :]).astype(BF16)
            router_val[rows, :] = jnp.sum(value * router[...], axis=-1, keepdims=True)

    def project_part(j):
        @over(width, tile)
        def _(low):
            cols = pl.ds(j * width + low, tile)
            weight = wq_all[:, :, :, cols].reshape(width, tile)
            project[:, cols] = dot(normed[...], weight).astype(BF16)

    def attention(first, last):
        @pl.loop(first, last)
        def _(p):
            span = 2 * HEAD_DIM
            q, k, v = [project[:, lanes(j * width + p * span, span)] for j in range(3)]
            total = jnp.zeros((entries, span), F32)
            for head in (0, 1):
                probs = probabilities(live[...], only(q, head), k)
                total = total + only(dot(probs.astype(BF16), v), head)
            heads[:, lanes(p * span, span)] = total.astype(BF16)

    def attend_project():
        @over(width, tile)
        def _(low):
            cols = pl.ds(low, tile)
            weight = wo_all[:, :, :, cols].reshape(width, tile)
            attend_out[:, cols] = dot(heads[...], weight)

        @over(entries, 32)
        def _(low):
            rows = pl.ds(low, 32)
            middle = rows_low[rows, :].astype(F32) + attend_out[rows, :]
            inverse = lax.rsqrt(jnp.mean(middle * middle, axis=-1, keepdims=True) + epsilon)
            value = middle * inverse
            second_n[rows, :] = value
            inverse_two[rows, :] = inverse
            second[rows, :] = (value * scales[1:2, :]).astype(BF16)

    def branch_grad():
        @over(entries, 32)
        def _(low):
            rows = pl.ds(low, 32)
            dout = (kept[1, rows] + got[1, rows]).astype(F32)
            d_mlp[rows, :] = (router_val[rows, :] * dout).astype(BF16)

    def up_part(first, size):
        owner = downs * depth
        for low in range(0, size, owner):
            chip, core = (first + low) // owner // 2, (first + low) // owner % 2
            cols = pl.ds(first + low, owner)
            pre = dot(second[...], wu_all[:, :, :, cols].reshape(width, owner))
            value, slope = gelu_pair(pre)
            value = value.astype(BF16)
            d_act = dot_nt(d_mlp[...], wd_all[chip, core].reshape(owner, width))
            act[:, pl.ds(low, owner)] = value
            d_pre[:, cols] = (d_act * slope).astype(BF16)
            act_t[chip, core] = value.T.reshape(downs, depth, entries)
        chip, core = first // owner // 2, first // owner % 2

        @over(width, tile)
        def _(low):
            cols = pl.ds(low, tile)
            if size == owner:
                down = wd_all[chip, core, :, :, cols]
            else:
                down = wd_all[chip, :, :, :, cols]
            part = dot(act[:, 0:size], down.reshape(size, tile))
            chips = pl.ds(low // (2 * depth), chips_of_tile)
            up = wu_all[chips, :, :, pl.ds(first, size)]
            back = dot_nt(d_pre[:, pl.ds(first, size)], up.reshape(tile, size))
            if first == 0:
                mlp_out[:, cols] = part
                d_second[:, cols] = back
            else:
                mlp_out[:, cols] += part
                d_second[:, cols] += back

    def close():
        small_acc[0] = jnp.zeros((8, width), F32)

        @over(entries, 32)
        def _(low):
            rows = pl.ds(low, 32)
            value = rows_low[rows, :].astype(F32)
            dout = (kept[1, rows] + got[1, rows]).astype(F32)
            gate = router_val[rows, :]
            branch = attend_out[rows, :] + mlp_out[rows, :]
            out_low[rows, :] = (value + gate * branch).astype(BF16)
            d_gate = jnp.sum(dout * branch, axis=-1, keepdims=True)
            normed_value = second_n[rows, :]
            back = d_second[rows, :]
            small_acc[0, 1:2, :] += jnp.sum(back * normed_value, axis=0, keepdims=True)
            small_acc[0, 2:3, :] += jnp.sum(d_gate * value, axis=0, keepdims=True)
            back = back * scales[1:2, :]
            back = inverse_two[rows, :] * (
                back - normed_value * jnp.mean(back * normed_value, axis=-1, keepdims=True)
            )
            d_attend[rows, :] = (gate * dout + back).astype(BF16)
            base[rows, :] = dout + back + d_gate * router[...]

    def heads_grad():
        @over(width, tile)
        def _(low):
            chips = pl.ds(low // (2 * depth), chips_of_tile)
            weight = wo_all[chips].reshape(tile, width)
            heads[:, pl.ds(low, tile)] = dot_nt(d_attend[...], weight).astype(BF16)

    def attention_back(first, last):
        span = 2 * HEAD_DIM

        @pl.loop(first, last)
        def _(p):
            places = [lanes(j * width + p * span, span) for j in range(3)]
            q, k, v = [project[:, place] for place in places]
            d_pair = heads[:, places[0]]
            d_q = jnp.zeros((entries, span), F32)
            d_k = jnp.zeros((entries, span), F32)
            d_v = jnp.zeros((entries, span), F32)
            for head in (0, 1):
                probs = probabilities(live[...], only(q, head), k)
                d_own = only(d_pair, head)
                d_probs = dot_nt(d_own, v)
                d_scores = probs * (d_probs - jnp.sum(probs * d_probs, axis=-1, keepdims=True))
                d_scores = d_scores.astype(BF16)
                d_q = d_q + only(dot(d_scores, k), head)
                d_k = d_k + only(dot_tn(d_scores, q), head)
                d_v = d_v + dot_tn(probs.astype(BF16), d_own)
            d_project[:, places[0]] = (d_q * 0.125).astype(BF16)
            d_project[:, places[1]] = (d_k * 0.125).astype(BF16)
            d_project[:, places[2]] = d_v.astype(BF16)

    def normed_grad(j):
        @over(width, tile)
        def _(low):
            chips = pl.ds(low // (2 * depth), chips_of_tile)
            weight = wq_all[chips, :, :, pl.ds(j * width, width)].reshape(tile, width)
            part = dot_nt(d_project[:, pl.ds(j * width, width)], weight)
            cols = pl.ds(low, tile)
            if j == 0:
                d_second[:, cols] = part
            else:
                d_second[:, cols] += part

    def finish():
        @over(entries, 32)
        def _(low):
            rows = pl.ds(low, 32)
            value = rows_low[rows, :].astype(F32)
            inverse = lax.rsqrt(jnp.mean(value * value, axis=-1, keepdims=True) + epsilon)
            value = value * inverse
            back = d_second[rows, :]
            small_acc[0, 0:1, :] += jnp.sum(back * value, axis=0, keepdims=True)
            back = back * scales[0:1, :]
            back = inverse * (back - value * jnp.mean(back * value, axis=-1, keepdims=True))
            grad_low[rows, :] = (base[rows, :] + back).astype(BF16)

    count = len(chunks)
    reused = [k for k in range(count) if chunks[k].panel >= ups]

    def spread(k, first, size):
        return lanes(chunks[k].panel * width + chunks[k].off + first, size)

    def sums(k, chip, rows, first, size):
        c = chunks[k]
        if c.panel < ups:
            return mine.at[chip, rows, spread(k, first, size)]
        p = c.panel - ups
        return wd_all.at[chip, p // downs, p % downs, rows, lanes(c.off + first, size)]

    def passing(k, t, d, rows, first, size):
        c = chunks[k]
        if c.panel < ups:
            if t == 0:
                return landed.at[d, rows, spread(k, first, size)]
            return moving.at[t - 1, d, rows, spread(k, first, size)]
        p = c.panel - ups
        cols = lanes(p % ups * width + c.off + first, size)
        slab = 12 + p // ups if t == 0 else p // ups * 6 + (t - 1) * 2 + d
        if t == 0:
            rows = pl.ds(d * half + rows.start, rows.size)
        return wu_all.at[slab // 2, slab % 2, rows, cols]

    every = pl.ds(0, depth)

    def ride(k):
        return chunks[k].give * at.n if chunks[k].give else 0, chunks[k].size - chunks[k].give

    def product(k, core, put):
        c = chunks[k]
        if c.kind == "down":
            left, right = act_t[:, core, c.j], d_mlp
        else:
            tall, right = {
                "up": (second_t, d_pre),
                "out": (heads_t, d_attend),
                "qkv": (normed_t, d_project),
            }[c.kind]
            left = tall[:, core]
        left = left.reshape(ring * depth, entries)

        @pl.loop(0, c.size // tile)
        def _(t):
            cols = pl.ds(pl.multiple_of(t * tile, tile), tile)
            take = pl.ds(pl.multiple_of(c.first + t * tile, tile), tile)
            put(cols, dot(left, right[:, take]).reshape(ring, depth, tile))

    def out_copy(k):
        c = chunks[k]
        out = {"up": o_up, "down": o_down, "out": o_out, "qkv": o_qkv}[c.kind]
        rows = pl.ds(c.j * depth if c.kind == "down" else 0, depth)
        return pltpu.make_async_copy(
            staged.at[k % 2, :, pl.ds(0, c.size)], out.at[rows, pl.ds(c.first, c.size)], out_sem.at[k]
        )

    def sib(k):
        src = to_sib.at[k % 2, :, :, pl.ds(0, chunks[k].size)]
        dst = sums(k, slice(None), slice(None), 0, chunks[k].size)
        return remote(src, dst, sib_send.at[k], sib_recv.at[k], at.sibling())

    def pre(k):
        c = chunks[k]
        src = sums(k, slice(None), slice(None), (c.size - c.give) * (1 - at.n), c.give)
        dst = x_pre.at[:, :, lanes(c.given_at, c.give)]
        return remote(src, dst, pre_send.at[k], pre_recv.at[k], at.across())

    def dest(t, d):
        return at.chip(steps - t if d == 0 else t - steps)

    def ring_out(k, t, d):
        rows = pl.ds(d * half, half) if t == 0 else every
        src = sums(k, dest(t, d), rows, *ride(k))
        land = passing(k, t, d, pl.ds(0, half) if t == 0 else every, *ride(k))
        return remote(src, land, ring_send.at[k, t, d], ring_recv.at[k, t, d], toward(d))

    def cross(k):
        first, size = ride(k)
        dst = x_in.at[:, lanes(chunks[k].start + first, size)]
        return remote(sums(k, at.q, every, first, size), dst, x_send.at[k], x_recv.at[k], at.across())

    bits = [1 << b for b in range(ring.bit_length() - 1)]
    partners = [at.sibling(), at.across()] + [at.flipped(bit) for bit in bits]
    stages = len(partners)

    def small_copy(j):
        return remote(
            small_acc.at[j], small_in.at[j], small_send.at[j], small_recv.at[j], partners[j]
        )

    def row_copy(j, p):
        rows = pl.ds(p * (entries // ROW_PIECES), entries // ROW_PIECES)
        src = out_low if j == 0 else grad_low
        return remote(
            src.at[rows], rows_got.at[j, rows], row_send.at[j, p], row_recv.at[j, p], at.across()
        )

    def release():
        for k in range(parts_count):
            g_sib(k).wait_send()
            if k > 0:
                g_cross(k).wait_send()
            for s in range(1, steps + 1):
                for d in (0, 1):
                    if not idle(k, s, d):
                        g_ring_out(k, s, d).wait_send()
        for j, device in enumerate((at.at_ring(-1), at.at_ring(1), at.sibling())):
            pl.semaphore_signal(free.at[j], inc=1, device_id=device, device_id_type=MESH)

    pairs = width // (2 * HEAD_DIM)
    cuts = [pairs * j // 8 for j in (0, 2, 5, 8)]
    work = {
        0: [normalise, lambda: turned(normed, normed_t)],
        1: [lambda: project_part(0)],
        2: [lambda: project_part(1)],
        3: [lambda: project_part(2), lambda: attention(cuts[0], cuts[1])],
        4: [lambda: attention(cuts[1], cuts[2])],
        5: [lambda: attention(cuts[2], cuts[3]), attend_project],
        6: [lambda: turned(heads, heads_t), lambda: turned(second, second_t)],
        7: [branch_grad],
    }
    back_cuts = [pairs * j // 4 for j in range(5)]
    back_work = [heads_grad]
    back_work += [functools.partial(attention_back, back_cuts[j], back_cuts[j + 1]) for j in range(4)]
    back_work += [functools.partial(normed_grad, j) for j in range(3)]
    back_work += [finish]

    def gather_turn(i):
        if i < parts_count:
            for d in (0, 1):
                g_ring_out(i, 1, d).start()
            own_copy(i).start()
        if i == 2:
            in_copy(1).start()
        for s in range(1, steps + 1):
            k = i - lag * s
            if 0 <= k < parts_count:
                for d in (0, 1):
                    if not idle(k, s, d):
                        g_ring_in(k, s, d).wait_recv()
                    if s < steps and not idle(k, s + 1, d):
                        g_ring_out(k, s + 1, d).start()
                if s == steps:
                    own_copy(k).wait()
                    if k > 0:
                        g_cross(k).start()
        k = i - lag * (steps + 1)
        if 0 <= k < parts_count:
            if k > 0:
                g_cross(k, True).wait_recv()
            g_sib(k).start()
        k = i - lag * (steps + 1) - 1
        if 0 <= k < parts_count:
            g_sib(k, True).wait_recv()
            if k == 0:
                for j in (0, 1):
                    in_copy(j).wait_recv()
            for piece in ready.get(k, ()):
                if isinstance(piece, int):
                    for job in work.get(piece, ()):
                        job()
                else:
                    up_part(*piece)

    ring_at = 1 + lag
    work_at = up_chunks
    small_at = work_at + len(back_work)

    def reduce_turn(i):
        k = i - ring_at - lag * steps - lag
        if 0 <= k < count:
            c = chunks[k]
            cross(k).wait_recv()
            if k >= 2:
                out_copy(k - 2).wait()
            inner = c.size - 2 * c.give

            @over(depth, step)
            def _(row):
                rows = pl.ds(row, step)

                def mixed(first, size):
                    return sums(k, at.q, rows, first, size)[...].astype(F32), x_in[
                        rows, lanes(c.start + first, size)
                    ].astype(F32)

                here, there = mixed(c.give, inner)
                staged[k % 2, rows, c.give : c.give + inner] = here + there
                if c.give:
                    alone = (c.size - c.give) * at.n
                    staged[k % 2, rows, lanes(alone, c.give)] = mixed(alone, c.give)[0]
                    alone = (c.size - c.give) * (1 - at.n)
                    staged[k % 2, rows, lanes(alone, c.give)] = mixed(alone, c.give)[1]

            out_copy(k).start()
        k = i - ring_at - lag * steps
        if 0 <= k < count:
            for d in (0, 1):
                land = passing(k, steps - 1, d, every, *ride(k))
                remote(
                    land,
                    land,
                    ring_send.at[k, steps - 1, d],
                    ring_recv.at[k, steps - 1, d],
                    toward(d),
                ).wait_recv()

            @over(depth, step)
            def _(row):
                rows = pl.ds(row, step)
                total = sums(k, at.q, rows, *ride(k))
                value = total[...].astype(F32)
                for d in (0, 1):
                    value = value + passing(k, steps - 1, d, rows, *ride(k))[...].astype(F32)
                total[...] = value.astype(BF16)

            cross(k).start()
        for t in range(steps - 1, 0, -1):
            k = i - ring_at - lag * t
            if 0 <= k < count:
                for d in (0, 1):
                    size = half if t == 1 else depth
                    land = passing(k, t - 1, d, pl.ds(0, size), *ride(k))
                    remote(
                        land, land, ring_send.at[k, t - 1, d], ring_recv.at[k, t - 1, d], toward(d)
                    ).wait_recv()
                    to = dest(t, d)
                    low = d * half if t == 1 else 0

                    @over(size, step)
                    def _(row):
                        total = sums(k, to, pl.ds(low + row, step), *ride(k))
                        came = passing(k, t - 1, d, pl.ds(row, step), *ride(k))
                        value = total[...].astype(F32) + came[...].astype(F32)
                        total[...] = value.astype(BF16)

                    ring_out(k, t, d).start()
        k = i - ring_at
        if 0 <= k < count:
            c = chunks[k]
            if c.give > 0:
                pre(k).wait_recv()
                alone = (c.size - c.give) * at.n

                @pl.loop(0, ring)
                def _(chip):
                    total = sums(k, chip, every, alone, c.give)
                    came = x_pre[chip, :, lanes(c.given_at, c.give)]
                    total[...] = (total[...].astype(F32) + came.astype(F32)).astype(BF16)

            for d in (0, 1):
                if k == reused[0]:
                    pl.semaphore_wait(free.at[d], 1)
                ring_out(k, 0, d).start()
        k = i - 1
        if 0 <= k < count:
            c = chunks[k]
            all_sums = sums(k, slice(None), slice(None), 0, c.size)
            remote(all_sums, all_sums, sib_send.at[k], sib_recv.at[k], at.sibling()).wait_recv()

            @pl.loop(0, ring)
            def _(chip):
                total = sums(k, chip, every, 0, c.size)
                total[...] = (total[...].astype(F32) + own[chip, :, 0 : c.size]).astype(BF16)

            if c.give > 0:
                pre(k).start()
        k = i
        if 0 <= k < count:
            if k >= 2:
                sib(k - 2).wait_send()

            def keep_other(cols, value):
                to_sib[k % 2, :, :, cols] = value.astype(BF16)

            def keep_own(cols, value):
                own[:, :, cols] = value

            product(k, 1 - at.c, keep_other)
            if k == reused[0]:
                pl.semaphore_wait(free.at[2], 1)
            sib(k).start()
            product(k, at.c, keep_own)
        j = i - work_at
        if 0 <= j < len(back_work):
            back_work[j]()
        if 0 <= j < ROW_PIECES:
            row_copy(0, j).start()
        p = i - small_at
        if 0 <= p < ROW_PIECES:
            row_copy(1, p).start()
        j = i - small_at
        if 0 <= j <= stages:
            if j > 0:
                small_copy(j - 1).wait_recv()
                small_acc[j] = small_acc[j - 1] + small_in[j - 1]
            if j < stages:
                small_copy(j).start()
            else:
                o_small[...] = small_acc[stages]

    greet(partners + [at.at_ring(1), at.at_ring(-1)])
    in_copy(0).start()
    offset = up_at + lag * (steps + 1) + 1
    for i in range(offset + count + ring_at + lag * steps + lag + 1):
        gather_turn(i)
        if i == offset + up_chunks - 1:
            release()
            close()
        reduce_turn(i - offset)

    for j in (0, 1):
        in_copy(j).wait_send()
    for k in range(count):
        if k >= count - 2:
            sib(k).wait_send()
            out_copy(k).wait()
        if chunks[k].give > 0:
            pre(k).wait_send()
        cross(k).wait_send()
        for t in range(steps):
            for d in (0, 1):
                ring_out(k, t, d).wait_send()
    for j in range(stages):
        small_copy(j).wait_send()
    for j in (0, 1):
        for p in range(ROW_PIECES):
            row_copy(j, p).wait()


class Chunk(NamedTuple):
    kind: str
    j: int
    first: int
    size: int
    panel: int
    off: int
    start: int
    give: int
    given_at: int


def cut_chunks(width, ff):
    panels = [("up", j, j * width) for j in range(ff // width)]
    panels += [("down", j, 0) for j in range(ff // width)]
    panels += [("out", 0, 0)] + [("qkv", j, j * width) for j in range(3)]
    plain = []
    for panel, (kind, j, first) in enumerate(panels):
        off = 0
        last = panel in (ff // width - 1, len(panels) - 1)
        for size in LAST_PIECES if last else PIECES:
            plain.append((kind, j, first + off, size, panel, off))
            off += size
    chunks, start, given = [], 0, 0
    for k, piece in enumerate(plain):
        inside = GIVE_SKIP[0] <= k < len(plain) - GIVE_SKIP[1]
        give = GIVE if inside and piece[3] == 512 else 0
        chunks.append(Chunk(*piece, start, give, given))
        start += piece[3]
        given += give
    return tuple(chunks), start, given


def layer(wide, gains, wq, wo, wu, wd, kept, given, router, live):
    depth, width = wo.shape
    ring, steps = wide // 2, wide // 4
    entries = kept.shape[1]
    ff = wu.shape[1]
    ups = downs = ff // width
    chunks, columns, given_columns = cut_chunks(width, ff)
    parts = 1 + (3 + downs + ups) * len(PIECES) + len(LAST_PIECES)
    count = len(chunks)
    stages = 2 + (ring.bit_length() - 1)
    in_vmem = pl.BlockSpec(memory_space=pltpu.VMEM)
    anywhere = pl.BlockSpec(memory_space=pl.ANY)
    dma = pltpu.SemaphoreType.DMA
    vmem = pltpu.VMEM
    shape = jax.ShapeDtypeStruct
    tall = (ring, 2, depth, entries)
    square = (entries, width)
    return pl.pallas_call(
        functools.partial(layer_kernel, wide, chunks),
        out_shape=[
            shape((depth, 3 * width), F32),
            shape((depth, width), F32),
            shape((depth, ff), F32),
            shape((ff // wide, width), F32),
            shape((8, width), F32),
            shape((2, entries, width), BF16),
            shape(square, BF16),
            shape(square, BF16),
        ],
        in_specs=[anywhere] * 5 + [in_vmem, anywhere, in_vmem, in_vmem],
        out_specs=[anywhere] * 4 + [in_vmem, anywhere, in_vmem, in_vmem],
        scratch_shapes=[
            vmem((ring, 2, depth, 3 * width), BF16),
            vmem((ring, 2, depth, width), BF16),
            vmem((ring, 2, depth, ff), BF16),
            vmem((ring, 2, downs, depth, width), BF16),
            vmem((ring, 2) + gains.shape, BF16),
            vmem((8, width), F32),
            vmem((2,) + square, BF16),
            vmem(square, BF16),
            vmem(square, BF16),
            vmem((entries, 3 * width), BF16),
            vmem(square, BF16),
            vmem(square, F32),
            vmem(square, F32),
            vmem(square, BF16),
            vmem((entries, 512), BF16),
            vmem((entries, ff), BF16),
            vmem(square, F32),
            vmem(square, F32),
            vmem(square, BF16),
            vmem(square, BF16),
            vmem(square, F32),
            vmem((entries, 3 * width), BF16),
            vmem(tall, BF16),
            vmem(tall, BF16),
            vmem(tall, BF16),
            vmem((ring, 2, downs, depth, entries), BF16),
            vmem((entries, 1), F32),
            vmem((entries, 1), F32),
            vmem((ring, depth, 512), F32),
            vmem((2, ring, depth, 512), BF16),
            vmem((ring, depth, ups * width), BF16),
            vmem((2, depth // 2, ups * width), BF16),
            vmem((steps - 1, 2, depth, ups * width), BF16),
            vmem((ring, depth, max(given_columns, 128)), BF16),
            vmem((depth, columns), BF16),
            vmem((2, depth, 512), F32),
            vmem((stages + 1, 8, width), F32),
            vmem((stages, 8, width), F32),
            dma((parts,)),
            dma((parts, steps, 2)),
            dma((parts, steps, 2)),
            dma((parts,)),
            dma((parts,)),
            dma((parts,)),
            dma((parts,)),
            dma((2,)),
            dma((2,)),
            dma((count,)),
            dma((count,)),
            dma((count,)),
            dma((count,)),
            dma((count, steps, 2)),
            dma((count, steps, 2)),
            dma((count,)),
            dma((count,)),
            dma((count,)),
            dma((stages,)),
            dma((stages,)),
            dma((2, ROW_PIECES)),
            dma((2, ROW_PIECES)),
            pltpu.SemaphoreType.REGULAR((3,)),
        ],
        compiler_params=pltpu.CompilerParams(
            collective_id=1, has_side_effects=True, vmem_limit_bytes=63 * 1024 * 1024
        ),
        name="layer",
    )(gains, wq, wo, wu, wd.reshape(downs, depth, width), kept, given, router, live)


def paired_body(
    wide, tokens, cotangent, lengths, routes, w_qkv, w_out, w_up, w_down, gain_attn, gain_mlp, router
):
    place = lax.axis_index("narrow")
    seqs, span, width = tokens.shape
    list_len = routes.shape[1]
    depth = gain_attn.shape[0]
    counts = lengths // 8
    entry = jnp.arange(list_len, dtype=jnp.int32)
    live = entry[None, :] < counts[:, None]
    local_slot = jnp.where(live, routes - place * span, -1)
    spots = jnp.arange(span, dtype=jnp.int32)
    chosen = (local_slot[:, :, None] == spots[None, None, :]).astype(BF16)

    def take(source):
        return jnp.einsum("sep,spd->sed", chosen, source, preferred_element_type=F32).astype(BF16)

    picked = jnp.stack([take(tokens), take(cotangent)])
    kept = lax.dynamic_index_in_dim(picked, place, 1, keepdims=False)
    given = lax.dynamic_index_in_dim(picked, 1 - place, 1, keepdims=False)
    gains = jnp.stack(
        [jnp.concatenate([gain_attn, gain_attn]), jnp.concatenate([gain_mlp, gain_mlp])]
    )
    gains = jnp.pad(gains, ((0, 14), (0, 0)))
    router_row = router.astype(F32)[None, :]
    live_row = lax.dynamic_index_in_dim(live, place, 0, keepdims=True).astype(jnp.int32)
    grad_qkv, grad_out, grad_up, grad_down, small, back_got, out_low, grad_low = layer(
        wide, gains, w_qkv, w_out, w_up, w_down, kept, given, router_row, live_row
    )
    back = jnp.stack([out_low, grad_low])
    first = place == 0
    rows_out = jnp.stack([jnp.where(first, back, back_got), jnp.where(first, back_got, back)], axis=1)
    hit = jnp.any(local_slot[:, :, None] == spots[None, None, :], axis=1)

    def put(base, fresh):
        spread = jnp.einsum("sep,sed->spd", chosen, fresh, preferred_element_type=F32)
        return jnp.where(hit[:, :, None], spread.astype(BF16), base)

    start = lax.axis_index("wide") * depth
    return (
        put(tokens, rows_out[0]),
        put(cotangent, rows_out[1]),
        grad_qkv,
        grad_out,
        grad_up,
        grad_down,
        lax.dynamic_slice_in_dim(small[0], start, depth),
        lax.dynamic_slice_in_dim(small[1], start, depth),
        small[2],
    )


def body(wide, narrow, tokens, *others):
    if narrow == 2 and tokens.shape[0] == 2 and wide == 16:
        return paired_body(wide, tokens, *others)
    return general_body(tokens, *others)


def solution(mesh):
    in_specs = (
        P("wide", "narrow", None),
        P("wide", "narrow", None),
        P("wide"),
        P("wide", None),
        P("wide", None),
        P("wide", None),
        P("wide", None),
        P("wide", None),
        P("wide"),
        P("wide"),
        P(),
    )
    out_specs = (
        P("wide", "narrow", None),
        P("wide", "narrow", None),
        P("wide", None),
        P("wide", None),
        P("wide", None),
        P("wide", None),
        P("wide"),
        P("wide"),
        P(),
    )
    sizes = mesh.shape["wide"], mesh.shape["narrow"]
    return jax.shard_map(functools.partial(body, *sizes), mesh=mesh, in_specs=in_specs, out_specs=out_specs, check_vma=False)
```

```python
import functools
from typing import NamedTuple

import jax
import jax.numpy as jnp
from jax import lax
from jax.experimental import pallas as pl
from jax.experimental.pallas import tpu as pltpu
from jax.sharding import PartitionSpec as P

HEAD_DIM = 64
MESH = pl.DeviceIdType.MESH
F32 = jnp.float32
BF16 = jnp.bfloat16
LAG = 2
LEAD = 6
ROWS_AT = 20
PICK_AT = (0, 3)
PIECES = (512, 512)
LAST_PIECES = (512, 256, 256)
GIVE = 128
GIVE_SKIP = (3, 6)
ROW_PIECES = 8

epsilon = 1e-06
masked_score = -1e30


def rms_parts(values):
    inverse = lax.rsqrt(jnp.mean(values * values, axis=-1, keepdims=True) + epsilon)
    return (values * inverse, inverse)


def rms_back(grad_normed, normed, inverse):
    return inverse * (grad_normed - normed * jnp.mean(grad_normed * normed, axis=-1, keepdims=True))


def attend_scores(queries, keys_all, allowed):
    scores = (
        jnp.einsum("sqhe,skhe->shqk", queries, keys_all, preferred_element_type=jnp.float32) * 0.125
    )
    return jnp.where(allowed, scores, masked_score)


def attend_forward(queries, keys_all, values_all, allowed):
    scores = attend_scores(queries, keys_all, allowed)
    top_score = jnp.max(scores, axis=-1, keepdims=True)
    expo = jnp.exp(scores - top_score)
    total = jnp.sum(expo, axis=-1, keepdims=True)
    log_total = top_score + jnp.log(total)
    probs_low = (expo / total).astype(jnp.bfloat16)
    heads_out = jnp.einsum(
        "shqk,skhe->sqhe", probs_low, values_all, preferred_element_type=jnp.float32
    )
    return (heads_out, log_total)


def attend_backward(queries, keys_all, values_all, allowed, log_total, d_heads):
    probs_again = jnp.exp(attend_scores(queries, keys_all, allowed) - log_total)
    d_probs = jnp.einsum("sqhe,skhe->shqk", d_heads, values_all, preferred_element_type=jnp.float32)
    row_dot = jnp.sum(probs_again * d_probs, axis=-1, keepdims=True)
    d_scores = (probs_again * (d_probs - row_dot)).astype(jnp.bfloat16)
    d_queries = (
        jnp.einsum("shqk,skhe->sqhe", d_scores, keys_all, preferred_element_type=jnp.float32)
        * 0.125
    )
    d_key_part = (
        jnp.einsum("shqk,sqhe->skhe", d_scores, queries, preferred_element_type=jnp.float32) * 0.125
    )
    d_value_part = jnp.einsum(
        "shqk,sqhe->skhe",
        probs_again.astype(jnp.bfloat16),
        d_heads,
        preferred_element_type=jnp.float32,
    )
    return (d_queries, d_key_part, d_value_part)


def general_body(
    tokens, cotangent, lengths, routes, w_qkv, w_out, w_up, w_down, gain_attn, gain_mlp, router
):
    parts_narrow = lax.axis_size("narrow")
    place = lax.axis_index("narrow")
    seqs, span, width = tokens.shape
    list_len = routes.shape[1]
    own_entries = list_len // parts_narrow
    rows_total = seqs * own_entries
    counts = lengths // 8
    entry = jnp.arange(list_len, dtype=jnp.int32)
    live = entry[None, :] < counts[:, None]
    local_slot = routes - place * span
    mine = live & (local_slot >= 0) & (local_slot < span)
    pick = jnp.clip(local_slot, 0, span - 1)
    keep = mine[:, :, None]
    taken_in = jnp.take_along_axis(tokens, pick[:, :, None], axis=1)
    taken_cot = jnp.take_along_axis(cotangent, pick[:, :, None], axis=1)
    blank = jnp.zeros_like(taken_in)
    rows_in, rows_cot = (
        lax.psum_scatter(
            jnp.where(keep, taken_in, blank), "narrow", scatter_dimension=1, tiled=True
        ).astype(jnp.float32),
        lax.psum_scatter(
            jnp.where(keep, taken_cot, blank), "narrow", scatter_dimension=1, tiled=True
        ).astype(jnp.float32),
    )
    inputs_rows = rows_in.reshape(rows_total, width)
    inputs_low = inputs_rows.astype(jnp.bfloat16)
    dout = rows_cot.reshape(rows_total, width)
    gathered = (
        lax.all_gather(w_qkv, "wide", axis=0, tiled=True),
        lax.all_gather(w_out, "wide", axis=0, tiled=True),
        lax.all_gather(w_up, "wide", axis=0, tiled=True),
        lax.all_gather(w_down, "wide", axis=0, tiled=True),
        lax.all_gather(gain_attn, "wide", axis=0, tiled=True),
        lax.all_gather(gain_mlp, "wide", axis=0, tiled=True),
    )
    weight_qkv, weight_out, weight_up, weight_down, gain_first, gain_second = gathered
    scale_first = gain_first.astype(jnp.float32)
    scale_second = gain_second.astype(jnp.float32)
    normed_one, inverse_one = rms_parts(inputs_rows)
    normed_low = (normed_one * scale_first).astype(jnp.bfloat16)
    project = jnp.dot(normed_low, weight_qkv, preferred_element_type=jnp.float32).astype(
        jnp.bfloat16
    )
    queries = project[:, :width].reshape(seqs, own_entries, -1, HEAD_DIM)
    key_own = project[:, width : 2 * width].reshape(seqs, own_entries, width)
    value_own = project[:, 2 * width :].reshape(seqs, own_entries, width)
    keys_all, values_all = (
        lax.all_gather(key_own, "narrow", axis=1, tiled=True),
        lax.all_gather(value_own, "narrow", axis=1, tiled=True),
    )
    keys_all = keys_all.reshape(seqs, list_len, -1, HEAD_DIM)
    values_all = values_all.reshape(seqs, list_len, -1, HEAD_DIM)
    query_pos = place * own_entries + jnp.arange(own_entries, dtype=jnp.int32)
    allowed = (entry[None, None, None, :] <= query_pos[None, None, :, None]) & (
        entry[None, None, None, :] < counts[:, None, None, None]
    )
    heads_out, log_total = attend_forward(queries, keys_all, values_all, allowed)
    heads_low = heads_out.reshape(rows_total, width).astype(jnp.bfloat16)
    attend_out = jnp.dot(heads_low, weight_out, preferred_element_type=jnp.float32)
    middle = inputs_rows + attend_out
    normed_two, inverse_two = rms_parts(middle)
    second_low = (normed_two * scale_second).astype(jnp.bfloat16)
    pre_act = jnp.dot(second_low, weight_up, preferred_element_type=jnp.float32)
    activ_full, gelu_back = jax.vjp(jax.nn.gelu, pre_act)
    activ_low = activ_full.astype(jnp.bfloat16)
    mlp_out = jnp.dot(activ_low, weight_down, preferred_element_type=jnp.float32)
    branch = attend_out + mlp_out
    router_val = jnp.dot(inputs_low, router, preferred_element_type=jnp.float32)
    out_low = (inputs_rows + router_val[:, None] * branch).astype(jnp.bfloat16)
    back_set = (
        lax.all_gather(w_qkv, "wide", axis=0, tiled=True),
        lax.all_gather(w_out, "wide", axis=0, tiled=True),
        lax.all_gather(w_up, "wide", axis=0, tiled=True),
        lax.all_gather(w_down, "wide", axis=0, tiled=True),
        lax.all_gather(gain_attn, "wide", axis=0, tiled=True),
        lax.all_gather(gain_mlp, "wide", axis=0, tiled=True),
    )
    back_qkv, back_out, back_up, back_down, back_gain_a, back_gain_m = back_set
    back_first = back_gain_a.astype(jnp.float32)
    back_second = back_gain_m.astype(jnp.float32)
    d_branch = router_val[:, None] * dout
    d_router_val = jnp.sum(dout * branch, axis=-1)
    d_mlp = d_branch.astype(jnp.bfloat16)
    grad_down_full = jnp.einsum("rf,rd->fd", activ_low, d_mlp, preferred_element_type=jnp.float32)
    d_act = jnp.einsum("rd,fd->rf", d_mlp, back_down, preferred_element_type=jnp.float32)
    d_pre = gelu_back(d_act)[0].astype(jnp.bfloat16)
    grad_up_full = jnp.einsum("rd,rf->df", second_low, d_pre, preferred_element_type=jnp.float32)
    d_normed_two = jnp.einsum("rf,df->rd", d_pre, back_up, preferred_element_type=jnp.float32)
    grad_gain_two = jnp.sum(d_normed_two * normed_two, axis=0)
    d_middle = rms_back(d_normed_two * back_second, normed_two, inverse_two)
    d_attend = (d_branch + d_middle).astype(jnp.bfloat16)
    grad_out_full = jnp.einsum("rd,re->de", heads_low, d_attend, preferred_element_type=jnp.float32)
    d_heads = jnp.einsum(
        "re,de->rd", d_attend, back_out, preferred_element_type=jnp.float32
    ).astype(jnp.bfloat16)
    d_heads_own = d_heads.reshape(seqs, own_entries, -1, HEAD_DIM)
    d_queries, d_key_part, d_value_part = attend_backward(
        queries, keys_all, values_all, allowed, log_total, d_heads_own
    )
    d_key_own, d_value_own = (
        lax.psum_scatter(
            d_key_part.reshape(seqs, list_len, width), "narrow", scatter_dimension=1, tiled=True
        ),
        lax.psum_scatter(
            d_value_part.reshape(seqs, list_len, width), "narrow", scatter_dimension=1, tiled=True
        ),
    )
    d_project = jnp.concatenate(
        [
            d_queries.reshape(rows_total, width),
            d_key_own.reshape(rows_total, width),
            d_value_own.reshape(rows_total, width),
        ],
        axis=-1,
    ).astype(jnp.bfloat16)
    grad_qkv_full = jnp.einsum(
        "rd,re->de", normed_low, d_project, preferred_element_type=jnp.float32
    )
    d_normed = jnp.einsum("re,de->rd", d_project, back_qkv, preferred_element_type=jnp.float32)
    grad_gain_one = jnp.sum(d_normed * normed_one, axis=0)
    d_norm_rows = rms_back(d_normed * back_first, normed_one, inverse_one)
    d_rows = dout + d_middle + d_norm_rows + d_router_val[:, None] * router.astype(jnp.float32)
    grad_router_part = jnp.dot(d_router_val, inputs_rows, precision=lax.Precision.HIGHEST)
    grad_low = d_rows.astype(jnp.bfloat16)
    out_all, grad_all = (
        lax.all_gather(out_low.reshape(seqs, own_entries, width), "narrow", axis=1, tiled=True),
        lax.all_gather(grad_low.reshape(seqs, own_entries, width), "narrow", axis=1, tiled=True),
    )
    target = jnp.where(mine, pick, span)
    put = jax.vmap(lambda base, where_to, fresh: base.at[where_to].set(fresh, mode="drop"))
    mixed = put(tokens, target, out_all)
    grad_tokens = put(cotangent, target, grad_all)
    shards = (
        lax.psum_scatter(grad_qkv_full, "wide", scatter_dimension=0, tiled=True),
        lax.psum_scatter(grad_out_full, "wide", scatter_dimension=0, tiled=True),
        lax.psum_scatter(grad_up_full, "wide", scatter_dimension=0, tiled=True),
        lax.psum_scatter(grad_down_full, "wide", scatter_dimension=0, tiled=True),
        lax.psum_scatter(grad_gain_one, "wide", scatter_dimension=0, tiled=True),
        lax.psum_scatter(grad_gain_two, "wide", scatter_dimension=0, tiled=True),
    )
    summed = lax.psum((shards[0], shards[1], shards[2], shards[3], shards[4], shards[5]), "narrow")
    grad_router = lax.psum(grad_router_part, ("wide", "narrow"))
    return (
        mixed,
        grad_tokens,
        summed[0],
        summed[1],
        summed[2],
        summed[3],
        summed[4],
        summed[5],
        grad_router,
    )


def dot(left, right):
    return jnp.dot(left, right, preferred_element_type=F32)


def dot_nt(left, right):
    return lax.dot_general(left, right, (((1,), (1,)), ((), ())), preferred_element_type=F32)


def dot_tn(left, right):
    return lax.dot_general(left, right, (((0,), (0,)), ((), ())), preferred_element_type=F32)


class Place:
    def __init__(self, wide):
        self.ring = wide // 2
        self.length = self.ring // 2
        self.w = lax.axis_index("wide")
        self.n = lax.axis_index("narrow")
        self.c = self.w % 2
        self.q = self.w // 2
        row = self.q % 2
        col = self.q // 2
        self.r = col + row * (2 * self.length - 1 - 2 * col)

        self.around = {}
        for offset in range(-(self.ring // 2), self.ring // 2 + 1):
            pos = lax.rem(self.r + offset + self.ring, self.ring)
            row = pos // self.length
            col = pos + row * (2 * self.length - 1 - 2 * pos)
            self.around[offset] = col * 2 + row

    def chip(self, offset):
        return self.around[offset]

    def at_ring(self, offset):
        return (self.around[offset] * 2 + self.c, self.n)

    def sibling(self):
        return (self.q * 2 + 1 - self.c, self.n)

    def across(self):
        return (self.w, 1 - self.n)

    def flipped(self, bit):
        return ((self.q + bit - 2 * bit * ((self.q // bit) % 2)) * 2 + self.c, self.n)


def greet(partners):
    barrier = pltpu.get_barrier_semaphore()
    for partner in partners:
        pl.semaphore_signal(barrier, inc=1, device_id=partner, device_id_type=MESH)
    pl.semaphore_wait(barrier, len(partners))


def remote(src, dst, send, recv, device):
    return pltpu.make_async_remote_copy(
        src_ref=src, dst_ref=dst, send_sem=send, recv_sem=recv, device_id=device, device_id_type=MESH
    )


def probabilities(live, queries, keys):
    entries = queries.shape[0]
    scores = dot_nt(queries, keys) * 0.125
    q_at = lax.broadcasted_iota(jnp.int32, (entries, entries), 0)
    k_at = lax.broadcasted_iota(jnp.int32, (entries, entries), 1)
    scores = jnp.where((k_at <= q_at) & (live > 0), scores, masked_score)
    expo = jnp.exp(scores - jnp.max(scores, axis=-1, keepdims=True))
    return expo / jnp.sum(expo, axis=-1, keepdims=True)


def only(value, head):
    lane = lax.broadcasted_iota(jnp.int32, value.shape, 1)
    return jnp.where(lane // HEAD_DIM == head, value, jnp.zeros_like(value))


def gelu_pair(x):
    inner = 0.7978845608028654 * (x + 0.044715 * (x * x * x))
    bent = jnp.tanh(inner)
    half = 0.5 * (1.0 + bent)
    slope = 0.7978845608028654 * (1.0 + 0.134145 * (x * x))
    return x * half, half + 0.5 * x * (1.0 - bent * bent) * slope


def layer_kernel(
    wide,
    chunks,
    gains,
    wq,
    wo,
    wu,
    wd,
    tokens,
    cotangent,
    slots,
    router,
    live,
    o_qkv,
    o_out,
    o_up,
    o_down,
    o_small,
    rows_all,
    wq_all,
    wo_all,
    wu_all,
    wd_all,
    gains_all,
    scales,
    kept,
    given,
    got,
    out_low,
    grad_low,
    rows_low,
    normed,
    project,
    heads,
    attend_out,
    second_n,
    second,
    act,
    d_pre,
    mlp_out,
    d_second,
    d_mlp,
    d_attend,
    base,
    d_project,
    normed_t,
    heads_t,
    second_t,
    act_t,
    router_val,
    inverse_two,
    own,
    to_sib,
    mine,
    landed,
    moving,
    x_pre,
    x_in,
    staged,
    small_acc,
    small_in,
    own_sem,
    g_ring_send,
    g_ring_recv,
    g_sib_send,
    g_sib_recv,
    g_x_send,
    g_x_recv,
    in_send,
    in_recv,
    sib_send,
    sib_recv,
    pre_send,
    pre_recv,
    ring_send,
    ring_recv,
    x_send,
    x_recv,
    out_sem,
    small_send,
    small_recv,
    row_send,
    row_recv,
    row_own,
    take_sem,
    free,
):
    at = Place(wide)
    ring, steps = at.ring, at.ring // 2
    depth, width = wo.shape
    quarter = depth // 4
    half = depth // 2
    most = depth - quarter
    entries = slots.shape[0] // 2
    ups, downs = wu.shape[1] // width, wd.shape[0]
    tile = 256
    step = 16
    lag = LAG
    chips_of_tile = tile // (2 * depth)

    def lanes(first, size):
        return pl.ds(first if isinstance(first, int) else pl.multiple_of(first, 128), size)

    def over(size, piece_size):
        def run(piece):
            @pl.loop(0, size // piece_size)
            def _(t):
                piece(pl.multiple_of(t * piece_size, piece_size))

        return run

    def toward(d):
        return at.at_ring(1 if d == 0 else -1)

    parts = [(gains, gains_all, 0)]
    ready = {0: [0]}

    def add(name, shard, full, first, pieces=PIECES):
        for size in pieces:
            cols = pl.ds(first, size)
            parts.append((shard.at[:, cols], full.at[:, :, :, cols], size))
            if name is None:
                ready[len(parts) - 1] = [(first, size)]
            first += size
        if name is not None:
            ready[len(parts) - 1] = [name]

    for j in range(3):
        add(1 + j, wq, wq_all, j * width)
    add(4, wo, wo_all, 0)
    for j in range(downs):
        add(5 + j, wd.at[j], wd_all.at[:, :, j], 0)
    up_at = len(parts)
    for j in range(ups):
        add(None, wu, wu_all, j * width, LAST_PIECES if j == ups - 1 else PIECES)
    parts_count = len(parts)
    up_chunks = parts_count - up_at

    def window(k, s=0, d=0):
        if k == 0:
            return pl.ds(0, gains.shape[0]), pl.ds(0, gains.shape[1])
        rows = pl.ds(pl.multiple_of(at.n * quarter, quarter), most)
        if s == steps:
            return rows, pl.ds(d * (parts[k][2] // 2), parts[k][2] // 2)
        return rows, pl.ds(0, parts[k][2])

    def idle(k, s, d):
        return k == 0 and s == steps and d == 1

    def g_ring_out(k, s, d):
        pos = -(s - 1) if d == 0 else s - 1
        rows, cols = window(k, s, d)
        dst = parts[k][1].at[at.chip(pos), at.c, rows, cols]
        src = parts[k][0].at[rows, cols] if s == 1 else dst
        return remote(src, dst, g_ring_send.at[k, s - 1, d], g_ring_recv.at[k, s - 1, d], toward(d))

    def g_ring_in(k, s, d):
        pos = -s if d == 0 else s
        rows, cols = window(k, s, d)
        ref = parts[k][1].at[at.chip(pos), at.c, rows, cols]
        return remote(ref, ref, g_ring_send.at[k, s - 1, d], g_ring_recv.at[k, s - 1, d], toward(d))

    def own_copy(k):
        rows, cols = window(k)
        return pltpu.make_async_copy(
            parts[k][0].at[rows, cols], parts[k][1].at[at.q, at.c, rows, cols], own_sem.at[k]
        )

    def g_cross(k, incoming=False):
        side = 1 - at.n if incoming else at.n
        rows = pl.ds(pl.multiple_of(side * most, quarter), quarter)
        ref = parts[k][1].at[:, at.c, rows]
        return remote(ref, ref, g_x_send.at[k], g_x_recv.at[k], at.across())

    def g_sib(k, incoming=False):
        ref = parts[k][1].at[:, 1 - at.c if incoming else at.c]
        return remote(ref, ref, g_sib_send.at[k], g_sib_recv.at[k], at.sibling())

    def in_copy(j):
        return remote(given.at[j], got.at[j], in_send.at[j], in_recv.at[j], at.across())

    def take_copy(j, s, h):
        source = tokens if j == 0 else cotangent
        place = mine.at[:, :, pl.ds((2 * s + h) * width, width)]
        return pltpu.make_async_copy(source.at[s, h], place, take_sem.at[2 * s + h])

    def pick(j, s, dst):
        span = ring * depth
        wanted = slots[pl.ds(pl.multiple_of(s * entries, entries), entries), :]
        for h in (0, 1):
            spots = lax.broadcasted_iota(jnp.int32, (entries, span), 1) + h * span
            chosen = (spots == wanted).astype(BF16)

            @over(width, tile)
            def _(low):
                cols = pl.ds(low, tile)
                held = mine[:, :, lanes((2 * s + h) * width + low, tile)].reshape(span, tile)
                part = dot(chosen, held).astype(BF16)
                dst[j, :, cols] = part if h == 0 else dst[j, :, cols] + part

    def pick_all(j):
        for s in (0, 1):
            for h in (0, 1):
                take_copy(j, s, h).wait()
        pick(j, 1 - at.n, given)
        in_copy(j).start()
        pick(j, at.n, kept)
        if j == 0:
            for s in (0, 1):
                for h in (0, 1):
                    take_copy(1, s, h).start()

    def turned(src, dst):
        @over(width, tile)
        def _(low):
            chips = pl.ds(low // (2 * depth), chips_of_tile)
            dst[chips] = src[:, pl.ds(low, tile)].T.reshape(chips_of_tile, 2, depth, entries)

    def normalise():
        lane = lax.broadcasted_iota(jnp.int32, (8, 2 * HEAD_DIM), 1)
        for chip in range(ring):
            pair = jnp.where(
                lane < depth, gains_all[chip, 0].astype(F32)[:8], gains_all[chip, 1].astype(F32)[:8]
            )
            scales[:, chip * 2 * depth : (chip + 1) * 2 * depth] = pair

        @over(entries, 32)
        def _(low):
            rows = pl.ds(low, 32)
            low_rows = kept[0, rows] + got[0, rows]
            value = low_rows.astype(F32)
            rows_low[rows, :] = low_rows
            inverse = lax.rsqrt(jnp.mean(value * value, axis=-1, keepdims=True) + epsilon)
            normed[rows, :] = (value * inverse * scales[0:1, :]).astype(BF16)
            router_val[rows, :] = jnp.sum(value * router[...], axis=-1, keepdims=True)

    def project_part(j):
        @over(width, tile)
        def _(low):
            cols = pl.ds(j * width + low, tile)
            weight = wq_all[:, :, :, cols].reshape(width, tile)
            project[:, cols] = dot(normed[...], weight).astype(BF16)

    def attention(first, last):
        @pl.loop(first, last)
        def _(p):
            span = 2 * HEAD_DIM
            q, k, v = [project[:, lanes(j * width + p * span, span)] for j in range(3)]
            total = jnp.zeros((entries, span), F32)
            for head in (0, 1):
                probs = probabilities(live[...], only(q, head), k)
                total = total + only(dot(probs.astype(BF16), v), head)
            heads[:, lanes(p * span, span)] = total.astype(BF16)

    def attend_project():
        @over(width, tile)
        def _(low):
            cols = pl.ds(low, tile)
            weight = wo_all[:, :, :, cols].reshape(width, tile)
            attend_out[:, cols] = dot(heads[...], weight)

        @over(entries, 32)
        def _(low):
            rows = pl.ds(low, 32)
            middle = rows_low[rows, :].astype(F32) + attend_out[rows, :]
            inverse = lax.rsqrt(jnp.mean(middle * middle, axis=-1, keepdims=True) + epsilon)
            value = middle * inverse
            second_n[rows, :] = value
            inverse_two[rows, :] = inverse
            second[rows, :] = (value * scales[1:2, :]).astype(BF16)

    def branch_grad():
        @over(entries, 32)
        def _(low):
            rows = pl.ds(low, 32)
            dout = (kept[1, rows] + got[1, rows]).astype(F32)
            d_mlp[rows, :] = (router_val[rows, :] * dout).astype(BF16)

    def up_part(first, size):
        owner = downs * depth
        for low in range(0, size, owner):
            chip, core = (first + low) // owner // 2, (first + low) // owner % 2
            cols = pl.ds(first + low, owner)
            pre = dot(second[...], wu_all[:, :, :, cols].reshape(width, owner))
            value, slope = gelu_pair(pre)
            value = value.astype(BF16)
            d_act = dot_nt(d_mlp[...], wd_all[chip, core].reshape(owner, width))
            act[:, pl.ds(low, owner)] = value
            d_pre[:, cols] = (d_act * slope).astype(BF16)
            act_t[chip, core] = value.T.reshape(downs, depth, entries)
        chip, core = first // owner // 2, first // owner % 2

        @over(width, tile)
        def _(low):
            cols = pl.ds(low, tile)
            if size == owner:
                down = wd_all[chip, core, :, :, cols]
            else:
                down = wd_all[chip, :, :, :, cols]
            part = dot(act[:, 0:size], down.reshape(size, tile))
            chips = pl.ds(low // (2 * depth), chips_of_tile)
            up = wu_all[chips, :, :, pl.ds(first, size)]
            back = dot_nt(d_pre[:, pl.ds(first, size)], up.reshape(tile, size))
            if first == 0:
                mlp_out[:, cols] = part
                d_second[:, cols] = back
            else:
                mlp_out[:, cols] += part
                d_second[:, cols] += back

    def close():
        small_acc[0] = jnp.zeros((8, width), F32)

        @over(entries, 32)
        def _(low):
            rows = pl.ds(low, 32)
            value = rows_low[rows, :].astype(F32)
            dout = (kept[1, rows] + got[1, rows]).astype(F32)
            gate = router_val[rows, :]
            branch = attend_out[rows, :] + mlp_out[rows, :]
            out_low[rows, :] = (value + gate * branch).astype(BF16)
            d_gate = jnp.sum(dout * branch, axis=-1, keepdims=True)
            normed_value = second_n[rows, :]
            back = d_second[rows, :]
            small_acc[0, 1:2, :] += jnp.sum(back * normed_value, axis=0, keepdims=True)
            small_acc[0, 2:3, :] += jnp.sum(d_gate * value, axis=0, keepdims=True)
            back = back * scales[1:2, :]
            back = inverse_two[rows, :] * (
                back - normed_value * jnp.mean(back * normed_value, axis=-1, keepdims=True)
            )
            d_attend[rows, :] = (gate * dout + back).astype(BF16)
            base[rows, :] = dout + back + d_gate * router[...]

    def heads_grad():
        @over(width, tile)
        def _(low):
            chips = pl.ds(low // (2 * depth), chips_of_tile)
            weight = wo_all[chips].reshape(tile, width)
            heads[:, pl.ds(low, tile)] = dot_nt(d_attend[...], weight).astype(BF16)

    def attention_back(first, last):
        span = 2 * HEAD_DIM

        @pl.loop(first, last)
        def _(p):
            places = [lanes(j * width + p * span, span) for j in range(3)]
            q, k, v = [project[:, place] for place in places]
            d_pair = heads[:, places[0]]
            d_q = jnp.zeros((entries, span), F32)
            d_k = jnp.zeros((entries, span), F32)
            d_v = jnp.zeros((entries, span), F32)
            for head in (0, 1):
                probs = probabilities(live[...], only(q, head), k)
                d_own = only(d_pair, head)
                d_probs = dot_nt(d_own, v)
                d_scores = probs * (d_probs - jnp.sum(probs * d_probs, axis=-1, keepdims=True))
                d_scores = d_scores.astype(BF16)
                d_q = d_q + only(dot(d_scores, k), head)
                d_k = d_k + only(dot_tn(d_scores, q), head)
                d_v = d_v + dot_tn(probs.astype(BF16), d_own)
            d_project[:, places[0]] = (d_q * 0.125).astype(BF16)
            d_project[:, places[1]] = (d_k * 0.125).astype(BF16)
            d_project[:, places[2]] = d_v.astype(BF16)

    def normed_grad(j):
        @over(width, tile)
        def _(low):
            chips = pl.ds(low // (2 * depth), chips_of_tile)
            weight = wq_all[chips, :, :, pl.ds(j * width, width)].reshape(tile, width)
            part = dot_nt(d_project[:, pl.ds(j * width, width)], weight)
            cols = pl.ds(low, tile)
            if j == 0:
                d_second[:, cols] = part
            else:
                d_second[:, cols] += part

    def finish():
        @over(entries, 32)
        def _(low):
            rows = pl.ds(low, 32)
            value = rows_low[rows, :].astype(F32)
            inverse = lax.rsqrt(jnp.mean(value * value, axis=-1, keepdims=True) + epsilon)
            value = value * inverse
            back = d_second[rows, :]
            small_acc[0, 0:1, :] += jnp.sum(back * value, axis=0, keepdims=True)
            back = back * scales[0:1, :]
            back = inverse * (back - value * jnp.mean(back * value, axis=-1, keepdims=True))
            grad_low[rows, :] = (base[rows, :] + back).astype(BF16)

    count = len(chunks)
    reused = [k for k in range(count) if chunks[k].panel >= ups]

    def spread(k, first, size):
        return lanes(chunks[k].panel * width + chunks[k].off + first, size)

    def sums(k, chip, rows, first, size):
        c = chunks[k]
        if c.panel < ups:
            return mine.at[chip, rows, spread(k, first, size)]
        p = c.panel - ups
        return wd_all.at[chip, p // downs, p % downs, rows, lanes(c.off + first, size)]

    def passing(k, t, d, rows, first, size):
        c = chunks[k]
        if c.panel < ups:
            if t == 0:
                return landed.at[d, rows, spread(k, first, size)]
            return moving.at[t - 1, d, rows, spread(k, first, size)]
        p = c.panel - ups
        cols = lanes(p % ups * width + c.off + first, size)
        slab = 12 + p // ups if t == 0 else p // ups * 6 + (t - 1) * 2 + d
        if t == 0:
            rows = pl.ds(d * half + rows.start, rows.size)
        return wu_all.at[slab // 2, slab % 2, rows, cols]

    every = pl.ds(0, depth)

    def ride(k):
        return chunks[k].give * at.n if chunks[k].give else 0, chunks[k].size - chunks[k].give

    def product(k, core, put):
        c = chunks[k]
        if c.kind == "down":
            left, right = act_t[:, core, c.j], d_mlp
        else:
            tall, right = {
                "up": (second_t, d_pre),
                "out": (heads_t, d_attend),
                "qkv": (normed_t, d_project),
            }[c.kind]
            left = tall[:, core]
        left = left.reshape(ring * depth, entries)

        @pl.loop(0, c.size // tile)
        def _(t):
            cols = pl.ds(pl.multiple_of(t * tile, tile), tile)
            take = pl.ds(pl.multiple_of(c.first + t * tile, tile), tile)
            put(cols, dot(left, right[:, take]).reshape(ring, depth, tile))

    def out_copy(k):
        c = chunks[k]
        out = {"up": o_up, "down": o_down, "out": o_out, "qkv": o_qkv}[c.kind]
        rows = pl.ds(c.j * depth if c.kind == "down" else 0, depth)
        return pltpu.make_async_copy(
            staged.at[k % 2, :, pl.ds(0, c.size)], out.at[rows, pl.ds(c.first, c.size)], out_sem.at[k]
        )

    def sib(k):
        src = to_sib.at[k % 2, :, :, pl.ds(0, chunks[k].size)]
        dst = sums(k, slice(None), slice(None), 0, chunks[k].size)
        return remote(src, dst, sib_send.at[k], sib_recv.at[k], at.sibling())

    def pre(k):
        c = chunks[k]
        src = sums(k, slice(None), slice(None), (c.size - c.give) * (1 - at.n), c.give)
        dst = x_pre.at[:, :, lanes(c.given_at, c.give)]
        return remote(src, dst, pre_send.at[k], pre_recv.at[k], at.across())

    def dest(t, d):
        return at.chip(steps - t if d == 0 else t - steps)

    def ring_out(k, t, d):
        rows = pl.ds(d * half, half) if t == 0 else every
        src = sums(k, dest(t, d), rows, *ride(k))
        land = passing(k, t, d, pl.ds(0, half) if t == 0 else every, *ride(k))
        return remote(src, land, ring_send.at[k, t, d], ring_recv.at[k, t, d], toward(d))

    def cross(k):
        first, size = ride(k)
        dst = x_in.at[:, lanes(chunks[k].start + first, size)]
        return remote(sums(k, at.q, every, first, size), dst, x_send.at[k], x_recv.at[k], at.across())

    bits = [1 << b for b in range(ring.bit_length() - 1)]
    partners = [at.sibling(), at.across()] + [at.flipped(bit) for bit in bits]
    stages = len(partners)

    def small_copy(j):
        return remote(
            small_acc.at[j], small_in.at[j], small_send.at[j], small_recv.at[j], partners[j]
        )

    def row_copy(j, p):
        rows = pl.ds(p * (entries // ROW_PIECES), entries // ROW_PIECES)
        src = out_low if j == 0 else grad_low
        dst = rows_all.at[j, at.n, rows]
        return remote(src.at[rows], dst, row_send.at[j, p], row_recv.at[j, p], at.across())

    def row_in(j, p):
        rows = pl.ds(p * (entries // ROW_PIECES), entries // ROW_PIECES)
        ref = rows_all.at[j, 1 - at.n, rows]
        return remote(ref, ref, row_send.at[j, p], row_recv.at[j, p], at.across())

    def row_keep(j):
        src = out_low if j == 0 else grad_low
        return pltpu.make_async_copy(src, rows_all.at[j, at.n], row_own.at[j])

    def release():
        for k in range(parts_count):
            g_sib(k).wait_send()
            if k > 0:
                g_cross(k).wait_send()
            for s in range(1, steps + 1):
                for d in (0, 1):
                    if not idle(k, s, d):
                        g_ring_out(k, s, d).wait_send()
        for j, device in enumerate((at.at_ring(-1), at.at_ring(1), at.sibling())):
            pl.semaphore_signal(free.at[j], inc=1, device_id=device, device_id_type=MESH)

    pairs = width // (2 * HEAD_DIM)
    cuts = [pairs * j // 8 for j in (0, 2, 5, 8)]
    work = {
        0: [normalise, lambda: turned(normed, normed_t)],
        1: [lambda: project_part(0)],
        2: [lambda: project_part(1)],
        3: [lambda: project_part(2), lambda: attention(cuts[0], cuts[1])],
        4: [lambda: attention(cuts[1], cuts[2])],
        5: [lambda: attention(cuts[2], cuts[3]), attend_project],
        6: [lambda: turned(heads, heads_t), lambda: turned(second, second_t)],
        7: [branch_grad],
    }
    back_cuts = [pairs * j // 4 for j in range(5)]
    back_work = [heads_grad]
    back_work += [functools.partial(attention_back, back_cuts[j], back_cuts[j + 1]) for j in range(4)]
    back_work += [functools.partial(normed_grad, j) for j in range(3)]
    back_work += [finish]

    def gather_turn(i):
        for k in range(LEAD + 1) if i == 0 else (i + LEAD,):
            if k < parts_count:
                for d in (0, 1):
                    g_ring_out(k, 1, d).start()
                own_copy(k).start()
        if i in PICK_AT:
            pick_all(PICK_AT.index(i))
        for s in range(1, steps + 1):
            k = i - lag * s
            if 0 <= k < parts_count:
                for d in (0, 1):
                    if not idle(k, s, d):
                        g_ring_in(k, s, d).wait_recv()
                    if s < steps and not idle(k, s + 1, d):
                        g_ring_out(k, s + 1, d).start()
                if s == steps:
                    own_copy(k).wait()
                    if k > 0:
                        g_cross(k).start()
        k = i - lag * (steps + 1)
        if 0 <= k < parts_count:
            if k > 0:
                g_cross(k, True).wait_recv()
            g_sib(k).start()
        k = i - lag * (steps + 1) - 1
        if 0 <= k < parts_count:
            g_sib(k, True).wait_recv()
            if k == 0:
                for j in (0, 1):
                    in_copy(j).wait_recv()
            for piece in ready.get(k, ()):
                if isinstance(piece, int):
                    for job in work.get(piece, ()):
                        job()
                else:
                    up_part(*piece)

    ring_at = 1 + lag
    work_at = up_chunks
    small_at = work_at + len(back_work)

    def reduce_turn(i):
        k = i - ring_at - lag * steps - lag
        if 0 <= k < count:
            c = chunks[k]
            cross(k).wait_recv()
            if k >= 2:
                out_copy(k - 2).wait()
            inner = c.size - 2 * c.give

            @over(depth, step)
            def _(row):
                rows = pl.ds(row, step)

                def mixed(first, size):
                    return sums(k, at.q, rows, first, size)[...].astype(F32), x_in[
                        rows, lanes(c.start + first, size)
                    ].astype(F32)

                here, there = mixed(c.give, inner)
                staged[k % 2, rows, c.give : c.give + inner] = here + there
                if c.give:
                    alone = (c.size - c.give) * at.n
                    staged[k % 2, rows, lanes(alone, c.give)] = mixed(alone, c.give)[0]
                    alone = (c.size - c.give) * (1 - at.n)
                    staged[k % 2, rows, lanes(alone, c.give)] = mixed(alone, c.give)[1]

            out_copy(k).start()
        k = i - ring_at - lag * steps
        if 0 <= k < count:
            for d in (0, 1):
                land = passing(k, steps - 1, d, every, *ride(k))
                remote(
                    land,
                    land,
                    ring_send.at[k, steps - 1, d],
                    ring_recv.at[k, steps - 1, d],
                    toward(d),
                ).wait_recv()

            @over(depth, step)
            def _(row):
                rows = pl.ds(row, step)
                total = sums(k, at.q, rows, *ride(k))
                value = total[...].astype(F32)
                for d in (0, 1):
                    value = value + passing(k, steps - 1, d, rows, *ride(k))[...].astype(F32)
                total[...] = value.astype(BF16)

            cross(k).start()
        for t in range(steps - 1, 0, -1):
            k = i - ring_at - lag * t
            if 0 <= k < count:
                for d in (0, 1):
                    size = half if t == 1 else depth
                    land = passing(k, t - 1, d, pl.ds(0, size), *ride(k))
                    remote(
                        land, land, ring_send.at[k, t - 1, d], ring_recv.at[k, t - 1, d], toward(d)
                    ).wait_recv()
                    to = dest(t, d)
                    low = d * half if t == 1 else 0

                    @over(size, step)
                    def _(row):
                        total = sums(k, to, pl.ds(low + row, step), *ride(k))
                        came = passing(k, t - 1, d, pl.ds(row, step), *ride(k))
                        value = total[...].astype(F32) + came[...].astype(F32)
                        total[...] = value.astype(BF16)

                    ring_out(k, t, d).start()
        k = i - ring_at
        if 0 <= k < count:
            c = chunks[k]
            if c.give > 0:
                pre(k).wait_recv()
                alone = (c.size - c.give) * at.n

                @pl.loop(0, ring)
                def _(chip):
                    total = sums(k, chip, every, alone, c.give)
                    came = x_pre[chip, :, lanes(c.given_at, c.give)]
                    total[...] = (total[...].astype(F32) + came.astype(F32)).astype(BF16)

            for d in (0, 1):
                if k == reused[0]:
                    pl.semaphore_wait(free.at[d], 1)
                ring_out(k, 0, d).start()
        k = i - 1
        if 0 <= k < count:
            c = chunks[k]
            all_sums = sums(k, slice(None), slice(None), 0, c.size)
            remote(all_sums, all_sums, sib_send.at[k], sib_recv.at[k], at.sibling()).wait_recv()

            @pl.loop(0, ring)
            def _(chip):
                total = sums(k, chip, every, 0, c.size)
                total[...] = (total[...].astype(F32) + own[chip, :, 0 : c.size]).astype(BF16)

            if c.give > 0:
                pre(k).start()
        k = i
        if 0 <= k < count:
            if k >= 2:
                sib(k - 2).wait_send()

            def keep_other(cols, value):
                to_sib[k % 2, :, :, cols] = value.astype(BF16)

            def keep_own(cols, value):
                own[:, :, cols] = value

            product(k, 1 - at.c, keep_other)
            if k == reused[0]:
                pl.semaphore_wait(free.at[2], 1)
            sib(k).start()
            product(k, at.c, keep_own)
        j = i - work_at
        if 0 <= j < len(back_work):
            back_work[j]()
        p = i - ROWS_AT
        if 0 <= p < ROW_PIECES:
            row_copy(0, p).start()
        if j == 0:
            row_keep(0).start()
        p = i - max(small_at, ROWS_AT)
        if 0 <= p < ROW_PIECES:
            row_copy(1, p).start()
        if p == 0:
            row_keep(1).start()
        j = i - small_at
        if 0 <= j <= stages:
            if j > 0:
                small_copy(j - 1).wait_recv()
                small_acc[j] = small_acc[j - 1] + small_in[j - 1]
            if j < stages:
                small_copy(j).start()
            else:
                o_small[...] = small_acc[stages]

    for s in (0, 1):
        for h in (0, 1):
            take_copy(0, s, h).start()
    greet(partners + [at.at_ring(1), at.at_ring(-1)])
    offset = up_at + lag * (steps + 1) + 1
    for i in range(offset + count + ring_at + lag * steps + lag + 1):
        gather_turn(i)
        if i == offset + up_chunks - 1:
            release()
            close()
        reduce_turn(i - offset)

    for j in (0, 1):
        in_copy(j).wait_send()
    for k in range(count):
        if k >= count - 2:
            sib(k).wait_send()
            out_copy(k).wait()
        if chunks[k].give > 0:
            pre(k).wait_send()
        cross(k).wait_send()
        for t in range(steps):
            for d in (0, 1):
                ring_out(k, t, d).wait_send()
    for j in range(stages):
        small_copy(j).wait_send()
    for j in (0, 1):
        for p in range(ROW_PIECES):
            row_copy(j, p).wait_send()
            row_in(j, p).wait_recv()
        row_keep(j).wait()


class Chunk(NamedTuple):
    kind: str
    j: int
    first: int
    size: int
    panel: int
    off: int
    start: int
    give: int
    given_at: int


def cut_chunks(width, ff):
    panels = [("up", j, j * width) for j in range(ff // width)]
    panels += [("down", j, 0) for j in range(ff // width)]
    panels += [("out", 0, 0)] + [("qkv", j, j * width) for j in range(3)]
    plain = []
    for panel, (kind, j, first) in enumerate(panels):
        off = 0
        last = panel in (ff // width - 1, len(panels) - 1)
        for size in LAST_PIECES if last else PIECES:
            plain.append((kind, j, first + off, size, panel, off))
            off += size
    chunks, start, given = [], 0, 0
    for k, piece in enumerate(plain):
        inside = GIVE_SKIP[0] <= k < len(plain) - GIVE_SKIP[1]
        give = GIVE if inside and piece[3] == 512 else 0
        chunks.append(Chunk(*piece, start, give, given))
        start += piece[3]
        given += give
    return tuple(chunks), start, given


def layer(wide, gains, wq, wo, wu, wd, tokens, cotangent, slots, router, live):
    depth, width = wo.shape
    ring, steps = wide // 2, wide // 4
    entries = slots.shape[0] // 2
    ff = wu.shape[1]
    ups = downs = ff // width
    chunks, columns, given_columns = cut_chunks(width, ff)
    parts = 1 + (3 + downs + ups) * len(PIECES) + len(LAST_PIECES)
    count = len(chunks)
    stages = 2 + (ring.bit_length() - 1)
    in_vmem = pl.BlockSpec(memory_space=pltpu.VMEM)
    anywhere = pl.BlockSpec(memory_space=pl.ANY)
    dma = pltpu.SemaphoreType.DMA
    vmem = pltpu.VMEM
    shape = jax.ShapeDtypeStruct
    tall = (ring, 2, depth, entries)
    square = (entries, width)
    return pl.pallas_call(
        functools.partial(layer_kernel, wide, chunks),
        out_shape=[
            shape((depth, 3 * width), F32),
            shape((depth, width), F32),
            shape((depth, ff), F32),
            shape((ff // wide, width), F32),
            shape((8, width), F32),
            shape((2, 2, entries, width), BF16),
        ],
        in_specs=[anywhere] * 7 + [in_vmem] * 3,
        out_specs=[anywhere] * 4 + [in_vmem, anywhere],
        scratch_shapes=[
            vmem((ring, 2, depth, 3 * width), BF16),
            vmem((ring, 2, depth, width), BF16),
            vmem((ring, 2, depth, ff), BF16),
            vmem((ring, 2, downs, depth, width), BF16),
            vmem((ring, 2) + gains.shape, BF16),
            vmem((8, width), F32),
            vmem((2,) + square, BF16),
            vmem((2,) + square, BF16),
            vmem((2,) + square, BF16),
            vmem(square, BF16),
            vmem(square, BF16),
            vmem(square, BF16),
            vmem(square, BF16),
            vmem((entries, 3 * width), BF16),
            vmem(square, BF16),
            vmem(square, F32),
            vmem(square, F32),
            vmem(square, BF16),
            vmem((entries, 512), BF16),
            vmem((entries, ff), BF16),
            vmem(square, F32),
            vmem(square, F32),
            vmem(square, BF16),
            vmem(square, BF16),
            vmem(square, F32),
            vmem((entries, 3 * width), BF16),
            vmem(tall, BF16),
            vmem(tall, BF16),
            vmem(tall, BF16),
            vmem((ring, 2, downs, depth, entries), BF16),
            vmem((entries, 1), F32),
            vmem((entries, 1), F32),
            vmem((ring, depth, 512), F32),
            vmem((2, ring, depth, 512), BF16),
            vmem((ring, depth, ups * width), BF16),
            vmem((2, depth // 2, ups * width), BF16),
            vmem((steps - 1, 2, depth, ups * width), BF16),
            vmem((ring, depth, max(given_columns, 128)), BF16),
            vmem((depth, columns), BF16),
            vmem((2, depth, 512), F32),
            vmem((stages + 1, 8, width), F32),
            vmem((stages, 8, width), F32),
            dma((parts,)),
            dma((parts, steps, 2)),
            dma((parts, steps, 2)),
            dma((parts,)),
            dma((parts,)),
            dma((parts,)),
            dma((parts,)),
            dma((2,)),
            dma((2,)),
            dma((count,)),
            dma((count,)),
            dma((count,)),
            dma((count,)),
            dma((count, steps, 2)),
            dma((count, steps, 2)),
            dma((count,)),
            dma((count,)),
            dma((count,)),
            dma((stages,)),
            dma((stages,)),
            dma((2, ROW_PIECES)),
            dma((2, ROW_PIECES)),
            dma((2,)),
            dma((4,)),
            pltpu.SemaphoreType.REGULAR((3,)),
        ],
        compiler_params=pltpu.CompilerParams(
            collective_id=1, has_side_effects=True, vmem_limit_bytes=63 * 1024 * 1024
        ),
        name="layer",
    )(
        gains,
        wq,
        wo,
        wu,
        wd.reshape(downs, depth, width),
        tokens.reshape(2, 2, ring, depth, width),
        cotangent.reshape(2, 2, ring, depth, width),
        slots,
        router,
        live,
    )


def paired_body(
    wide, tokens, cotangent, lengths, routes, w_qkv, w_out, w_up, w_down, gain_attn, gain_mlp, router
):
    place = lax.axis_index("narrow")
    seqs, span, width = tokens.shape
    list_len = routes.shape[1]
    depth = gain_attn.shape[0]
    counts = lengths // 8
    entry = jnp.arange(list_len, dtype=jnp.int32)
    live = entry[None, :] < counts[:, None]
    local_slot = jnp.where(live, routes - place * span, -1)
    spots = jnp.arange(span, dtype=jnp.int32)
    chosen = (local_slot[:, :, None] == spots[None, None, :]).astype(BF16)

    slots = local_slot.reshape(seqs * list_len, 1)
    gains = jnp.stack(
        [jnp.concatenate([gain_attn, gain_attn]), jnp.concatenate([gain_mlp, gain_mlp])]
    )
    gains = jnp.pad(gains, ((0, 14), (0, 0)))
    router_row = router.astype(F32)[None, :]
    live_row = lax.dynamic_index_in_dim(live, place, 0, keepdims=True).astype(jnp.int32)
    grad_qkv, grad_out, grad_up, grad_down, small, rows_out = layer(
        wide, gains, w_qkv, w_out, w_up, w_down, tokens, cotangent, slots, router_row, live_row
    )
    hit = jnp.any(local_slot[:, :, None] == spots[None, None, :], axis=1)

    def put(base, fresh):
        spread = jnp.einsum("sep,sed->spd", chosen, fresh, preferred_element_type=F32)
        return jnp.where(hit[:, :, None], spread.astype(BF16), base)

    start = lax.axis_index("wide") * depth
    return (
        put(tokens, rows_out[0]),
        put(cotangent, rows_out[1]),
        grad_qkv,
        grad_out,
        grad_up,
        grad_down,
        lax.dynamic_slice_in_dim(small[0], start, depth),
        lax.dynamic_slice_in_dim(small[1], start, depth),
        small[2],
    )


def body(wide, narrow, tokens, *others):
    if narrow == 2 and tokens.shape == (2, wide * 64, 1024) and wide == 16:
        return paired_body(wide, tokens, *others)
    return general_body(tokens, *others)


def solution(mesh):
    in_specs = (
        P("wide", "narrow", None),
        P("wide", "narrow", None),
        P("wide"),
        P("wide", None),
        P("wide", None),
        P("wide", None),
        P("wide", None),
        P("wide", None),
        P("wide"),
        P("wide"),
        P(),
    )
    out_specs = (
        P("wide", "narrow", None),
        P("wide", "narrow", None),
        P("wide", None),
        P("wide", None),
        P("wide", None),
        P("wide", None),
        P("wide"),
        P("wide"),
        P(),
    )
    sizes = mesh.shape["wide"], mesh.shape["narrow"]
    return jax.shard_map(functools.partial(body, *sizes), mesh=mesh, in_specs=in_specs, out_specs=out_specs, check_vma=False)
```

```python
import functools
from typing import NamedTuple

import jax
import jax.numpy as jnp
from jax import lax
from jax.experimental import pallas as pl
from jax.experimental.pallas import tpu as pltpu
from jax.sharding import PartitionSpec as P

HEAD_DIM = 64
MESH = pl.DeviceIdType.MESH
F32 = jnp.float32
BF16 = jnp.bfloat16
LAG = 2
LEAD = 6
ROWS_AT = 20
PICK_AT = (0, 3)
PIECES = (512, 512)
LAST_PIECES = (512, 256, 256)
GIVE = 128
GIVE_SKIP = (3, 6)
ROW_PIECES = 8

epsilon = 1e-06
masked_score = -1e30


def rms_parts(values):
    inverse = lax.rsqrt(jnp.mean(values * values, axis=-1, keepdims=True) + epsilon)
    return (values * inverse, inverse)


def rms_back(grad_normed, normed, inverse):
    return inverse * (grad_normed - normed * jnp.mean(grad_normed * normed, axis=-1, keepdims=True))


def attend_scores(queries, keys_all, allowed):
    scores = (
        jnp.einsum("sqhe,skhe->shqk", queries, keys_all, preferred_element_type=jnp.float32) * 0.125
    )
    return jnp.where(allowed, scores, masked_score)


def attend_forward(queries, keys_all, values_all, allowed):
    scores = attend_scores(queries, keys_all, allowed)
    top_score = jnp.max(scores, axis=-1, keepdims=True)
    expo = jnp.exp(scores - top_score)
    total = jnp.sum(expo, axis=-1, keepdims=True)
    log_total = top_score + jnp.log(total)
    probs_low = (expo / total).astype(jnp.bfloat16)
    heads_out = jnp.einsum(
        "shqk,skhe->sqhe", probs_low, values_all, preferred_element_type=jnp.float32
    )
    return (heads_out, log_total)


def attend_backward(queries, keys_all, values_all, allowed, log_total, d_heads):
    probs_again = jnp.exp(attend_scores(queries, keys_all, allowed) - log_total)
    d_probs = jnp.einsum("sqhe,skhe->shqk", d_heads, values_all, preferred_element_type=jnp.float32)
    row_dot = jnp.sum(probs_again * d_probs, axis=-1, keepdims=True)
    d_scores = (probs_again * (d_probs - row_dot)).astype(jnp.bfloat16)
    d_queries = (
        jnp.einsum("shqk,skhe->sqhe", d_scores, keys_all, preferred_element_type=jnp.float32)
        * 0.125
    )
    d_key_part = (
        jnp.einsum("shqk,sqhe->skhe", d_scores, queries, preferred_element_type=jnp.float32) * 0.125
    )
    d_value_part = jnp.einsum(
        "shqk,sqhe->skhe",
        probs_again.astype(jnp.bfloat16),
        d_heads,
        preferred_element_type=jnp.float32,
    )
    return (d_queries, d_key_part, d_value_part)


def general_body(
    tokens, cotangent, lengths, routes, w_qkv, w_out, w_up, w_down, gain_attn, gain_mlp, router
):
    parts_narrow = lax.axis_size("narrow")
    place = lax.axis_index("narrow")
    seqs, span, width = tokens.shape
    list_len = routes.shape[1]
    own_entries = list_len // parts_narrow
    rows_total = seqs * own_entries
    counts = lengths // 8
    entry = jnp.arange(list_len, dtype=jnp.int32)
    live = entry[None, :] < counts[:, None]
    local_slot = routes - place * span
    mine = live & (local_slot >= 0) & (local_slot < span)
    pick = jnp.clip(local_slot, 0, span - 1)
    keep = mine[:, :, None]
    taken_in = jnp.take_along_axis(tokens, pick[:, :, None], axis=1)
    taken_cot = jnp.take_along_axis(cotangent, pick[:, :, None], axis=1)
    blank = jnp.zeros_like(taken_in)
    rows_in, rows_cot = (
        lax.psum_scatter(
            jnp.where(keep, taken_in, blank), "narrow", scatter_dimension=1, tiled=True
        ).astype(jnp.float32),
        lax.psum_scatter(
            jnp.where(keep, taken_cot, blank), "narrow", scatter_dimension=1, tiled=True
        ).astype(jnp.float32),
    )
    inputs_rows = rows_in.reshape(rows_total, width)
    inputs_low = inputs_rows.astype(jnp.bfloat16)
    dout = rows_cot.reshape(rows_total, width)
    gathered = (
        lax.all_gather(w_qkv, "wide", axis=0, tiled=True),
        lax.all_gather(w_out, "wide", axis=0, tiled=True),
        lax.all_gather(w_up, "wide", axis=0, tiled=True),
        lax.all_gather(w_down, "wide", axis=0, tiled=True),
        lax.all_gather(gain_attn, "wide", axis=0, tiled=True),
        lax.all_gather(gain_mlp, "wide", axis=0, tiled=True),
    )
    weight_qkv, weight_out, weight_up, weight_down, gain_first, gain_second = gathered
    scale_first = gain_first.astype(jnp.float32)
    scale_second = gain_second.astype(jnp.float32)
    normed_one, inverse_one = rms_parts(inputs_rows)
    normed_low = (normed_one * scale_first).astype(jnp.bfloat16)
    project = jnp.dot(normed_low, weight_qkv, preferred_element_type=jnp.float32).astype(
        jnp.bfloat16
    )
    queries = project[:, :width].reshape(seqs, own_entries, -1, HEAD_DIM)
    key_own = project[:, width : 2 * width].reshape(seqs, own_entries, width)
    value_own = project[:, 2 * width :].reshape(seqs, own_entries, width)
    keys_all, values_all = (
        lax.all_gather(key_own, "narrow", axis=1, tiled=True),
        lax.all_gather(value_own, "narrow", axis=1, tiled=True),
    )
    keys_all = keys_all.reshape(seqs, list_len, -1, HEAD_DIM)
    values_all = values_all.reshape(seqs, list_len, -1, HEAD_DIM)
    query_pos = place * own_entries + jnp.arange(own_entries, dtype=jnp.int32)
    allowed = (entry[None, None, None, :] <= query_pos[None, None, :, None]) & (
        entry[None, None, None, :] < counts[:, None, None, None]
    )
    heads_out, log_total = attend_forward(queries, keys_all, values_all, allowed)
    heads_low = heads_out.reshape(rows_total, width).astype(jnp.bfloat16)
    attend_out = jnp.dot(heads_low, weight_out, preferred_element_type=jnp.float32)
    middle = inputs_rows + attend_out
    normed_two, inverse_two = rms_parts(middle)
    second_low = (normed_two * scale_second).astype(jnp.bfloat16)
    pre_act = jnp.dot(second_low, weight_up, preferred_element_type=jnp.float32)
    activ_full, gelu_back = jax.vjp(jax.nn.gelu, pre_act)
    activ_low = activ_full.astype(jnp.bfloat16)
    mlp_out = jnp.dot(activ_low, weight_down, preferred_element_type=jnp.float32)
    branch = attend_out + mlp_out
    router_val = jnp.dot(inputs_low, router, preferred_element_type=jnp.float32)
    out_low = (inputs_rows + router_val[:, None] * branch).astype(jnp.bfloat16)
    back_set = (
        lax.all_gather(w_qkv, "wide", axis=0, tiled=True),
        lax.all_gather(w_out, "wide", axis=0, tiled=True),
        lax.all_gather(w_up, "wide", axis=0, tiled=True),
        lax.all_gather(w_down, "wide", axis=0, tiled=True),
        lax.all_gather(gain_attn, "wide", axis=0, tiled=True),
        lax.all_gather(gain_mlp, "wide", axis=0, tiled=True),
    )
    back_qkv, back_out, back_up, back_down, back_gain_a, back_gain_m = back_set
    back_first = back_gain_a.astype(jnp.float32)
    back_second = back_gain_m.astype(jnp.float32)
    d_branch = router_val[:, None] * dout
    d_router_val = jnp.sum(dout * branch, axis=-1)
    d_mlp = d_branch.astype(jnp.bfloat16)
    grad_down_full = jnp.einsum("rf,rd->fd", activ_low, d_mlp, preferred_element_type=jnp.float32)
    d_act = jnp.einsum("rd,fd->rf", d_mlp, back_down, preferred_element_type=jnp.float32)
    d_pre = gelu_back(d_act)[0].astype(jnp.bfloat16)
    grad_up_full = jnp.einsum("rd,rf->df", second_low, d_pre, preferred_element_type=jnp.float32)
    d_normed_two = jnp.einsum("rf,df->rd", d_pre, back_up, preferred_element_type=jnp.float32)
    grad_gain_two = jnp.sum(d_normed_two * normed_two, axis=0)
    d_middle = rms_back(d_normed_two * back_second, normed_two, inverse_two)
    d_attend = (d_branch + d_middle).astype(jnp.bfloat16)
    grad_out_full = jnp.einsum("rd,re->de", heads_low, d_attend, preferred_element_type=jnp.float32)
    d_heads = jnp.einsum(
        "re,de->rd", d_attend, back_out, preferred_element_type=jnp.float32
    ).astype(jnp.bfloat16)
    d_heads_own = d_heads.reshape(seqs, own_entries, -1, HEAD_DIM)
    d_queries, d_key_part, d_value_part = attend_backward(
        queries, keys_all, values_all, allowed, log_total, d_heads_own
    )
    d_key_own, d_value_own = (
        lax.psum_scatter(
            d_key_part.reshape(seqs, list_len, width), "narrow", scatter_dimension=1, tiled=True
        ),
        lax.psum_scatter(
            d_value_part.reshape(seqs, list_len, width), "narrow", scatter_dimension=1, tiled=True
        ),
    )
    d_project = jnp.concatenate(
        [
            d_queries.reshape(rows_total, width),
            d_key_own.reshape(rows_total, width),
            d_value_own.reshape(rows_total, width),
        ],
        axis=-1,
    ).astype(jnp.bfloat16)
    grad_qkv_full = jnp.einsum(
        "rd,re->de", normed_low, d_project, preferred_element_type=jnp.float32
    )
    d_normed = jnp.einsum("re,de->rd", d_project, back_qkv, preferred_element_type=jnp.float32)
    grad_gain_one = jnp.sum(d_normed * normed_one, axis=0)
    d_norm_rows = rms_back(d_normed * back_first, normed_one, inverse_one)
    d_rows = dout + d_middle + d_norm_rows + d_router_val[:, None] * router.astype(jnp.float32)
    grad_router_part = jnp.dot(d_router_val, inputs_rows, precision=lax.Precision.HIGHEST)
    grad_low = d_rows.astype(jnp.bfloat16)
    out_all, grad_all = (
        lax.all_gather(out_low.reshape(seqs, own_entries, width), "narrow", axis=1, tiled=True),
        lax.all_gather(grad_low.reshape(seqs, own_entries, width), "narrow", axis=1, tiled=True),
    )
    target = jnp.where(mine, pick, span)
    put = jax.vmap(lambda base, where_to, fresh: base.at[where_to].set(fresh, mode="drop"))
    mixed = put(tokens, target, out_all)
    grad_tokens = put(cotangent, target, grad_all)
    shards = (
        lax.psum_scatter(grad_qkv_full, "wide", scatter_dimension=0, tiled=True),
        lax.psum_scatter(grad_out_full, "wide", scatter_dimension=0, tiled=True),
        lax.psum_scatter(grad_up_full, "wide", scatter_dimension=0, tiled=True),
        lax.psum_scatter(grad_down_full, "wide", scatter_dimension=0, tiled=True),
        lax.psum_scatter(grad_gain_one, "wide", scatter_dimension=0, tiled=True),
        lax.psum_scatter(grad_gain_two, "wide", scatter_dimension=0, tiled=True),
    )
    summed = lax.psum((shards[0], shards[1], shards[2], shards[3], shards[4], shards[5]), "narrow")
    grad_router = lax.psum(grad_router_part, ("wide", "narrow"))
    return (
        mixed,
        grad_tokens,
        summed[0],
        summed[1],
        summed[2],
        summed[3],
        summed[4],
        summed[5],
        grad_router,
    )


def dot(left, right):
    return jnp.dot(left, right, preferred_element_type=F32)


def dot_nt(left, right):
    return lax.dot_general(left, right, (((1,), (1,)), ((), ())), preferred_element_type=F32)


def dot_tn(left, right):
    return lax.dot_general(left, right, (((0,), (0,)), ((), ())), preferred_element_type=F32)


class Place:
    def __init__(self, wide):
        self.ring = wide // 2
        self.length = self.ring // 2
        self.w = lax.axis_index("wide")
        self.n = lax.axis_index("narrow")
        self.c = self.w % 2
        self.q = self.w // 2
        row = self.q % 2
        col = self.q // 2
        self.r = col + row * (2 * self.length - 1 - 2 * col)

        self.around = {}
        for offset in range(-(self.ring // 2), self.ring // 2 + 1):
            pos = lax.rem(self.r + offset + self.ring, self.ring)
            row = pos // self.length
            col = pos + row * (2 * self.length - 1 - 2 * pos)
            self.around[offset] = col * 2 + row

    def chip(self, offset):
        return self.around[offset]

    def at_ring(self, offset):
        return (self.around[offset] * 2 + self.c, self.n)

    def sibling(self):
        return (self.q * 2 + 1 - self.c, self.n)

    def across(self):
        return (self.w, 1 - self.n)

    def flipped(self, bit):
        return ((self.q + bit - 2 * bit * ((self.q // bit) % 2)) * 2 + self.c, self.n)


def greet(partners):
    barrier = pltpu.get_barrier_semaphore()
    for partner in partners:
        pl.semaphore_signal(barrier, inc=1, device_id=partner, device_id_type=MESH)
    pl.semaphore_wait(barrier, len(partners))


def remote(src, dst, send, recv, device):
    return pltpu.make_async_remote_copy(
        src_ref=src, dst_ref=dst, send_sem=send, recv_sem=recv, device_id=device, device_id_type=MESH
    )


def probabilities(live, queries, keys):
    entries = queries.shape[0]
    scores = dot_nt(queries, keys) * 0.125
    q_at = lax.broadcasted_iota(jnp.int32, (entries, entries), 0)
    k_at = lax.broadcasted_iota(jnp.int32, (entries, entries), 1)
    scores = jnp.where((k_at <= q_at) & (live > 0), scores, masked_score)
    expo = jnp.exp(scores - jnp.max(scores, axis=-1, keepdims=True))
    return expo / jnp.sum(expo, axis=-1, keepdims=True)


def only(value, head):
    lane = lax.broadcasted_iota(jnp.int32, value.shape, 1)
    return jnp.where(lane // HEAD_DIM == head, value, jnp.zeros_like(value))


def gelu_pair(x):
    inner = 0.7978845608028654 * (x + 0.044715 * (x * x * x))
    bent = jnp.tanh(inner)
    half = 0.5 * (1.0 + bent)
    slope = 0.7978845608028654 * (1.0 + 0.134145 * (x * x))
    return x * half, half + 0.5 * x * (1.0 - bent * bent) * slope


def layer_kernel(
    wide,
    chunks,
    gains,
    wq,
    wo,
    wu,
    wd,
    tokens,
    cotangent,
    slots,
    router,
    live,
    o_qkv,
    o_out,
    o_up,
    o_down,
    o_small,
    rows_all,
    wq_all,
    wo_all,
    wu_all,
    wd_all,
    gains_all,
    scales,
    kept,
    given,
    got,
    out_low,
    grad_low,
    rows_low,
    normed,
    project,
    heads,
    attend_out,
    second_n,
    second,
    act,
    d_pre,
    mlp_out,
    d_second,
    d_mlp,
    d_attend,
    base,
    d_project,
    normed_t,
    heads_t,
    second_t,
    act_t,
    router_val,
    inverse_two,
    own,
    to_sib,
    mine,
    landed,
    moving,
    x_pre,
    x_in,
    staged,
    small_acc,
    small_in,
    own_sem,
    g_ring_send,
    g_ring_recv,
    g_sib_send,
    g_sib_recv,
    g_x_send,
    g_x_recv,
    in_send,
    in_recv,
    sib_send,
    sib_recv,
    pre_send,
    pre_recv,
    ring_send,
    ring_recv,
    x_send,
    x_recv,
    out_sem,
    small_send,
    small_recv,
    row_send,
    row_recv,
    row_own,
    take_sem,
    free,
):
    at = Place(wide)
    ring, steps = at.ring, at.ring // 2
    depth, width = wo.shape
    quarter = depth // 4
    half = depth // 2
    most = depth - quarter
    entries = slots.shape[0] // 2
    ups, downs = wu.shape[1] // width, wd.shape[0]
    tile = 256
    step = 16
    lag = LAG
    chips_of_tile = tile // (2 * depth)

    def lanes(first, size):
        return pl.ds(first if isinstance(first, int) else pl.multiple_of(first, 128), size)

    def over(size, piece_size):
        def run(piece):
            @pl.loop(0, size // piece_size)
            def _(t):
                piece(pl.multiple_of(t * piece_size, piece_size))

        return run

    def toward(d):
        return at.at_ring(1 if d == 0 else -1)

    parts = [(gains, gains_all, 0)]
    ready = {0: [0]}

    def add(name, shard, full, first, pieces=PIECES):
        for size in pieces:
            cols = pl.ds(first, size)
            parts.append((shard.at[:, cols], full.at[:, :, :, cols], size))
            if name is None:
                ready[len(parts) - 1] = [(first, size)]
            first += size
        if name is not None:
            ready[len(parts) - 1] = [name]

    for j in range(3):
        add(1 + j, wq, wq_all, j * width)
    add(4, wo, wo_all, 0)
    for j in range(downs):
        add(5 + j, wd.at[j], wd_all.at[:, :, j], 0)
    up_at = len(parts)
    for j in range(ups):
        add(None, wu, wu_all, j * width, LAST_PIECES if j == ups - 1 else PIECES)
    parts_count = len(parts)
    up_chunks = parts_count - up_at

    def window(k, s=0, d=0):
        if k == 0:
            return pl.ds(0, gains.shape[0]), pl.ds(0, gains.shape[1])
        rows = pl.ds(pl.multiple_of(at.n * quarter, quarter), most)
        if s == steps:
            return rows, pl.ds(d * (parts[k][2] // 2), parts[k][2] // 2)
        return rows, pl.ds(0, parts[k][2])

    def idle(k, s, d):
        return k == 0 and s == steps and d == 1

    def g_ring_out(k, s, d):
        pos = -(s - 1) if d == 0 else s - 1
        rows, cols = window(k, s, d)
        dst = parts[k][1].at[at.chip(pos), at.c, rows, cols]
        src = parts[k][0].at[rows, cols] if s == 1 else dst
        return remote(src, dst, g_ring_send.at[k, s - 1, d], g_ring_recv.at[k, s - 1, d], toward(d))

    def g_ring_in(k, s, d):
        pos = -s if d == 0 else s
        rows, cols = window(k, s, d)
        ref = parts[k][1].at[at.chip(pos), at.c, rows, cols]
        return remote(ref, ref, g_ring_send.at[k, s - 1, d], g_ring_recv.at[k, s - 1, d], toward(d))

    def own_copy(k):
        rows, cols = window(k)
        return pltpu.make_async_copy(
            parts[k][0].at[rows, cols], parts[k][1].at[at.q, at.c, rows, cols], own_sem.at[k]
        )

    def g_cross(k, incoming=False):
        side = 1 - at.n if incoming else at.n
        rows = pl.ds(pl.multiple_of(side * most, quarter), quarter)
        ref = parts[k][1].at[:, at.c, rows]
        return remote(ref, ref, g_x_send.at[k], g_x_recv.at[k], at.across())

    def g_sib(k, incoming=False):
        ref = parts[k][1].at[:, 1 - at.c if incoming else at.c]
        return remote(ref, ref, g_sib_send.at[k], g_sib_recv.at[k], at.sibling())

    def in_copy(j):
        return remote(given.at[j], got.at[j], in_send.at[j], in_recv.at[j], at.across())

    def take_copy(j, s, h):
        source = tokens if j == 0 else cotangent
        place = mine.at[:, :, pl.ds((2 * s + h) * width, width)]
        return pltpu.make_async_copy(source.at[s, h], place, take_sem.at[2 * s + h])

    def pick(j, s, dst):
        span = ring * depth
        wanted = slots[pl.ds(pl.multiple_of(s * entries, entries), entries), :]
        for h in (0, 1):
            spots = lax.broadcasted_iota(jnp.int32, (entries, span), 1) + h * span
            chosen = (spots == wanted).astype(BF16)

            @over(width, tile)
            def _(low):
                cols = pl.ds(low, tile)
                held = mine[:, :, lanes((2 * s + h) * width + low, tile)].reshape(span, tile)
                part = dot(chosen, held).astype(BF16)
                dst[j, :, cols] = part if h == 0 else dst[j, :, cols] + part

    def pick_all(j):
        for s in (0, 1):
            for h in (0, 1):
                take_copy(j, s, h).wait()
        pick(j, 1 - at.n, given)
        in_copy(j).start()
        pick(j, at.n, kept)
        if j == 0:
            for s in (0, 1):
                for h in (0, 1):
                    take_copy(1, s, h).start()

    def turned(src, dst):
        @over(width, tile)
        def _(low):
            chips = pl.ds(low // (2 * depth), chips_of_tile)
            dst[chips] = src[:, pl.ds(low, tile)].T.reshape(chips_of_tile, 2, depth, entries)

    def normalise():
        lane = lax.broadcasted_iota(jnp.int32, (8, 2 * HEAD_DIM), 1)
        for chip in range(ring):
            pair = jnp.where(
                lane < depth, gains_all[chip, 0].astype(F32)[:8], gains_all[chip, 1].astype(F32)[:8]
            )
            scales[:, chip * 2 * depth : (chip + 1) * 2 * depth] = pair

        @over(entries, 32)
        def _(low):
            rows = pl.ds(low, 32)
            low_rows = kept[0, rows] + got[0, rows]
            value = low_rows.astype(F32)
            rows_low[rows, :] = low_rows
            inverse = lax.rsqrt(jnp.mean(value * value, axis=-1, keepdims=True) + epsilon)
            normed[rows, :] = (value * inverse * scales[0:1, :]).astype(BF16)
            router_val[rows, :] = jnp.sum(value * router[...], axis=-1, keepdims=True)

    def project_part(j):
        @over(width, tile)
        def _(low):
            cols = pl.ds(j * width + low, tile)
            weight = wq_all[:, :, :, cols].reshape(width, tile)
            project[:, cols] = dot(normed[...], weight).astype(BF16)

    def attention(first, last):
        @pl.loop(first, last)
        def _(p):
            span = 2 * HEAD_DIM
            q, k, v = [project[:, lanes(j * width + p * span, span)] for j in range(3)]
            total = jnp.zeros((entries, span), F32)
            for head in (0, 1):
                probs = probabilities(live[...], only(q, head), k)
                total = total + only(dot(probs.astype(BF16), v), head)
            heads[:, lanes(p * span, span)] = total.astype(BF16)

    def attend_project():
        @over(width, tile)
        def _(low):
            cols = pl.ds(low, tile)
            weight = wo_all[:, :, :, cols].reshape(width, tile)
            attend_out[:, cols] = dot(heads[...], weight)

        @over(entries, 32)
        def _(low):
            rows = pl.ds(low, 32)
            middle = rows_low[rows, :].astype(F32) + attend_out[rows, :]
            inverse = lax.rsqrt(jnp.mean(middle * middle, axis=-1, keepdims=True) + epsilon)
            value = middle * inverse
            second_n[rows, :] = value
            inverse_two[rows, :] = inverse
            second[rows, :] = (value * scales[1:2, :]).astype(BF16)

    def branch_grad():
        @over(entries, 32)
        def _(low):
            rows = pl.ds(low, 32)
            dout = (kept[1, rows] + got[1, rows]).astype(F32)
            d_mlp[rows, :] = (router_val[rows, :] * dout).astype(BF16)

    def up_part(first, size):
        owner = downs * depth
        for low in range(0, size, owner):
            chip, core = (first + low) // owner // 2, (first + low) // owner % 2
            cols = pl.ds(first + low, owner)
            pre = dot(second[...], wu_all[:, :, :, cols].reshape(width, owner))
            value, slope = gelu_pair(pre)
            value = value.astype(BF16)
            d_act = dot_nt(d_mlp[...], wd_all[chip, core].reshape(owner, width))
            act[:, pl.ds(low, owner)] = value
            d_pre[:, cols] = (d_act * slope).astype(BF16)
            act_t[chip, core] = value.T.reshape(downs, depth, entries)
        chip, core = first // owner // 2, first // owner % 2

        @over(width, tile)
        def _(low):
            cols = pl.ds(low, tile)
            if size == owner:
                down = wd_all[chip, core, :, :, cols]
            else:
                down = wd_all[chip, :, :, :, cols]
            part = dot(act[:, 0:size], down.reshape(size, tile))
            chips = pl.ds(low // (2 * depth), chips_of_tile)
            up = wu_all[chips, :, :, pl.ds(first, size)]
            back = dot_nt(d_pre[:, pl.ds(first, size)], up.reshape(tile, size))
            if first == 0:
                mlp_out[:, cols] = part
                d_second[:, cols] = back
            else:
                mlp_out[:, cols] += part
                d_second[:, cols] += back

    def close():
        small_acc[0] = jnp.zeros((8, width), F32)

        @over(entries, 32)
        def _(low):
            rows = pl.ds(low, 32)
            value = rows_low[rows, :].astype(F32)
            dout = (kept[1, rows] + got[1, rows]).astype(F32)
            gate = router_val[rows, :]
            branch = attend_out[rows, :] + mlp_out[rows, :]
            out_low[rows, :] = (value + gate * branch).astype(BF16)
            d_gate = jnp.sum(dout * branch, axis=-1, keepdims=True)
            normed_value = second_n[rows, :]
            back = d_second[rows, :]
            small_acc[0, 1:2, :] += jnp.sum(back * normed_value, axis=0, keepdims=True)
            small_acc[0, 2:3, :] += jnp.sum(d_gate * value, axis=0, keepdims=True)
            back = back * scales[1:2, :]
            back = inverse_two[rows, :] * (
                back - normed_value * jnp.mean(back * normed_value, axis=-1, keepdims=True)
            )
            d_attend[rows, :] = (gate * dout + back).astype(BF16)
            base[rows, :] = dout + back + d_gate * router[...]

    def heads_grad():
        @over(width, tile)
        def _(low):
            chips = pl.ds(low // (2 * depth), chips_of_tile)
            weight = wo_all[chips].reshape(tile, width)
            heads[:, pl.ds(low, tile)] = dot_nt(d_attend[...], weight).astype(BF16)

    def attention_back(first, last):
        span = 2 * HEAD_DIM

        @pl.loop(first, last)
        def _(p):
            places = [lanes(j * width + p * span, span) for j in range(3)]
            q, k, v = [project[:, place] for place in places]
            d_pair = heads[:, places[0]]
            d_q = jnp.zeros((entries, span), F32)
            d_k = jnp.zeros((entries, span), F32)
            d_v = jnp.zeros((entries, span), F32)
            for head in (0, 1):
                probs = probabilities(live[...], only(q, head), k)
                d_own = only(d_pair, head)
                d_probs = dot_nt(d_own, v)
                d_scores = probs * (d_probs - jnp.sum(probs * d_probs, axis=-1, keepdims=True))
                d_scores = d_scores.astype(BF16)
                d_q = d_q + only(dot(d_scores, k), head)
                d_k = d_k + only(dot_tn(d_scores, q), head)
                d_v = d_v + dot_tn(probs.astype(BF16), d_own)
            d_project[:, places[0]] = (d_q * 0.125).astype(BF16)
            d_project[:, places[1]] = (d_k * 0.125).astype(BF16)
            d_project[:, places[2]] = d_v.astype(BF16)

    def normed_grad(j):
        @over(width, tile)
        def _(low):
            chips = pl.ds(low // (2 * depth), chips_of_tile)
            weight = wq_all[chips, :, :, pl.ds(j * width, width)].reshape(tile, width)
            part = dot_nt(d_project[:, pl.ds(j * width, width)], weight)
            cols = pl.ds(low, tile)
            if j == 0:
                d_second[:, cols] = part
            else:
                d_second[:, cols] += part

    def finish():
        @over(entries, 32)
        def _(low):
            rows = pl.ds(low, 32)
            value = rows_low[rows, :].astype(F32)
            inverse = lax.rsqrt(jnp.mean(value * value, axis=-1, keepdims=True) + epsilon)
            value = value * inverse
            back = d_second[rows, :]
            small_acc[0, 0:1, :] += jnp.sum(back * value, axis=0, keepdims=True)
            back = back * scales[0:1, :]
            back = inverse * (back - value * jnp.mean(back * value, axis=-1, keepdims=True))
            grad_low[rows, :] = (base[rows, :] + back).astype(BF16)

    count = len(chunks)
    reused = [k for k in range(count) if chunks[k].panel >= ups]

    def spread(k, first, size):
        return lanes(chunks[k].panel * width + chunks[k].off + first, size)

    def sums(k, chip, rows, first, size):
        c = chunks[k]
        if c.panel < ups:
            return mine.at[chip, rows, spread(k, first, size)]
        p = c.panel - ups
        return wd_all.at[chip, p // downs, p % downs, rows, lanes(c.off + first, size)]

    def passing(k, t, d, rows, first, size):
        c = chunks[k]
        if c.panel < ups:
            if t == 0:
                return landed.at[d, rows, spread(k, first, size)]
            return moving.at[t - 1, d, rows, spread(k, first, size)]
        p = c.panel - ups
        cols = lanes(p % ups * width + c.off + first, size)
        slab = 12 + p // ups if t == 0 else p // ups * 6 + (t - 1) * 2 + d
        if t == 0:
            rows = pl.ds(d * half + rows.start, rows.size)
        return wu_all.at[slab // 2, slab % 2, rows, cols]

    every = pl.ds(0, depth)

    def ride(k):
        return chunks[k].give * at.n if chunks[k].give else 0, chunks[k].size - chunks[k].give

    def product(k, core, put):
        c = chunks[k]
        if c.kind == "down":
            left, right = act_t[:, core, c.j], d_mlp
        else:
            tall, right = {
                "up": (second_t, d_pre),
                "out": (heads_t, d_attend),
                "qkv": (normed_t, d_project),
            }[c.kind]
            left = tall[:, core]
        left = left.reshape(ring * depth, entries)

        @pl.loop(0, c.size // tile)
        def _(t):
            cols = pl.ds(pl.multiple_of(t * tile, tile), tile)
            take = pl.ds(pl.multiple_of(c.first + t * tile, tile), tile)
            put(cols, dot(left, right[:, take]).reshape(ring, depth, tile))

    def out_copy(k):
        c = chunks[k]
        out = {"up": o_up, "down": o_down, "out": o_out, "qkv": o_qkv}[c.kind]
        rows = pl.ds(c.j * depth if c.kind == "down" else 0, depth)
        return pltpu.make_async_copy(
            staged.at[k % 2, :, pl.ds(0, c.size)], out.at[rows, pl.ds(c.first, c.size)], out_sem.at[k]
        )

    def sib(k):
        src = to_sib.at[k % 2, :, :, pl.ds(0, chunks[k].size)]
        dst = sums(k, slice(None), slice(None), 0, chunks[k].size)
        return remote(src, dst, sib_send.at[k], sib_recv.at[k], at.sibling())

    def pre(k):
        c = chunks[k]
        src = sums(k, slice(None), slice(None), (c.size - c.give) * (1 - at.n), c.give)
        dst = x_pre.at[:, :, lanes(c.given_at, c.give)]
        return remote(src, dst, pre_send.at[k], pre_recv.at[k], at.across())

    def dest(t, d):
        return at.chip(steps - t if d == 0 else t - steps)

    def ring_out(k, t, d):
        rows = pl.ds(d * half, half) if t == 0 else every
        src = sums(k, dest(t, d), rows, *ride(k))
        land = passing(k, t, d, pl.ds(0, half) if t == 0 else every, *ride(k))
        return remote(src, land, ring_send.at[k, t, d], ring_recv.at[k, t, d], toward(d))

    def cross(k):
        first, size = ride(k)
        dst = x_in.at[:, lanes(chunks[k].start + first, size)]
        return remote(sums(k, at.q, every, first, size), dst, x_send.at[k], x_recv.at[k], at.across())

    bits = [1 << b for b in range(ring.bit_length() - 1)]
    partners = [at.sibling(), at.across()] + [at.flipped(bit) for bit in bits]
    stages = len(partners)

    def small_copy(j):
        return remote(
            small_acc.at[j], small_in.at[j], small_send.at[j], small_recv.at[j], partners[j]
        )

    def row_copy(j, p):
        rows = pl.ds(p * (entries // ROW_PIECES), entries // ROW_PIECES)
        src = out_low if j == 0 else grad_low
        dst = rows_all.at[j, at.n, rows]
        return remote(src.at[rows], dst, row_send.at[j, p], row_recv.at[j, p], at.across())

    def row_in(j, p):
        rows = pl.ds(p * (entries // ROW_PIECES), entries // ROW_PIECES)
        ref = rows_all.at[j, 1 - at.n, rows]
        return remote(ref, ref, row_send.at[j, p], row_recv.at[j, p], at.across())

    def row_keep(j):
        src = out_low if j == 0 else grad_low
        return pltpu.make_async_copy(src, rows_all.at[j, at.n], row_own.at[j])

    def release():
        for k in range(parts_count):
            g_sib(k).wait_send()
            if k > 0:
                g_cross(k).wait_send()
            for s in range(1, steps + 1):
                for d in (0, 1):
                    if not idle(k, s, d):
                        g_ring_out(k, s, d).wait_send()
        for j, device in enumerate((at.at_ring(-1), at.at_ring(1), at.sibling())):
            pl.semaphore_signal(free.at[j], inc=1, device_id=device, device_id_type=MESH)

    pairs = width // (2 * HEAD_DIM)
    cuts = [pairs * j // 8 for j in (0, 2, 5, 8)]
    work = {
        0: [normalise, lambda: turned(normed, normed_t)],
        1: [lambda: project_part(0)],
        2: [lambda: project_part(1)],
        3: [lambda: project_part(2), lambda: attention(cuts[0], cuts[1])],
        4: [lambda: attention(cuts[1], cuts[2])],
        5: [lambda: attention(cuts[2], cuts[3]), attend_project],
        6: [lambda: turned(heads, heads_t), lambda: turned(second, second_t)],
        7: [branch_grad],
    }
    back_cuts = [pairs * j // 4 for j in range(5)]
    back_work = [heads_grad]
    back_work += [functools.partial(attention_back, back_cuts[j], back_cuts[j + 1]) for j in range(4)]
    back_work += [functools.partial(normed_grad, j) for j in range(3)]
    back_work += [finish]

    def gather_turn(i):
        for k in range(LEAD + 1) if i == 0 else (i + LEAD,):
            if k < parts_count:
                for d in (0, 1):
                    g_ring_out(k, 1, d).start()
                own_copy(k).start()
        if i in PICK_AT:
            pick_all(PICK_AT.index(i))
        for s in range(1, steps + 1):
            k = i - lag * s
            if 0 <= k < parts_count:
                for d in (0, 1):
                    if not idle(k, s, d):
                        g_ring_in(k, s, d).wait_recv()
                    if s < steps and not idle(k, s + 1, d):
                        g_ring_out(k, s + 1, d).start()
                if s == steps:
                    own_copy(k).wait()
                    if k > 0:
                        g_cross(k).start()
        k = i - lag * (steps + 1)
        if 0 <= k < parts_count:
            if k > 0:
                g_cross(k, True).wait_recv()
            g_sib(k).start()
        k = i - lag * (steps + 1) - 1
        if 0 <= k < parts_count:
            g_sib(k, True).wait_recv()
            if k == 0:
                for j in (0, 1):
                    in_copy(j).wait_recv()
            for piece in ready.get(k, ()):
                if isinstance(piece, int):
                    for job in work.get(piece, ()):
                        job()
                else:
                    up_part(*piece)

    ring_at = 1 + lag
    work_at = up_chunks
    small_at = work_at + len(back_work)

    def reduce_turn(i):
        k = i - ring_at - lag * steps - lag
        if 0 <= k < count:
            c = chunks[k]
            cross(k).wait_recv()
            if k >= 2:
                out_copy(k - 2).wait()
            inner = c.size - 2 * c.give

            @over(depth, step)
            def _(row):
                rows = pl.ds(row, step)

                def mixed(first, size):
                    return sums(k, at.q, rows, first, size)[...].astype(F32), x_in[
                        rows, lanes(c.start + first, size)
                    ].astype(F32)

                here, there = mixed(c.give, inner)
                staged[k % 2, rows, c.give : c.give + inner] = here + there
                if c.give:
                    alone = (c.size - c.give) * at.n
                    staged[k % 2, rows, lanes(alone, c.give)] = mixed(alone, c.give)[0]
                    alone = (c.size - c.give) * (1 - at.n)
                    staged[k % 2, rows, lanes(alone, c.give)] = mixed(alone, c.give)[1]

            out_copy(k).start()
        k = i - ring_at - lag * steps
        if 0 <= k < count:
            for d in (0, 1):
                land = passing(k, steps - 1, d, every, *ride(k))
                remote(
                    land,
                    land,
                    ring_send.at[k, steps - 1, d],
                    ring_recv.at[k, steps - 1, d],
                    toward(d),
                ).wait_recv()

            @over(depth, step)
            def _(row):
                rows = pl.ds(row, step)
                total = sums(k, at.q, rows, *ride(k))
                value = total[...].astype(F32)
                for d in (0, 1):
                    value = value + passing(k, steps - 1, d, rows, *ride(k))[...].astype(F32)
                total[...] = value.astype(BF16)

            cross(k).start()
        for t in range(steps - 1, 0, -1):
            k = i - ring_at - lag * t
            if 0 <= k < count:
                for d in (0, 1):
                    size = half if t == 1 else depth
                    land = passing(k, t - 1, d, pl.ds(0, size), *ride(k))
                    remote(
                        land, land, ring_send.at[k, t - 1, d], ring_recv.at[k, t - 1, d], toward(d)
                    ).wait_recv()
                    to = dest(t, d)
                    low = d * half if t == 1 else 0

                    @over(size, step)
                    def _(row):
                        total = sums(k, to, pl.ds(low + row, step), *ride(k))
                        came = passing(k, t - 1, d, pl.ds(row, step), *ride(k))
                        value = total[...].astype(F32) + came[...].astype(F32)
                        total[...] = value.astype(BF16)

                    ring_out(k, t, d).start()
        k = i - ring_at
        if 0 <= k < count:
            c = chunks[k]
            if c.give > 0:
                pre(k).wait_recv()
                alone = (c.size - c.give) * at.n

                @pl.loop(0, ring)
                def _(chip):
                    total = sums(k, chip, every, alone, c.give)
                    came = x_pre[chip, :, lanes(c.given_at, c.give)]
                    total[...] = (total[...].astype(F32) + came.astype(F32)).astype(BF16)

            for d in (0, 1):
                if k == reused[0]:
                    pl.semaphore_wait(free.at[d], 1)
                ring_out(k, 0, d).start()
        k = i - 1
        if 0 <= k < count:
            c = chunks[k]
            all_sums = sums(k, slice(None), slice(None), 0, c.size)
            remote(all_sums, all_sums, sib_send.at[k], sib_recv.at[k], at.sibling()).wait_recv()

            @pl.loop(0, ring)
            def _(chip):
                total = sums(k, chip, every, 0, c.size)
                total[...] = (total[...].astype(F32) + own[chip, :, 0 : c.size]).astype(BF16)

            if c.give > 0:
                pre(k).start()
        k = i
        if 0 <= k < count:
            if k >= 2:
                sib(k - 2).wait_send()

            def keep_other(cols, value):
                to_sib[k % 2, :, :, cols] = value.astype(BF16)

            def keep_own(cols, value):
                own[:, :, cols] = value

            product(k, 1 - at.c, keep_other)
            if k == reused[0]:
                pl.semaphore_wait(free.at[2], 1)
            sib(k).start()
            product(k, at.c, keep_own)
        j = i - work_at
        if 0 <= j < len(back_work):
            back_work[j]()
        p = i - ROWS_AT
        if 0 <= p < ROW_PIECES:
            row_copy(0, p).start()
        if j == 0:
            row_keep(0).start()
        p = i - max(small_at, ROWS_AT)
        if 0 <= p < ROW_PIECES:
            row_copy(1, p).start()
        if p == 0:
            row_keep(1).start()
        j = i - small_at
        if 0 <= j <= stages:
            if j > 0:
                small_copy(j - 1).wait_recv()
                small_acc[j] = small_acc[j - 1] + small_in[j - 1]
            if j < stages:
                small_copy(j).start()
            else:
                o_small[...] = small_acc[stages]

    for s in (0, 1):
        for h in (0, 1):
            take_copy(0, s, h).start()
    greet(partners + [at.at_ring(1), at.at_ring(-1)])
    offset = up_at + lag * (steps + 1) + 1
    for i in range(offset + count + ring_at + lag * steps + lag + 1):
        gather_turn(i)
        if i == offset + up_chunks - 1:
            release()
            close()
        reduce_turn(i - offset)

    for j in (0, 1):
        in_copy(j).wait_send()
    for k in range(count):
        if k >= count - 2:
            sib(k).wait_send()
            out_copy(k).wait()
        if chunks[k].give > 0:
            pre(k).wait_send()
        cross(k).wait_send()
        for t in range(steps):
            for d in (0, 1):
                ring_out(k, t, d).wait_send()
    for j in range(stages):
        small_copy(j).wait_send()
    for j in (0, 1):
        for p in range(ROW_PIECES):
            row_copy(j, p).wait_send()
            row_in(j, p).wait_recv()
        row_keep(j).wait()


class Chunk(NamedTuple):
    kind: str
    j: int
    first: int
    size: int
    panel: int
    off: int
    start: int
    give: int
    given_at: int


def cut_chunks(width, ff):
    panels = [("up", j, j * width) for j in range(ff // width)]
    panels += [("down", j, 0) for j in range(ff // width)]
    panels += [("out", 0, 0)] + [("qkv", j, j * width) for j in range(3)]
    plain = []
    for panel, (kind, j, first) in enumerate(panels):
        off = 0
        last = panel in (ff // width - 1, len(panels) - 1)
        for size in LAST_PIECES if last else PIECES:
            plain.append((kind, j, first + off, size, panel, off))
            off += size
    chunks, start, given = [], 0, 0
    for k, piece in enumerate(plain):
        inside = GIVE_SKIP[0] <= k < len(plain) - GIVE_SKIP[1]
        give = GIVE if inside and piece[3] == 512 else 0
        chunks.append(Chunk(*piece, start, give, given))
        start += piece[3]
        given += give
    return tuple(chunks), start, given


def layer(wide, gains, wq, wo, wu, wd, tokens, cotangent, slots, router, live):
    depth, width = wo.shape
    ring, steps = wide // 2, wide // 4
    entries = slots.shape[0] // 2
    ff = wu.shape[1]
    ups = downs = ff // width
    chunks, columns, given_columns = cut_chunks(width, ff)
    parts = 1 + (3 + downs + ups) * len(PIECES) + len(LAST_PIECES)
    count = len(chunks)
    stages = 2 + (ring.bit_length() - 1)
    in_vmem = pl.BlockSpec(memory_space=pltpu.VMEM)
    anywhere = pl.BlockSpec(memory_space=pl.ANY)
    dma = pltpu.SemaphoreType.DMA
    vmem = pltpu.VMEM
    shape = jax.ShapeDtypeStruct
    tall = (ring, 2, depth, entries)
    square = (entries, width)
    return pl.pallas_call(
        functools.partial(layer_kernel, wide, chunks),
        out_shape=[
            shape((depth, 3 * width), F32),
            shape((depth, width), F32),
            shape((depth, ff), F32),
            shape((ff // wide, width), F32),
            shape((8, width), F32),
            shape((2, 2, entries, width), BF16),
        ],
        in_specs=[anywhere] * 7 + [in_vmem] * 3,
        out_specs=[anywhere] * 4 + [in_vmem] * 2,
        scratch_shapes=[
            vmem((ring, 2, depth, 3 * width), BF16),
            vmem((ring, 2, depth, width), BF16),
            vmem((ring, 2, depth, ff), BF16),
            vmem((ring, 2, downs, depth, width), BF16),
            vmem((ring, 2) + gains.shape, BF16),
            vmem((8, width), F32),
            vmem((2,) + square, BF16),
            vmem((2,) + square, BF16),
            vmem((2,) + square, BF16),
            vmem(square, BF16),
            vmem(square, BF16),
            vmem(square, BF16),
            vmem(square, BF16),
            vmem((entries, 3 * width), BF16),
            vmem(square, BF16),
            vmem(square, F32),
            vmem(square, F32),
            vmem(square, BF16),
            vmem((entries, 512), BF16),
            vmem((entries, ff), BF16),
            vmem(square, F32),
            vmem(square, F32),
            vmem(square, BF16),
            vmem(square, BF16),
            vmem(square, F32),
            vmem((entries, 3 * width), BF16),
            vmem(tall, BF16),
            vmem(tall, BF16),
            vmem(tall, BF16),
            vmem((ring, 2, downs, depth, entries), BF16),
            vmem((entries, 1), F32),
            vmem((entries, 1), F32),
            vmem((ring, depth, 512), F32),
            vmem((2, ring, depth, 512), BF16),
            vmem((ring, depth, ups * width), BF16),
            vmem((2, depth // 2, ups * width), BF16),
            vmem((steps - 1, 2, depth, ups * width), BF16),
            vmem((ring, depth, max(given_columns, 128)), BF16),
            vmem((depth, columns), BF16),
            vmem((2, depth, 512), F32),
            vmem((stages + 1, 8, width), F32),
            vmem((stages, 8, width), F32),
            dma((parts,)),
            dma((parts, steps, 2)),
            dma((parts, steps, 2)),
            dma((parts,)),
            dma((parts,)),
            dma((parts,)),
            dma((parts,)),
            dma((2,)),
            dma((2,)),
            dma((count,)),
            dma((count,)),
            dma((count,)),
            dma((count,)),
            dma((count, steps, 2)),
            dma((count, steps, 2)),
            dma((count,)),
            dma((count,)),
            dma((count,)),
            dma((stages,)),
            dma((stages,)),
            dma((2, ROW_PIECES)),
            dma((2, ROW_PIECES)),
            dma((2,)),
            dma((4,)),
            pltpu.SemaphoreType.REGULAR((3,)),
        ],
        compiler_params=pltpu.CompilerParams(
            collective_id=1, has_side_effects=True, vmem_limit_bytes=63 * 1024 * 1024
        ),
        name="layer",
    )(
        gains,
        wq,
        wo,
        wu,
        wd.reshape(downs, depth, width),
        tokens.reshape(2, 2, ring, depth, width),
        cotangent.reshape(2, 2, ring, depth, width),
        slots,
        router,
        live,
    )


def paired_body(
    wide, tokens, cotangent, lengths, routes, w_qkv, w_out, w_up, w_down, gain_attn, gain_mlp, router
):
    place = lax.axis_index("narrow")
    seqs, span, width = tokens.shape
    list_len = routes.shape[1]
    depth = gain_attn.shape[0]
    counts = lengths // 8
    entry = jnp.arange(list_len, dtype=jnp.int32)
    live = entry[None, :] < counts[:, None]
    local_slot = jnp.where(live, routes - place * span, -1)
    spots = jnp.arange(span, dtype=jnp.int32)
    chosen = (local_slot[:, :, None] == spots[None, None, :]).astype(BF16)

    slots = local_slot.reshape(seqs * list_len, 1)
    gains = jnp.stack(
        [jnp.concatenate([gain_attn, gain_attn]), jnp.concatenate([gain_mlp, gain_mlp])]
    )
    gains = jnp.pad(gains, ((0, 14), (0, 0)))
    router_row = router.astype(F32)[None, :]
    live_row = lax.dynamic_index_in_dim(live, place, 0, keepdims=True).astype(jnp.int32)
    grad_qkv, grad_out, grad_up, grad_down, small, rows_out = layer(
        wide, gains, w_qkv, w_out, w_up, w_down, tokens, cotangent, slots, router_row, live_row
    )
    hit = jnp.any(local_slot[:, :, None] == spots[None, None, :], axis=1)

    def put(base, fresh):
        spread = jnp.einsum("sep,sed->spd", chosen, fresh, preferred_element_type=F32)
        return jnp.where(hit[:, :, None], spread.astype(BF16), base)

    start = lax.axis_index("wide") * depth
    return (
        put(tokens, rows_out[0]),
        put(cotangent, rows_out[1]),
        grad_qkv,
        grad_out,
        grad_up,
        grad_down,
        lax.dynamic_slice_in_dim(small[0], start, depth),
        lax.dynamic_slice_in_dim(small[1], start, depth),
        small[2],
    )


def body(wide, narrow, tokens, *others):
    if narrow == 2 and tokens.shape == (2, wide * 64, 1024) and wide == 16:
        return paired_body(wide, tokens, *others)
    return general_body(tokens, *others)


def solution(mesh):
    in_specs = (
        P("wide", "narrow", None),
        P("wide", "narrow", None),
        P("wide"),
        P("wide", None),
        P("wide", None),
        P("wide", None),
        P("wide", None),
        P("wide", None),
        P("wide"),
        P("wide"),
        P(),
    )
    out_specs = (
        P("wide", "narrow", None),
        P("wide", "narrow", None),
        P("wide", None),
        P("wide", None),
        P("wide", None),
        P("wide", None),
        P("wide"),
        P("wide"),
        P(),
    )
    sizes = mesh.shape["wide"], mesh.shape["narrow"]
    return jax.shard_map(functools.partial(body, *sizes), mesh=mesh, in_specs=in_specs, out_specs=out_specs, check_vma=False)
```
